32 devices in a mesh: aisle: 4 (over x, core), row: 8 (over z, y).
Axes of the slice: x: 2, y: 2, z: 4, core: 2. Of those that a mesh axis runs over, the one named last changes fastest.
Arguments:
- source: float32 [8, 128, 512], P(None, 'row', 'aisle'), may hold values from -6 to 6
- conduct: float32 [8, 128, 512], P(None, 'row', 'aisle'), may hold values from 1 to 10
- solid: int32 [8, 128, 512], P(None, 'row', 'aisle'), may hold values 0 or 1
Outputs:
- correction: float32 [8, 128, 512], P(None, 'row', 'aisle')
The draws below stay inside these ranges and needn't reach their ends.
All inputs are finite; a program needn't handle non-finite values. No bound on the sum of `solid` on one device may be relied on, other than what follows from the above.
Results may differ from the reference program's by a relative error of at most 0.0003.
Values sent between devices are 32-bit elements; how exact they have to be, the bound alone decides.
No kernel may reach another device: no remote copies, remote signals or barrier semaphores. Data moves between devices by JAX's collectives and lax.ppermute only.
A program may use at most 64 MiB of HBM per device.

```python
import math
import jax
import jax.numpy as jnp
from jax import lax

NZ = 8
CR = 16
CA = 128
OV = 2
SWEEPS = 6
NR = 128
NA = 512
N_AISLE = 4
N_ROW = 8


def draw_source(key, part):
    rough_key = jax.random.fold_in(key, 11)
    return jax.random.truncated_normal(rough_key, -6.0, 6.0, (NZ, NR, NA), jnp.float32)


def touch_ends(entries, stream_key, low, high):
    index_at = [jax.random.randint(jax.random.fold_in(stream_key, axis), (), 0, length) for axis, length in enumerate(entries.shape)]
    widest = entries.shape.index(max(entries.shape))
    neighbour = index_at[:widest] + [(index_at[widest] + 1) % entries.shape[widest]] + index_at[widest + 1:]
    return entries.at[tuple(index_at)].set(low).at[tuple(neighbour)].set(high)


def levels(rng, shape, shards, least, largest):
    level = 1.0
    for axis_at, parts in shards:
        steps = jax.random.uniform(jax.random.fold_in(jax.random.fold_in(rng, 6), axis_at), (parts,), jnp.float32, least / len(shards), largest / len(shards))
        level = level * jnp.repeat(jnp.exp(steps), shape[axis_at] // parts).reshape((-1,) + (1,) * (len(shape) - 1 - axis_at))
    return level


def setup_inputs(seed: int = 0) -> dict:
    splits = jax.random.split(jax.random.key(seed), 4)
    source = draw_source(jax.random.fold_in(splits[3], 71), 0)
    conduct = jnp.clip(jnp.exp(math.log(10.0) - 2.3025851 * jax.random.uniform(splits[1], (NZ, NR, NA), jnp.float32) ** levels(splits[1], (NZ, NR, NA), ((1, 8), (2, 4)), -0.2, 0.2)), 1.0, 10.0)
    solid = touch_ends((jax.random.randint(splits[2], (NZ, NR, NA), 0, 4) < 1).astype(jnp.int32), jax.random.fold_in(splits[2], 1), 0, 1)
    return {"source": source, "conduct": conduct, "solid": solid}


lower_end = 0.2
upper_end = 2.0


def padded(values):
    return jnp.pad(values, [(0, 0)] * (values.ndim - 3) + [(1, 1)] * 3)


def beside(padded_values):
    return [padded_values[..., 2:, 1:-1, 1:-1], padded_values[..., :-2, 1:-1, 1:-1],
            padded_values[..., 1:-1, 2:, 1:-1], padded_values[..., 1:-1, :-2, 1:-1],
            padded_values[..., 1:-1, 1:-1, 2:], padded_values[..., 1:-1, 1:-1, :-2]]


def coupling(padded_cond, shift_term):
    centre = padded_cond[..., 1:-1, 1:-1, 1:-1]
    weights = [0.5 * (centre + other) for other in beside(padded_cond)]
    diagonal = shift_term
    for weight in weights:
        diagonal = diagonal + weight
    return weights, diagonal


def operate(padded_values, weights, diagonal):
    others = beside(padded_values)
    summed = weights[0] * others[0]
    for number in range(1, 6):
        summed = summed + weights[number] * others[number]
    return diagonal * padded_values[..., 1:-1, 1:-1, 1:-1] - summed


def smooth_local(source_ext, weights, diagonal):
    middle = 0.5 * (upper_end + lower_end)
    spread = 0.5 * (upper_end - lower_end)
    ratio_now = spread / middle
    inverse = 1.0 / diagonal
    update = inverse * source_ext / middle
    estimate = update
    for sweep_no in range(SWEEPS):
        remain = source_ext - operate(padded(estimate), weights, diagonal)
        ratio_next = 1.0 / (2.0 * middle / spread - ratio_now)
        update = (ratio_next * ratio_now) * update + (2.0 * ratio_next / spread) * inverse * remain
        estimate = estimate + update
        ratio_now = ratio_next
    return estimate


def schwarz(source, cond, shift_term):
    total_cols = CA * N_AISLE
    width_rows = CR + 2 * OV
    cond_rows = jnp.pad(cond, ((0, 0), (OV, OV), (0, 0)))
    shift_rows = jnp.pad(shift_term, ((0, 0), (OV, OV), (0, 0)), constant_values=1.0)
    source_rows = jnp.pad(source, ((0, 0), (OV, OV), (0, 0)))
    table = ((jnp.arange(N_AISLE, dtype=jnp.int32)[:, None] * CA - OV
              + jnp.arange(CA + 2 * OV, dtype=jnp.int32)[None, :]) % total_cols).astype(jnp.int32)
    core_mask = jnp.pad(jnp.ones((CR, CA), jnp.float32), OV)

    def blocks(slab):
        return jnp.moveaxis(jnp.take(slab, table, axis=2), 2, 0)

    def step(total, block_row):
        start = (block_row * CR).astype(jnp.int32)

        def cut(values):
            return lax.dynamic_slice_in_dim(values, start, width_rows, axis=1)

        weights, diagonal = coupling(padded(blocks(cut(cond_rows))), blocks(cut(shift_rows)))
        result = smooth_local(blocks(cut(source_rows)) * core_mask, weights, diagonal)
        folded = jnp.zeros((NZ, width_rows, total_cols), jnp.float32).at[:, :, table].add(jnp.moveaxis(result, 0, 2))
        current = lax.dynamic_slice_in_dim(total, start, width_rows, axis=1)
        total = lax.dynamic_update_slice_in_dim(total, current + folded, start, axis=1)
        return total, None

    total = jnp.zeros((NZ, CR * N_ROW + 2 * OV, total_cols), jnp.float32)
    total, unused = lax.scan(step, total, jnp.arange(N_ROW, dtype=jnp.int32))
    return total[:, OV:OV + CR * N_ROW, :]


def wrap_pad(values):
    with_cols = jnp.concatenate([values[..., -1:], values, values[..., :1]], axis=-1)
    return jnp.pad(with_cols, ((1, 1), (1, 1), (0, 0)))


def reference(source, conduct, solid):
    shift_term = 0.05 + 20.0 * solid.astype(jnp.float32)
    first = schwarz(source, conduct, shift_term)
    weights, diagonal = coupling(wrap_pad(conduct), shift_term)
    remain = source - operate(wrap_pad(first), weights, diagonal)
    return first + schwarz(remain, conduct, shift_term)
```

```python
import jax
import jax.numpy as jnp
from jax import lax
from jax.experimental import pallas as pl
from jax.experimental.pallas import tpu as pltpu
from jax.sharding import PartitionSpec as P

OV = 2
SWEEPS = 6
LOWER_END = 0.2
UPPER_END = 2.0
MIDDLE = 0.5 * (UPPER_END + LOWER_END)
SPREAD = 0.5 * (UPPER_END - LOWER_END)

NZ = 8
CR = 16
CA = 128
DG = 2 * SWEEPS + 1
DK = DG + 1
UP = DG + OV
OWN = CR + 2 * OV
ROWS = UP + OWN + UP
OWN0 = UP
DOWN0 = UP + OWN
WIDE = 2 * CA
TWIN = 5
STRIP = 14
PERIOD = 40
TILES = 2 * DG + 2 * DK


def chebyshev():
    ratio = SPREAD / MIDDLE
    steps = []
    for _ in range(SWEEPS):
        ratio_next = 1.0 / (2.0 * MIDDLE / SPREAD - ratio)
        steps.append((ratio_next * ratio, 2.0 * ratio_next / SPREAD))
        ratio = ratio_next
    return steps


def lanes(width=CA):
    return lax.broadcasted_iota(jnp.int32, (NZ, width), 1)


def turn(value, by, axis=1):
    return pltpu.roll(value, by % value.shape[axis], axis)


def any_of(lane, *spans):
    mask = None
    for low, high in spans:
        here = (lane >= low) & (lane < high)
        mask = here if mask is None else mask | here
    return mask


def pack_edges(source, conduct, solid, main, to_left, to_right):
    odd = lax.rem(lax.axis_index("row"), 2)
    lane = lanes()
    lefts, rights = [], []
    for row in range(CR):
        at = pl.ds(odd * (CR - 1 - 2 * row) + row, NZ, stride=CR)
        fields = [source[at, :], conduct[at, :], 0.05 + 20.0 * solid[at, :].astype(jnp.float32)]
        left = right = jnp.zeros((NZ, CA), jnp.float32)
        for number, field in enumerate(fields):
            main[number, row] = field
            base = PERIOD * number
            left = jnp.where(any_of(lane, (base + 24, base + 38)), turn(field, base + 24), left)
            right = jnp.where(any_of(lane, (base, base + STRIP)), turn(field, base + STRIP), right)
        lefts.append(left)
        rights.append(right)
    half = CR // 2
    for row in range(half):
        to_left[row] = lefts[row] + turn(lefts[row + half], -16)
        to_right[row] = rights[row] + turn(rights[row + half], 16)


def pack_rows(main, from_right, from_left, strips, to_far, to_near):
    lane = lanes()
    in_right = any_of(lane, *[(PERIOD * n + 24, PERIOD * n + 38) for n in range(3)])
    half = CR // 2
    for row in range(half):
        strips[row] = jnp.where(in_right, from_right[row], from_left[row])
        strips[row + half] = jnp.where(in_right, turn(from_right[row], 16), turn(from_left[row], -16))
    for out, place in ((to_far, lambda q: q), (to_near, lambda q: CR - 1 - q)):
        for q in range(DG):
            out[q] = main[0, place(q)]
            out[DG + DK + q] = main[2, place(q)]
        for q in range(DK):
            out[DG + q] = main[1, place(q)]
            out[2 * DG + DK + q] = strips[place(q)]


def beside_block(block, strip, number, lane, fill):
    boxes = jnp.where(any_of(lane, (5, 19), (109, 123)), turn(strip, -19 - PERIOD * number), 0.0)
    if not fill:
        return boxes
    mixed = jnp.where(any_of(lane, (5, 7), (121, 123)), boxes, block)
    low = any_of(lane, (0, 2), (123, 125))
    high = any_of(lane, (3, 5), (126, 128))
    return jnp.where(low, turn(mixed, -TWIN), jnp.where(high, turn(mixed, TWIN), boxes))


def loop_rows(low, high, unroll, body, carry=None):
    count = (high - low) // unroll

    def chunk(number, carry):
        for k in range(unroll):
            carry = body(low + number * unroll + k, carry)
        return carry

    if count > 0:
        carry = lax.fori_loop(0, count, chunk, carry)
    for row in range(low + count * unroll, high):
        carry = body(row, carry)
    return carry


def solve_all(main, strips, far, near, out, cond, shift, face_x, face_z, face_r, inverse, diag, rhs, est, upd, total):
    row_at = lax.axis_index("row")
    rows_all = lax.axis_size("row")
    odd = lax.rem(row_at, 2)
    far_there = jnp.where(odd == 0, row_at > 0, row_at < rows_all - 1)
    far_here = jnp.full((NZ, CA), far_there.astype(jnp.float32)) > 0.5
    far_wide = jnp.full((NZ, WIDE), far_there.astype(jnp.float32)) > 0.5
    lane = lanes()
    wide = lanes(WIDE)
    level = lax.broadcasted_iota(jnp.int32, (NZ, WIDE), 0)
    zeros = jnp.zeros((NZ, WIDE), jnp.float32)

    def put(block, strip, number, fill):
        return jnp.concatenate([block, beside_block(block, strip, number, lane, fill)], axis=1)

    def unpack_own(row, carry):
        strip = strips[row]
        rhs[OWN0 + OV + row] = put(main[0, row], strip, 0, False)
        cond[DK + row] = put(main[1, row], strip, 1, True)
        shift[DG + row] = put(main[2, row], strip, 2, True)
        return carry

    loop_rows(0, CR, 4, unpack_own)

    def unpack_sides(q, carry):
        strip = far[2 * DG + DK + q]
        rhs[DG - 1 - q] = put(far[q], strip, 0, False)
        cond[DK - 1 - q] = put(far[DG + q], strip, 1, True)
        shift[DG - 1 - q] = jnp.where(far_wide, put(far[DG + DK + q], strip, 2, True), 1.0)
        strip = near[2 * DG + DK + q]
        rhs[DOWN0 + OV + q] = put(near[q], strip, 0, False)
        cond[DK + CR + q] = put(near[DG + q], strip, 1, True)
        shift[DG + CR + q] = put(near[DG + DK + q], strip, 2, True)
        return carry

    loop_rows(0, DG, 3, unpack_sides)
    last = DK - 1
    cond[0] = put(far[DG + last], far[2 * DG + DK + last], 1, True)
    cond[DK + CR + last] = put(near[DG + last], near[2 * DG + DK + last], 1, True)
    for row in (UP - 2, UP - 1, OWN0, OWN0 + 1, DOWN0 - 2, DOWN0 - 1, DOWN0, DOWN0 + 1):
        rhs[row] = zeros

    in_box = any_of(wide, (0, 130), (131, 147), (237, 253), (254, 256))
    core = any_of(wide, (0, 128), (133, 147), (237, 251))
    top = level == NZ - 1
    bottom = level == 0

    def weights(row, place, low_end=False, high_end=False):
        here = cond[place + DK]
        below = zeros if low_end else cond[place + DK - 1]
        above = zeros if high_end else cond[place + DK + 1]
        z_up = jnp.where(top, 0.0, turn(here, -1, 0))
        z_down = jnp.where(bottom, 0.0, turn(here, 1, 0))
        x_up = turn(here, -1)
        x_down = turn(here, 1)
        diagonal = shift[place + DG] + 3.0 * here + 0.5 * (z_up + z_down + x_up + x_down + below + above)
        diag[row] = diagonal
        inverse[row] = jnp.where(in_box, 1.0 / diagonal, 0.0)
        face_x[row] = 0.5 * (here + x_up)
        face_z[row] = jnp.where(top, 0.0, 0.5 * (here + z_up))
        face_r[row] = zeros if low_end else 0.5 * (here + below)

    def span(first, count, place):
        def body(row, carry):
            weights(row, row + (place - first))
            return carry

        loop_rows(first, first + count, 4, body)

    span(0, UP - 1, -DG)
    weights(UP - 1, OV - 1, high_end=True)
    weights(OWN0, -OV, low_end=True)
    span(OWN0 + 1, OWN - 2, 1 - OV)
    weights(DOWN0 - 1, CR + OV - 1, high_end=True)
    weights(DOWN0, CR - OV, low_end=True)
    span(DOWN0 + 1, UP - 1, CR - OV + 1)
    face_r[ROWS] = zeros
    est[0] = zeros
    est[ROWS + 1] = zeros

    def around(row, here, below, above):
        fx = face_x[row]
        fz = face_z[row]
        summed = face_r[row] * below + face_r[row + 1] * above
        summed += fx * turn(here, -1) + turn(fx * here, 1)
        return summed + (fz * turn(here, -1, 0) + turn(fz * here, 1, 0))

    def solve(low, high):
        def begin(row, carry):
            first = inverse[row] * rhs[row] * (1.0 / MIDDLE)
            est[row + 1] = first
            upd[row] = first
            return carry

        loop_rows(low, high, 4, begin)
        for number, (keep, gain) in enumerate(chebyshev()):
            def sweep(row, carry):
                below, here = carry
                above = est[row + 2]
                summed = rhs[row] + around(row, here, below, above)
                step = keep * upd[row] + gain * (inverse[row] * summed - here)
                upd[row] = step
                est[row + 1] = here + step
                return here, above

            start = low + number + 1
            loop_rows(start, high - number - 1, 4, sweep, (est[start], est[start + 1]))

    solve(0, ROWS)

    reach = SWEEPS + 1
    to_low = any_of(wide, (126, 130), (249, 253))
    to_high = any_of(wide, (131, 135), (254, 256), (0, 2))

    def joined(value):
        other = jnp.where(to_low, turn(value, -TWIN), jnp.where(to_high, turn(value, TWIN), 0.0))
        return value + other

    for place in range(-reach, CR + reach):
        parts = []
        if place < OV:
            parts.append(est[place + DG + 1])
        if -OV <= place < CR + OV:
            parts.append(est[OWN0 + OV + place + 1])
        if place >= CR - OV:
            parts.append(est[DOWN0 + OV - CR + place + 1])
        value = joined(sum(parts[1:], parts[0]))
        if place < 0:
            value = jnp.where(far_wide, value, 0.0)
        total[place + reach] = value

    def remainder(row, place):
        at = place + reach
        here = total[at]
        summed = around(row, here, total[at - 1], total[at + 1])
        return jnp.where(core, rhs[row] - (diag[row] * here - summed), 0.0)

    def remain_own(row, carry):
        rhs[row] = remainder(row, row - (OWN0 + OV))
        return carry

    loop_rows(OWN0 + OV, OWN0 + OV + CR, 4, remain_own)
    for layer in range(SWEEPS):
        row = DG - 1 - layer
        rhs[row] = jnp.where(far_wide, remainder(row, -1 - layer), 0.0)
        row = DOWN0 + OV + layer
        rhs[row] = remainder(row, CR + layer)

    cut = DG - SWEEPS
    solve(cut, ROWS - cut)

    for place in range(CR):
        value = est[OWN0 + OV + place + 1]
        if place < OV:
            value = value + est[place + DG + 1]
        if place >= CR - OV:
            value = value + est[DOWN0 + OV - CR + place + 1]
        value = total[place + reach] + joined(value)
        out[pl.ds(odd * (CR - 1 - 2 * place) + place, NZ, stride=CR), :] = value[:, :CA]


def body(source, conduct, solid):
    aisles = lax.axis_size("aisle")
    rows = lax.axis_size("row")
    flat = (NZ * CR, CA)
    tile = lambda *lead: jax.ShapeDtypeStruct(lead + (NZ, CA), jnp.float32)
    main, to_left, to_right = pl.pallas_call(
        pack_edges, out_shape=(tile(3, CR), tile(CR // 2), tile(CR // 2)), name="pack_edges"
    )(source.reshape(flat), conduct.reshape(flat), solid.reshape(flat))
    up = [(i, (i + 1) % aisles) for i in range(aisles)]
    from_left = lax.ppermute(to_right, "aisle", up)
    from_right = lax.ppermute(to_left, "aisle", [(b, a) for a, b in up])
    strips, to_far, to_near = pl.pallas_call(
        pack_rows, out_shape=(tile(CR), tile(TILES), tile(TILES)), name="pack_rows"
    )(main, from_right, from_left)
    far_pairs = [(i, i + 1) for i in range(1, rows - 1, 2)]
    far = lax.ppermute(to_far, "row", far_pairs + [(b, a) for a, b in far_pairs])
    near = lax.ppermute(to_near, "row", [(i, i ^ 1) for i in range(rows)])
    rowbuf = lambda count: pltpu.VMEM((count, NZ, WIDE), jnp.float32)
    result = pl.pallas_call(
        solve_all,
        out_shape=jax.ShapeDtypeStruct(flat, jnp.float32),
        scratch_shapes=[
            rowbuf(CR + 2 * DK), rowbuf(CR + 2 * DG), rowbuf(ROWS), rowbuf(ROWS), rowbuf(ROWS + 1), rowbuf(ROWS),
            rowbuf(ROWS), rowbuf(ROWS), rowbuf(ROWS + 2), rowbuf(ROWS), rowbuf(CR + 2 * SWEEPS + 2),
        ],
        compiler_params=pltpu.CompilerParams(vmem_limit_bytes=16 * 1024 * 1024),
        name="solve_all",
    )(main, strips, far, near)
    return result.reshape(NZ, CR, CA)


def solution(mesh):
    spec = P(None, "row", "aisle")
    return jax.shard_map(body, mesh=mesh, in_specs=(spec, spec, spec), out_specs=spec, check_vma=False)
```

```python
import jax
import jax.numpy as jnp
from jax import lax
from jax.experimental import pallas as pl
from jax.experimental.pallas import tpu as pltpu
from jax.sharding import PartitionSpec as P

OV = 2
SWEEPS = 6
LOWER_END = 0.2
UPPER_END = 2.0
MIDDLE = 0.5 * (UPPER_END + LOWER_END)
SPREAD = 0.5 * (UPPER_END - LOWER_END)

NZ = 8
CR = 16
CA = 128
HALF = CA // 2
MIB = 1024 * 1024
DG = 2 * SWEEPS + 1
DK = DG + 1
TILES = 2 * DG + DK
SIDE = DG + OV
OWN = CR + 2 * OV
ROWS = 2 * SIDE + OWN
REACH = SWEEPS + 1
FAR_BOX = (-DG, SIDE, 0, 1)
OWN_BOX = (-OV, OWN, SIDE, SIDE + 2)
NEAR_BOX = (CR - OV, SIDE, SIDE + OWN, SIDE + OWN + 3)
GUARDED = ROWS + 4
TWIN = 3
GROUP = 8
STRIP = 7
RIGHT0 = 67
LEFT0 = 118
SPAN = 48
LEFT_AT = LEFT0 - RIGHT0


def coefficients():
    ratio = SPREAD / MIDDLE
    update = [1.0 / MIDDLE] + [0.0] * SWEEPS
    estimate = list(update)
    for _ in range(SWEEPS):
        image = [0.0] + estimate[:-1]
        remain = [float(n == 0) - e + i for n, (e, i) in enumerate(zip(estimate, image))]
        ratio_next = 1.0 / (2.0 * MIDDLE / SPREAD - ratio)
        update = [ratio_next * ratio * u + 2.0 * ratio_next / SPREAD * r for u, r in zip(update, remain)]
        estimate = [e + u for e, u in zip(estimate, update)]
        ratio = ratio_next
    return estimate


def lanes():
    return lax.broadcasted_iota(jnp.int32, (NZ, CA), 1)


def turn(value, by, axis=1):
    return pltpu.roll(value, by % value.shape[axis], axis)


def any_of(lane, *spans):
    mask = None
    for low, high in spans:
        here = (lane >= low) & (lane < high)
        mask = here if mask is None else mask | here
    return mask


def needed(layer):
    return (max(DK - 1 - layer, OV) + 1) // 2


def block_of(ref, first, count):
    return ref[pl.ds(first, count)]


def pack_block(fields, main, to_far, to_near, to_left, to_right):
    odd = lax.rem(lax.axis_index("row"), 2)
    lane = lax.broadcasted_iota(jnp.int32, (CR * NZ, CA), 1)
    order = jnp.where(lane < HALF, 2 * lane, 2 * lane - (CA - 1))
    left = right = jnp.zeros((CR * NZ, CA), jnp.float32)
    for number in range(3):
        rows = []
        for row in range(CR):
            at = pl.ds(odd * (CR - 1 - 2 * row) + row, NZ, stride=CR)
            rows.append(fields[number, at, :])
        field = jnp.take_along_axis(jnp.concatenate(rows), order, axis=1)
        rows = field.reshape(CR, NZ, CA)
        main[number] = rows
        depth = DK if number == 1 else DG
        start = (0, DG, DG + DK)[number]
        to_far[pl.ds(start, depth)] = jnp.stack([rows[depth - 1 - n] for n in range(depth)])
        to_near[pl.ds(start, depth)] = jnp.stack([rows[CR - 1 - n] for n in range(depth)])
        base = 16 * number
        left = jnp.where(any_of(lane, (base, base + 8)), turn(field, base), left)
        left = jnp.where(any_of(lane, (base + 8, base + 16)), turn(field, base + 8 - HALF), left)
        base = base + LEFT_AT
        right = jnp.where(any_of(lane, (base, base + 8)), turn(field, base + STRIP - HALF), right)
        right = jnp.where(any_of(lane, (base + 8, base + 16)), turn(field, base + 8 + STRIP - CA), right)
    half = CR * NZ // 2
    few = lane[:half] < SPAN
    to_left[...] = jnp.where(few, left[:half], turn(left[half:], SPAN)).reshape(CR // 2, NZ, CA)
    to_right[...] = jnp.where(few, turn(right[half:], -LEFT_AT), right[:half]).reshape(CR // 2, NZ, CA)


def slots(lane):
    return lax.rem(lane, 8), lax.rem(lane + 6, 8)


def pack_strips(from_right, from_left, strips, to_far, to_near):
    lane = lanes()
    in_right = lane < SPAN
    slot_right, slot_left = slots(lane)
    half = CR // 2
    rows = []
    for row in range(half):
        rows.append(jnp.where(in_right, from_right[row], from_left[row]))
    for row in range(half):
        rows.append(jnp.where(in_right, turn(from_right[row], -SPAN), turn(from_left[row], LEFT_AT)))
    strips[...] = jnp.stack(rows)
    around_left = any_of(lane, (LEFT_AT - 1, LEFT_AT + SPAN))
    for out, place in ((to_far, lambda q: q), (to_near, lambda q: CR - 1 - q)):
        for layer in range(DK // 2):
            first, second = needed(layer), needed(DK - 1 - layer)
            deep = rows[place(DK - 1 - layer)]
            takes_right = in_right & (slot_right >= 8 - second)
            takes_left = around_left & (slot_left >= 8 - first - second) & (slot_left < 8 - first)
            value = jnp.where(takes_left, turn(deep, -first), rows[place(layer)])
            out[layer] = jnp.where(takes_right, turn(deep, 8 - second), value)


def unpack_strips(pairs, lane):
    slot_right, slot_left = slots(lane)
    half = DK // 2
    near_part = [pairs[layer] for layer in range(half)]
    deep_part = []
    for layer in reversed(range(half)):
        first, second = needed(layer), needed(DK - 1 - layer)
        right = (lane < SPAN) & (slot_right < second)
        left = any_of(lane, (LEFT_AT, LEFT_AT + SPAN)) & (slot_left >= 8 - second)
        value = jnp.where(left, turn(pairs[layer], first), 0.0)
        deep_part.append(jnp.where(right, turn(pairs[layer], second - 8), value))
    return near_part + deep_part


def expand(block, strip, number, fill):
    lane = lax.broadcasted_iota(jnp.int32, block.shape, 2)
    beside = any_of(lane, (RIGHT0, RIGHT0 + STRIP), (LEFT0, LEFT0 + STRIP))
    tiles = []
    for colour in range(2):
        part = turn(block, HALF, 2) if colour else block
        value = jnp.where(beside, turn(strip, RIGHT0 - 16 * number - 8 * colour, 2), 0.0)
        tiles.append(jnp.where(lane < HALF, part, value))
    if fill:
        low = any_of(lane, (64, 65), (125, 126))
        high = any_of(lane, (66, 67), (127, 128))
        tiles = [jnp.where(low, turn(v, -TWIN, 2), jnp.where(high, turn(v, TWIN, 2), v)) for v in tiles]
    return jnp.stack(tiles, axis=1)


def spread(here, shift):
    level = lax.broadcasted_iota(jnp.int32, here.shape, 2)
    even, uneven = here[:, 0], here[:, 1]
    after, before = turn(even, -1, 2), turn(uneven, 1, 2)
    x_up = jnp.stack([uneven, after], axis=1)
    x_both = jnp.stack([uneven + before, even + after], axis=1)
    z_up = turn(here, -1, 2)
    z_both = jnp.where(level == NZ - 1, 0.0, z_up) + jnp.where(level == 0, 0.0, turn(here, 1, 2))
    part = shift + 3.0 * here + 0.5 * (z_both + x_both)
    return 0.5 * (here + x_up), jnp.where(level == NZ - 1, 0.0, 0.5 * (here + z_up)), part


def prepare_own(main, strips, rhs, cond, face_x, face_z, part):
    for first in range(0, CR, 8):
        at = pl.ds(first, 8)
        strip = strips[at]
        rhs[at] = expand(main[0, at], strip, 0, False)
        cond[at] = expand(main[1, at], strip, 1, True)
        shift = expand(main[2, at], strip, 2, True)
        face_x[at], face_z[at], part[at] = spread(cond[at], shift)


def solve_all(own_rhs, own_cond, own_x, own_z, own_part, far, near, far_strips, near_strips, out,
              cond, face_x, face_z, face_r, part, inverse, rhs, est_a, est_b, total):
    row_at = lax.axis_index("row")
    odd = lax.rem(row_at, 2)
    far_there = jnp.where(odd == 0, row_at > 0, row_at < lax.axis_size("row") - 1)
    far_level = far_there.astype(jnp.float32)
    far_tile = jnp.full((NZ, CA), far_level) > 0.5
    lane = lanes()

    own = pl.ds(DK, CR)
    cond[own] = own_cond[...]
    face_x[own] = own_x[...]
    face_z[own] = own_z[...]
    part[own] = own_part[...]
    p0, count, at, guarded = OWN_BOX
    zeros = jnp.zeros((1, 2, NZ, CA), jnp.float32)
    rhs[pl.ds(at + OV, CR)] = own_rhs[...]
    for row in (SIDE - 2, SIDE - 1, SIDE, SIDE + 1, SIDE + OWN - 2, SIDE + OWN - 1, SIDE + OWN, SIDE + OWN + 1):
        rhs[pl.ds(row, 1)] = zeros
    for est in (est_a, est_b):
        for row in (0, SIDE + 1, SIDE + OWN + 2, GUARDED - 1):
            est[pl.ds(row, 1)] = zeros

    for block, pairs, is_far in ((far, far_strips, True), (near, near_strips, False)):
        strip = unpack_strips(pairs, lane)
        strip = strip[::-1] if is_far else strip
        for low, high in ((0, 7), (7, DK)):
            at = pl.ds((0 if is_far else DK + CR) + low, high - low)
            cond[at] = expand(block[pl.ds(DG + low, high - low)], jnp.stack(strip[low:high]), 1, True)
        strip = strip[1:] if is_far else strip[:DG]
        for low, high in ((0, 7), (7, DG)):
            beside = jnp.stack(strip[low:high])
            at = pl.ds((0 if is_far else NEAR_BOX[2] + OV) + low, high - low)
            rhs[at] = expand(block[pl.ds(low, high - low)], beside, 0, False)
            shift = expand(block[pl.ds(DG + DK + low, high - low)], beside, 2, True)
            if is_far:
                shift = jnp.where(far_tile, shift, 1.0)
            at = pl.ds((1 if is_far else DK + CR) + low, high - low)
            face_x[at], face_z[at], part[at] = spread(cond[at], shift)

    for low in range(1, 2 * DG + CR + 2, 7):
        count = min(7, 2 * DG + CR + 2 - low)
        face_r[pl.ds(low, count)] = 0.5 * (cond[pl.ds(low - 1, count)] + cond[pl.ds(low, count)])

    both = lax.broadcasted_iota(jnp.int32, (2, NZ, CA), 2)
    in_box = any_of(both, (0, 65), (66, 74), (118, 126), (127, 128))
    core = any_of(both, (0, 64), (67, 74), (118, 125))

    def invert(box, first, count, has_below=True, has_above=True):
        p0, _, at, _ = box
        place = p0 + first + DK
        diagonal = part[pl.ds(place, count)]
        if has_below:
            diagonal += 0.5 * cond[pl.ds(place - 1, count)]
        if has_above:
            diagonal += 0.5 * cond[pl.ds(place + 1, count)]
        good = in_box & (diagonal > 0.0)
        inverse[pl.ds(at + first, count)] = jnp.where(good, 1.0 / jnp.where(good, diagonal, 1.0), 0.0)

    for low, high in ((0, 7), (7, SIDE - 1)):
        invert(FAR_BOX, low, high - low)
        invert(NEAR_BOX, low + 1, high - low)
    invert(FAR_BOX, SIDE - 1, 1, has_above=False)
    invert(NEAR_BOX, 0, 1, has_below=False)
    for low, high in ((1, 7), (7, 13), (13, OWN - 1)):
        invert(OWN_BOX, low, high - low)
    invert(OWN_BOX, 0, 1, has_below=False)
    invert(OWN_BOX, OWN - 1, 1, has_above=False)

    def around(p, count, here, below, above):
        at = pl.ds(p + DK, count)
        fx, fz = face_x[at], face_z[at]
        even, uneven = here[:, 0], here[:, 1]
        summed = face_r[at] * below + face_r[pl.ds(p + DK + 1, count)] * above
        summed += fz * turn(here, -1, 2) + turn(fz * here, 1, 2)
        sum_even = fx[:, 0] * uneven + turn(fx[:, 1] * uneven, 1, 2)
        sum_odd = fx[:, 0] * even + fx[:, 1] * turn(even, -1, 2)
        return summed + jnp.stack([sum_even, sum_odd], axis=1)

    powers = coefficients()

    def pieces(low, high):
        number = -(-(high - low) // GROUP)
        cuts = [low + (high - low) * n // number for n in range(number + 1)]
        return zip(cuts[:-1], cuts[1:])

    def solve(spans):
        for (p0, _, at, guarded), (low, high) in zip((FAR_BOX, OWN_BOX, NEAR_BOX), spans(0)):
            for first, last in pieces(low, high):
                here = pl.ds(at + first, last - first)
                est_a[pl.ds(guarded + first, last - first)] = powers[-1] * (inverse[here] * rhs[here])
        source, target = est_a, est_b
        for number, power in enumerate(reversed(powers[:-1])):
            for (p0, _, at, guarded), (low, high) in zip((FAR_BOX, OWN_BOX, NEAR_BOX), spans(number + 1)):
                for first, last in pieces(low, high):
                    count = last - first
                    here, below, above = [source[pl.ds(guarded + first + n, count)] for n in (0, -1, 1)]
                    summed = power * rhs[pl.ds(at + first, count)] + around(p0 + first, count, here, below, above)
                    target[pl.ds(guarded + first, count)] = inverse[pl.ds(at + first, count)] * summed
            source, target = target, source

    solve(lambda done: ((done, SIDE), (0, OWN), (0, SIDE - done)))
    est = est_a if SWEEPS % 2 == 0 else est_b

    to_low = any_of(both, (63, 65), (124, 126))
    to_high = any_of(both, (66, 68), (127, 128), (0, 1))

    def joined(value):
        other = jnp.where(to_low, turn(value, -TWIN, 3), jnp.where(to_high, turn(value, TWIN, 3), 0.0))
        return value + other

    def summed_boxes(p, count):
        value = None
        for p0, rows, _, guarded in (FAR_BOX, OWN_BOX, NEAR_BOX):
            if p0 <= p and p + count <= p0 + rows:
                share = est[pl.ds(guarded + p - p0, count)]
                value = share if value is None else value + share
        return value

    for low, high in ((-REACH, -OV), (-OV, 0), (0, OV), (OV, 8), (8, CR - OV), (CR - OV, CR + OV), (CR + OV, CR + REACH)):
        value = joined(summed_boxes(low, high - low))
        if low < 0:
            value = jnp.where(far_tile, value, 0.0)
        total[pl.ds(low + REACH, high - low)] = value

    def remainder(box, p, count):
        p0, _, at, _ = box
        here, below, above = [total[pl.ds(p + REACH + n, count)] for n in (0, -1, 1)]
        place = p + DK
        diagonal = part[pl.ds(place, count)] + 0.5 * (cond[pl.ds(place - 1, count)] + cond[pl.ds(place + 1, count)])
        summed = around(p, count, here, below, above)
        here_rhs = pl.ds(at + p - p0, count)
        value = jnp.where(core, rhs[here_rhs] - (diagonal * here - summed), 0.0)
        if p < 0:
            value = jnp.where(far_tile, value, 0.0)
        rhs[here_rhs] = value

    remainder(FAR_BOX, -SWEEPS, SWEEPS)
    for p in range(0, CR, 8):
        remainder(OWN_BOX, p, 8)
    remainder(NEAR_BOX, CR, SWEEPS)

    def second(done):
        cut = max(0, done + OV - SWEEPS)
        return (DG - SWEEPS + done, SIDE), (cut, OWN - cut), (0, SWEEPS + OV - done)

    solve(second)

    order = lax.div(lane, 2) + HALF * lax.rem(lane, 2)
    for low, high in ((0, OV), (OV, 8), (8, CR - OV), (CR - OV, CR)):
        value = joined(summed_boxes(low, high - low)) + total[pl.ds(low + REACH, high - low)]
        value = jnp.where(lane < HALF, value[:, 0], turn(value[:, 1], HALF, 2))
        value = value.reshape((high - low) * NZ, CA)
        value = jnp.take_along_axis(value, jnp.concatenate([order] * (high - low)), axis=1)
        for n in range(high - low):
            row = low + n
            out[pl.ds(odd * (CR - 1 - 2 * row) + row, NZ, stride=CR), :] = value[n * NZ : (n + 1) * NZ]


def call(kernel, outs, *args, scratch=(), limit=4):
    vmem = pl.BlockSpec(memory_space=pltpu.VMEM)
    return pl.pallas_call(
        kernel,
        out_shape=outs,
        in_specs=[vmem] * len(args),
        out_specs=jax.tree.map(lambda _: vmem, outs),
        scratch_shapes=scratch,
        compiler_params=pltpu.CompilerParams(vmem_limit_bytes=limit * MIB),
        name=kernel.__name__,
    )(*args)


def body(source, conduct, solid):
    aisles = lax.axis_size("aisle")
    rows = lax.axis_size("row")
    flat = (NZ * CR, CA)
    tile = lambda *lead: jax.ShapeDtypeStruct(lead + (NZ, CA), jnp.float32)
    fields = jnp.stack([source, conduct, 0.05 + 20.0 * solid.astype(jnp.float32)])
    main, to_far, to_near, to_left, to_right = call(
        pack_block,
        (tile(3, CR), tile(TILES), tile(TILES), tile(CR // 2), tile(CR // 2)),
        fields.reshape((3,) + flat),
    )
    up = [(i, (i + 1) % aisles) for i in range(aisles)]
    far_pairs = [(i, i + 1) for i in range(1, rows - 1, 2)]
    far_pairs += [(b, a) for a, b in far_pairs]
    near_pairs = [(i, i ^ 1) for i in range(rows)]
    from_left = lax.ppermute(to_right, "aisle", up)
    from_right = lax.ppermute(to_left, "aisle", [(b, a) for a, b in up])
    far = lax.ppermute(to_far, "row", far_pairs)
    near = lax.ppermute(to_near, "row", near_pairs)
    strips, strips_far, strips_near = call(
        pack_strips, (tile(CR), tile(DK // 2), tile(DK // 2)), from_right, from_left
    )
    far_strips = lax.ppermute(strips_far, "row", far_pairs)
    near_strips = lax.ppermute(strips_near, "row", near_pairs)
    own = call(prepare_own, (tile(CR, 2),) * 5, main, strips)
    pair_rows = lambda count: pltpu.VMEM((count, 2, NZ, CA), jnp.float32)
    around = CR + 2 * DK
    result = call(
        solve_all,
        jax.ShapeDtypeStruct(flat, jnp.float32),
        *own, far, near, far_strips, near_strips,
        scratch=[
            pair_rows(around), pair_rows(around), pair_rows(around), pair_rows(around), pair_rows(around),
            pair_rows(ROWS), pair_rows(ROWS), pair_rows(GUARDED), pair_rows(GUARDED), pair_rows(CR + 2 * REACH),
        ],
        limit=16,
    )
    return result.reshape(NZ, CR, CA)


def solution(mesh):
    spec = P(None, "row", "aisle")
    return jax.shard_map(body, mesh=mesh, in_specs=(spec, spec, spec), out_specs=spec, check_vma=False)
```

```python
import jax
import jax.numpy as jnp
from jax import lax
from jax.experimental import pallas as pl
from jax.experimental.pallas import tpu as pltpu
from jax.sharding import PartitionSpec as P

OV = 2
SWEEPS = 6
LOWER_END = 0.2
UPPER_END = 2.0
MIDDLE = 0.5 * (UPPER_END + LOWER_END)
SPREAD = 0.5 * (UPPER_END - LOWER_END)

NZ = 8
CR = 16
CA = 128
HALF = CA // 2
MIB = 1024 * 1024
DG = 2 * SWEEPS + 1
DK = DG + 1
TILES = 2 * DG + DK
SIDE = DG + OV
OWN = CR + 2 * OV
ROWS = 2 * SIDE + OWN
REACH = SWEEPS + 1
FAR_BOX = (-DG, SIDE, 0, 1)
OWN_BOX = (-OV, OWN, SIDE, SIDE + 2)
NEAR_BOX = (CR - OV, SIDE, SIDE + OWN, SIDE + OWN + 3)
GUARDED = ROWS + 4
TWIN = 3
GROUP = 8
STRIP = 7
RIGHT0 = 67
LEFT0 = 118
SPAN = 48
LEFT_AT = LEFT0 - RIGHT0


def coefficients():
    ratio = SPREAD / MIDDLE
    update = [1.0 / MIDDLE] + [0.0] * SWEEPS
    estimate = list(update)
    for _ in range(SWEEPS):
        image = [0.0] + estimate[:-1]
        remain = [float(n == 0) - e + i for n, (e, i) in enumerate(zip(estimate, image))]
        ratio_next = 1.0 / (2.0 * MIDDLE / SPREAD - ratio)
        update = [ratio_next * ratio * u + 2.0 * ratio_next / SPREAD * r for u, r in zip(update, remain)]
        estimate = [e + u for e, u in zip(estimate, update)]
        ratio = ratio_next
    return estimate


LEAD = coefficients()[-1]
POWERS = [power / LEAD for power in coefficients()[:-1]]


def lanes():
    return lax.broadcasted_iota(jnp.int32, (NZ, CA), 1)


def turn(value, by, axis=1):
    return pltpu.roll(value, by % value.shape[axis], axis)


def any_of(lane, *spans):
    mask = None
    for low, high in spans:
        here = (lane >= low) & (lane < high)
        mask = here if mask is None else mask | here
    return mask


def needed(layer):
    return (max(DK - 1 - layer, OV) + 1) // 2


def block_of(ref, first, count):
    return ref[pl.ds(first, count)]


def pack_edges(source, conduct, shift, main, to_other, to_pair):
    odd = lax.rem(lax.axis_index("row"), 2)
    lane = lax.broadcasted_iota(jnp.int32, (CR * NZ, CA), 1)
    order = jnp.where(lane < HALF, 2 * lane, 2 * lane - (CA - 1))
    left = right = jnp.zeros((CR * NZ, CA), jnp.float32)
    for number, (field, scale) in enumerate(((source, 2.0 * LEAD), (conduct, 1.0), (shift, 1.0))):
        rows = []
        for row in range(CR):
            at = pl.ds(odd * (CR - 1 - 2 * row) + row, NZ, stride=CR)
            rows.append(field[at, :])
        field = scale * jnp.take_along_axis(jnp.concatenate(rows), order, axis=1)
        main[number] = field.reshape(CR, NZ, CA)
        base = 16 * number
        left = jnp.where(any_of(lane, (base, base + 8)), turn(field, base), left)
        left = jnp.where(any_of(lane, (base + 8, base + 16)), turn(field, base + 8 - HALF), left)
        base = base + LEFT_AT
        right = jnp.where(any_of(lane, (base, base + 8)), turn(field, base + STRIP - HALF), right)
        right = jnp.where(any_of(lane, (base + 8, base + 16)), turn(field, base + 8 + STRIP - CA), right)
    half = CR * NZ // 2
    few = lane[:half] < SPAN
    left = jnp.where(few, left[:half], turn(left[half:], SPAN)).reshape(CR // 2, NZ, CA)
    right = jnp.where(few, turn(right[half:], -LEFT_AT), right[:half]).reshape(CR // 2, NZ, CA)
    uneven = odd_aisle()
    to_pair[...] = jnp.where(uneven, left, right)
    to_other[...] = jnp.where(uneven, right, left)


def odd_aisle():
    return jnp.full((NZ, CA), lax.rem(lax.axis_index("aisle"), 2)) > 0


def pack_rows(main, to_far, to_near):
    start = 0
    for number, depth in enumerate((DG, DK, DG)):
        to_far[pl.ds(start, depth)] = jnp.stack([main[number, depth - 1 - n] for n in range(depth)])
        to_near[pl.ds(start, depth)] = jnp.stack([main[number, CR - 1 - n] for n in range(depth)])
        start += depth


def slots(lane):
    return lax.rem(lane, 8), lax.rem(lane + 6, 8)


def pack_strips(from_other, from_pair, strips, to_far, to_near):
    lane = lanes()
    in_right = lane < SPAN
    slot_right, slot_left = slots(lane)
    uneven = odd_aisle()
    from_right = jnp.where(uneven, from_other[...], from_pair[...])
    from_left = jnp.where(uneven, from_pair[...], from_other[...])
    half = CR // 2
    rows = []
    for row in range(half):
        rows.append(jnp.where(in_right, from_right[row], from_left[row]))
    for row in range(half):
        rows.append(jnp.where(in_right, turn(from_right[row], -SPAN), turn(from_left[row], LEFT_AT)))
    strips[...] = jnp.stack(rows)
    around_left = any_of(lane, (LEFT_AT - 1, LEFT_AT + SPAN))
    for out, place in ((to_far, lambda q: q), (to_near, lambda q: CR - 1 - q)):
        for layer in range(DK // 2):
            first, second = needed(layer), needed(DK - 1 - layer)
            deep = rows[place(DK - 1 - layer)]
            takes_right = in_right & (slot_right >= 8 - second)
            takes_left = around_left & (slot_left >= 8 - first - second) & (slot_left < 8 - first)
            value = jnp.where(takes_left, turn(deep, -first), rows[place(layer)])
            out[layer] = jnp.where(takes_right, turn(deep, 8 - second), value)


def unpack_strips(pairs, lane):
    slot_right, slot_left = slots(lane)
    half = DK // 2
    near_part = [pairs[layer] for layer in range(half)]
    deep_part = []
    for layer in reversed(range(half)):
        first, second = needed(layer), needed(DK - 1 - layer)
        right = (lane < SPAN) & (slot_right < second)
        left = any_of(lane, (LEFT_AT, LEFT_AT + SPAN)) & (slot_left >= 8 - second)
        value = jnp.where(left, turn(pairs[layer], first), 0.0)
        deep_part.append(jnp.where(right, turn(pairs[layer], second - 8), value))
    return near_part + deep_part


def expand(block, strip, number, fill):
    lane = lax.broadcasted_iota(jnp.int32, block.shape, 2)
    beside = any_of(lane, (RIGHT0, RIGHT0 + STRIP), (LEFT0, LEFT0 + STRIP))
    tiles = []
    for colour in range(2):
        part = turn(block, HALF, 2) if colour else block
        value = jnp.where(beside, turn(strip, RIGHT0 - 16 * number - 8 * colour, 2), 0.0)
        tiles.append(jnp.where(lane < HALF, part, value))
    if fill:
        low = any_of(lane, (64, 65), (125, 126))
        high = any_of(lane, (66, 67), (127, 128))
        tiles = [jnp.where(low, turn(v, -TWIN, 2), jnp.where(high, turn(v, TWIN, 2), v)) for v in tiles]
    return jnp.stack(tiles, axis=1)


def spread(here, shift):
    level = lax.broadcasted_iota(jnp.int32, here.shape, 2)
    even, uneven = here[:, 0], here[:, 1]
    after, before = turn(even, -1, 2), turn(uneven, 1, 2)
    x_up = jnp.stack([uneven, after], axis=1)
    x_both = jnp.stack([uneven + before, even + after], axis=1)
    z_up = turn(here, -1, 2)
    z_both = jnp.where(level == NZ - 1, 0.0, z_up) + jnp.where(level == 0, 0.0, turn(here, 1, 2))
    part = shift + 6.0 * here + (z_both + x_both)
    return here + x_up, jnp.where(level == NZ - 1, 0.0, here + z_up), part


def prepare_own(main, strips, rhs, cond, face_x, face_z, part):
    for first in range(0, CR, 8):
        at = pl.ds(first, 8)
        strip = strips[at]
        rhs[at] = expand(main[0, at], strip, 0, False)
        cond[at] = expand(main[1, at], strip, 1, True)
        shift = expand(main[2, at], strip, 2, True)
        face_x[at], face_z[at], part[at] = spread(cond[at], shift)


def solve_all(own_rhs, own_cond, own_x, own_z, own_part, near, far, far_strips, near_strips, out,
              cond, face_x, face_z, face_r, part, inverse, rhs, est_a, est_b, total):
    row_at = lax.axis_index("row")
    odd = lax.rem(row_at, 2)
    far_there = jnp.where(odd == 0, row_at > 0, row_at < lax.axis_size("row") - 1)
    far_level = far_there.astype(jnp.float32)
    far_tile = jnp.full((NZ, CA), far_level) > 0.5
    lane = lanes()

    own = pl.ds(DK, CR)
    cond[own] = own_cond[...]
    face_x[own] = own_x[...]
    face_z[own] = own_z[...]
    part[own] = own_part[...]
    p0, count, at, guarded = OWN_BOX
    zeros = jnp.zeros((1, 2, NZ, CA), jnp.float32)
    rhs[pl.ds(at + OV, CR)] = own_rhs[...]
    for row in (SIDE - 2, SIDE - 1, SIDE, SIDE + 1, SIDE + OWN - 2, SIDE + OWN - 1, SIDE + OWN, SIDE + OWN + 1):
        rhs[pl.ds(row, 1)] = zeros
    for est in (est_a, est_b):
        for row in (0, SIDE + 1, SIDE + OWN + 2, GUARDED - 1):
            est[pl.ds(row, 1)] = zeros

    for block, pairs, is_far in ((far, far_strips, True), (near, near_strips, False)):
        strip = unpack_strips(pairs, lane)
        strip = strip[::-1] if is_far else strip
        for low, high in ((0, 7), (7, DK)):
            at = pl.ds((0 if is_far else DK + CR) + low, high - low)
            cond[at] = expand(block[pl.ds(DG + low, high - low)], jnp.stack(strip[low:high]), 1, True)
        strip = strip[1:] if is_far else strip[:DG]
        for low, high in ((0, 7), (7, DG)):
            beside = jnp.stack(strip[low:high])
            at = pl.ds((0 if is_far else NEAR_BOX[2] + OV) + low, high - low)
            rhs[at] = expand(block[pl.ds(low, high - low)], beside, 0, False)
            shift = expand(block[pl.ds(DG + DK + low, high - low)], beside, 2, True)
            if is_far:
                shift = jnp.where(far_tile, shift, 2.0)
            at = pl.ds((1 if is_far else DK + CR) + low, high - low)
            face_x[at], face_z[at], part[at] = spread(cond[at], shift)

    for low in range(1, 2 * DG + CR + 2, 7):
        count = min(7, 2 * DG + CR + 2 - low)
        face_r[pl.ds(low, count)] = cond[pl.ds(low - 1, count)] + cond[pl.ds(low, count)]

    both = lax.broadcasted_iota(jnp.int32, (2, NZ, CA), 2)
    in_box = any_of(both, (0, 65), (66, 74), (118, 126), (127, 128))
    core = any_of(both, (0, 64), (67, 74), (118, 125))

    def invert(box, first, count, has_below=True, has_above=True):
        p0, _, at, _ = box
        place = p0 + first + DK
        diagonal = part[pl.ds(place, count)]
        if has_below:
            diagonal += cond[pl.ds(place - 1, count)]
        if has_above:
            diagonal += cond[pl.ds(place + 1, count)]
        good = in_box & (diagonal > 0.0)
        inverse[pl.ds(at + first, count)] = jnp.where(good, 1.0 / jnp.where(good, diagonal, 1.0), 0.0)

    for low, high in ((0, 7), (7, SIDE - 1)):
        invert(FAR_BOX, low, high - low)
        invert(NEAR_BOX, low + 1, high - low)
    invert(FAR_BOX, SIDE - 1, 1, has_above=False)
    invert(NEAR_BOX, 0, 1, has_below=False)
    for low, high in ((1, 7), (7, 13), (13, OWN - 1)):
        invert(OWN_BOX, low, high - low)
    invert(OWN_BOX, 0, 1, has_below=False)
    invert(OWN_BOX, OWN - 1, 1, has_above=False)

    def around(p, count, here, below, above):
        at = pl.ds(p + DK, count)
        fx, fz = face_x[at], face_z[at]
        even, uneven = here[:, 0], here[:, 1]
        summed = face_r[at] * below + face_r[pl.ds(p + DK + 1, count)] * above
        summed += fz * turn(here, -1, 2) + turn(fz * here, 1, 2)
        sum_even = fx[:, 0] * uneven + turn(fx[:, 1] * uneven, 1, 2)
        sum_odd = fx[:, 0] * even + fx[:, 1] * turn(even, -1, 2)
        return summed + jnp.stack([sum_even, sum_odd], axis=1)


    def pieces(low, high):
        number = -(-(high - low) // GROUP)
        cuts = [low + (high - low) * n // number for n in range(number + 1)]
        return zip(cuts[:-1], cuts[1:])

    def solve(spans):
        for (p0, _, at, guarded), (low, high) in zip((FAR_BOX, OWN_BOX, NEAR_BOX), spans(0)):
            for first, last in pieces(low, high):
                here = pl.ds(at + first, last - first)
                est_a[pl.ds(guarded + first, last - first)] = inverse[here] * rhs[here]
        source, target = est_a, est_b
        for number, power in enumerate(reversed(POWERS)):
            for (p0, _, at, guarded), (low, high) in zip((FAR_BOX, OWN_BOX, NEAR_BOX), spans(number + 1)):
                for first, last in pieces(low, high):
                    count = last - first
                    here, below, above = [source[pl.ds(guarded + first + n, count)] for n in (0, -1, 1)]
                    summed = power * rhs[pl.ds(at + first, count)] + around(p0 + first, count, here, below, above)
                    target[pl.ds(guarded + first, count)] = inverse[pl.ds(at + first, count)] * summed
            source, target = target, source

    solve(lambda done: ((done, SIDE), (0, OWN), (0, SIDE - done)))
    est = est_a if SWEEPS % 2 == 0 else est_b

    to_low = any_of(both, (63, 65), (124, 126))
    to_high = any_of(both, (66, 68), (127, 128), (0, 1))

    def joined(value):
        other = jnp.where(to_low, turn(value, -TWIN, 3), jnp.where(to_high, turn(value, TWIN, 3), 0.0))
        return value + other

    def summed_boxes(p, count):
        value = None
        for p0, rows, _, guarded in (FAR_BOX, OWN_BOX, NEAR_BOX):
            if p0 <= p and p + count <= p0 + rows:
                share = est[pl.ds(guarded + p - p0, count)]
                value = share if value is None else value + share
        return value

    for low, high in ((-REACH, -OV), (-OV, 0), (0, OV), (OV, 8), (8, CR - OV), (CR - OV, CR + OV), (CR + OV, CR + REACH)):
        value = joined(summed_boxes(low, high - low))
        if low < 0:
            value = jnp.where(far_tile, value, 0.0)
        total[pl.ds(low + REACH, high - low)] = value

    def remainder(box, p, count):
        p0, _, at, _ = box
        here, below, above = [total[pl.ds(p + REACH + n, count)] for n in (0, -1, 1)]
        place = p + DK
        diagonal = part[pl.ds(place, count)] + (cond[pl.ds(place - 1, count)] + cond[pl.ds(place + 1, count)])
        summed = around(p, count, here, below, above)
        here_rhs = pl.ds(at + p - p0, count)
        value = jnp.where(core, rhs[here_rhs] - LEAD * (diagonal * here - summed), 0.0)
        if p < 0:
            value = jnp.where(far_tile, value, 0.0)
        rhs[here_rhs] = value

    remainder(FAR_BOX, -SWEEPS, SWEEPS)
    for p in range(0, CR, 8):
        remainder(OWN_BOX, p, 8)
    remainder(NEAR_BOX, CR, SWEEPS)

    def second(done):
        cut = max(0, done + OV - SWEEPS)
        return (DG - SWEEPS + done, SIDE), (cut, OWN - cut), (0, SWEEPS + OV - done)

    solve(second)

    order = lax.div(lane, 2) + HALF * lax.rem(lane, 2)
    for low, high in ((0, OV), (OV, 8), (8, CR - OV), (CR - OV, CR)):
        value = joined(summed_boxes(low, high - low)) + total[pl.ds(low + REACH, high - low)]
        value = jnp.where(lane < HALF, value[:, 0], turn(value[:, 1], HALF, 2))
        value = value.reshape((high - low) * NZ, CA)
        value = jnp.take_along_axis(value, jnp.concatenate([order] * (high - low)), axis=1)
        for n in range(high - low):
            row = low + n
            out[pl.ds(odd * (CR - 1 - 2 * row) + row, NZ, stride=CR), :] = value[n * NZ : (n + 1) * NZ]


def call(kernel, outs, *args, scratch=(), limit=4, cost=None):
    vmem = pl.BlockSpec(memory_space=pltpu.VMEM)
    return pl.pallas_call(
        kernel,
        out_shape=outs,
        in_specs=[vmem] * len(args),
        out_specs=jax.tree.map(lambda _: vmem, outs),
        scratch_shapes=scratch,
        compiler_params=pltpu.CompilerParams(vmem_limit_bytes=limit * MIB),
        cost_estimate=cost,
        name=kernel.__name__,
    )(*args)


def body(source, conduct, solid):
    aisles = lax.axis_size("aisle")
    rows = lax.axis_size("row")
    flat = (NZ * CR, CA)
    tile = lambda *lead: jax.ShapeDtypeStruct(lead + (NZ, CA), jnp.float32)
    busy = pl.CostEstimate(flops=10**11, bytes_accessed=1024 * MIB, transcendentals=0)
    shift = 0.1 + 40.0 * solid.astype(jnp.float32)
    main, to_other, to_pair = call(
        pack_edges, (tile(3, CR), tile(CR // 2), tile(CR // 2)),
        source.reshape(flat), conduct.reshape(flat), shift.reshape(flat),
    )
    pair = [(i, i ^ 1) for i in range(aisles)]
    other = [(i, (i - 1 + 2 * (i % 2)) % aisles) for i in range(aisles)]
    far_pairs = [(i, i + 1) for i in range(1, rows - 1, 2)]
    far_pairs += [(b, a) for a, b in far_pairs]
    near_pairs = [(i, i ^ 1) for i in range(rows)]
    from_other = lax.ppermute(to_other, "aisle", other)
    from_pair = lax.ppermute(to_pair, "aisle", pair)
    to_far, to_near = call(
        pack_rows, (tile(TILES), tile(TILES)), main,
        cost=busy,
    )
    near = lax.ppermute(to_near, "row", near_pairs)
    far = lax.ppermute(to_far, "row", far_pairs)
    strips, strips_far, strips_near = call(
        pack_strips, (tile(CR), tile(DK // 2), tile(DK // 2)), from_other, from_pair
    )
    far_strips = lax.ppermute(strips_far, "row", far_pairs)
    near_strips = lax.ppermute(strips_near, "row", near_pairs)
    own = call(prepare_own, (tile(CR, 2),) * 5, main, strips, cost=busy)
    pair_rows = lambda count: pltpu.VMEM((count, 2, NZ, CA), jnp.float32)
    around = CR + 2 * DK
    result = call(
        solve_all,
        jax.ShapeDtypeStruct(flat, jnp.float32),
        *own, near, far, far_strips, near_strips,
        scratch=[
            pair_rows(around), pair_rows(around), pair_rows(around), pair_rows(around), pair_rows(around),
            pair_rows(ROWS), pair_rows(ROWS), pair_rows(GUARDED), pair_rows(GUARDED), pair_rows(CR + 2 * REACH),
        ],
        limit=16,
    )
    return result.reshape(NZ, CR, CA)


def solution(mesh):
    spec = P(None, "row", "aisle")
    return jax.shard_map(body, mesh=mesh, in_specs=(spec, spec, spec), out_specs=spec, check_vma=False)
```

```python
import jax
import jax.numpy as jnp
from jax import lax
from jax.experimental import pallas as pl
from jax.experimental.pallas import tpu as pltpu
from jax.sharding import PartitionSpec as P

OV = 2
SWEEPS = 6
LOWER_END = 0.2
UPPER_END = 2.0
MIDDLE = 0.5 * (UPPER_END + LOWER_END)
SPREAD = 0.5 * (UPPER_END - LOWER_END)

NZ = 8
CR = 16
CA = 128
HALF = CA // 2
MIB = 1024 * 1024
DG = 2 * SWEEPS + 1
DK = DG + 1
TILES = 2 * DG + DK
SIDE = DG + OV
OWN = CR + 2 * OV
ROWS = 2 * SIDE + OWN
REACH = SWEEPS + 1
FAR_BOX = (-DG, SIDE, 0, 1)
OWN_BOX = (-OV, OWN, SIDE, SIDE + 2)
NEAR_BOX = (CR - OV, SIDE, SIDE + OWN, SIDE + OWN + 3)
GUARDED = ROWS + 4
TWIN = 3
GROUP = 8
STRIP = 7
RIGHT0 = 67
LEFT0 = 118
SPAN = 48
LEFT_AT = LEFT0 - RIGHT0


def coefficients():
    ratio = SPREAD / MIDDLE
    update = [1.0 / MIDDLE] + [0.0] * SWEEPS
    estimate = list(update)
    for _ in range(SWEEPS):
        image = [0.0] + estimate[:-1]
        remain = [float(n == 0) - e + i for n, (e, i) in enumerate(zip(estimate, image))]
        ratio_next = 1.0 / (2.0 * MIDDLE / SPREAD - ratio)
        update = [ratio_next * ratio * u + 2.0 * ratio_next / SPREAD * r for u, r in zip(update, remain)]
        estimate = [e + u for e, u in zip(estimate, update)]
        ratio = ratio_next
    return estimate


LEAD = coefficients()[-1]
POWERS = [power / LEAD for power in coefficients()[:-1]]


def lanes():
    return lax.broadcasted_iota(jnp.int32, (NZ, CA), 1)


def turn(value, by, axis=1):
    return pltpu.roll(value, by % value.shape[axis], axis)


def any_of(lane, *spans):
    mask = None
    for low, high in spans:
        here = (lane >= low) & (lane < high)
        mask = here if mask is None else mask | here
    return mask


def needed(layer):
    return (max(DK - 1 - layer, OV) + 1) // 2


def block_of(ref, first, count):
    return ref[pl.ds(first, count)]


def pack_edges(source, conduct, shift, main, to_other, to_pair):
    odd = lax.rem(lax.axis_index("row"), 2)
    half = CR // 2
    shape = (half * NZ, CA)
    lane = lax.broadcasted_iota(jnp.int32, shape, 1)
    order = jnp.where(lane < HALF, 2 * lane, 2 * lane - (CA - 1))

    def edge(slot, first):
        return first + 2 * lax.rem(slot, 8) + lax.rem(lax.div(slot, 8), 2)

    end = CA - 2 * STRIP
    left_order = edge(lane, 0)
    right_order = jnp.where(lane < SPAN, edge(lane, end), edge(lane + (16 * 4 - LEFT_AT), end))
    right_order = jnp.minimum(right_order, CA - 1)
    pick = lambda value, index: jnp.take_along_axis(value, index, axis=1)
    left = right = jnp.zeros(shape, jnp.float32)
    for number, (field, scale) in enumerate(((source, 2.0 * LEAD), (conduct, 1.0), (shift, 1.0))):
        for part in range(2):
            rows = []
            for row in range(part * half, (part + 1) * half):
                rows.append(field[pl.ds(odd * (CR - 1 - 2 * row) + row, NZ, stride=CR), :])
            rows = scale * jnp.concatenate(rows)
            main[number, pl.ds(part * half, half)] = pick(rows, order).reshape(half, NZ, CA)
            base = part * SPAN + 16 * number
            left = jnp.where(any_of(lane, (base, base + 16)), pick(rows, left_order), left)
            base = (1 - part) * LEFT_AT + 16 * number
            right = jnp.where(any_of(lane, (base, base + 16)), pick(rows, right_order), right)
    left = left.reshape(half, NZ, CA)
    right = right.reshape(half, NZ, CA)
    uneven = odd_aisle()
    to_pair[...] = jnp.where(uneven, left, right)
    to_other[...] = jnp.where(uneven, right, left)


def odd_aisle():
    return jnp.full((NZ, CA), lax.rem(lax.axis_index("aisle"), 2)) > 0


def pack_rows(main, to_far, to_near):
    start = 0
    for number, depth in enumerate((DG, DK, DG)):
        to_far[pl.ds(start, depth)] = jnp.stack([main[number, depth - 1 - n] for n in range(depth)])
        to_near[pl.ds(start, depth)] = jnp.stack([main[number, CR - 1 - n] for n in range(depth)])
        start += depth


def slots(lane):
    return lax.rem(lane, 8), lax.rem(lane + 6, 8)


def pack_strips(from_other, from_pair, strips, to_far, to_near):
    lane = lanes()
    in_right = lane < SPAN
    slot_right, slot_left = slots(lane)
    uneven = odd_aisle()
    from_right = jnp.where(uneven, from_other[...], from_pair[...])
    from_left = jnp.where(uneven, from_pair[...], from_other[...])
    half = CR // 2
    rows = []
    for row in range(half):
        rows.append(jnp.where(in_right, from_right[row], from_left[row]))
    for row in range(half):
        rows.append(jnp.where(in_right, turn(from_right[row], -SPAN), turn(from_left[row], LEFT_AT)))
    strips[...] = jnp.stack(rows)
    around_left = any_of(lane, (LEFT_AT - 1, LEFT_AT + SPAN))
    for out, place in ((to_far, lambda q: q), (to_near, lambda q: CR - 1 - q)):
        for layer in range(DK // 2):
            first, second = needed(layer), needed(DK - 1 - layer)
            deep = rows[place(DK - 1 - layer)]
            takes_right = in_right & (slot_right >= 8 - second)
            takes_left = around_left & (slot_left >= 8 - first - second) & (slot_left < 8 - first)
            value = jnp.where(takes_left, turn(deep, -first), rows[place(layer)])
            out[layer] = jnp.where(takes_right, turn(deep, 8 - second), value)


def unpack_strips(pairs, lane):
    slot_right, slot_left = slots(lane)
    half = DK // 2
    near_part = [pairs[layer] for layer in range(half)]
    deep_part = []
    for layer in reversed(range(half)):
        first, second = needed(layer), needed(DK - 1 - layer)
        right = (lane < SPAN) & (slot_right < second)
        left = any_of(lane, (LEFT_AT, LEFT_AT + SPAN)) & (slot_left >= 8 - second)
        value = jnp.where(left, turn(pairs[layer], first), 0.0)
        deep_part.append(jnp.where(right, turn(pairs[layer], second - 8), value))
    return near_part + deep_part


def merge(block, strip, number):
    lane = lax.broadcasted_iota(jnp.int32, block.shape, 2)
    beside = any_of(lane, (RIGHT0, RIGHT0 + STRIP), (LEFT0, LEFT0 + STRIP))
    tiles = []
    for colour in range(2):
        part = turn(block, HALF, 2) if colour else block
        value = jnp.where(beside, turn(strip, RIGHT0 - 16 * number - 8 * colour, 2), 0.0)
        tiles.append(jnp.where(lane < HALF, part, value))
    return jnp.stack(tiles, axis=1)


def fill(tiles):
    lane = lax.broadcasted_iota(jnp.int32, tiles.shape, 3)
    low = any_of(lane, (64, 65), (125, 126))
    high = any_of(lane, (66, 67), (127, 128))
    return jnp.where(low, turn(tiles, -TWIN, 3), jnp.where(high, turn(tiles, TWIN, 3), tiles))


def spread(here, shift):
    level = lax.broadcasted_iota(jnp.int32, here.shape, 2)
    even, uneven = here[:, 0], here[:, 1]
    after, before = turn(even, -1, 2), turn(uneven, 1, 2)
    x_up = jnp.stack([uneven, after], axis=1)
    x_both = jnp.stack([uneven + before, even + after], axis=1)
    z_up = turn(here, -1, 2)
    z_both = jnp.where(level == NZ - 1, 0.0, z_up) + jnp.where(level == 0, 0.0, turn(here, 1, 2))
    part = shift + 6.0 * here + (z_both + x_both)
    return here + x_up, jnp.where(level == NZ - 1, 0.0, here + z_up), part


def pieces(low, high):
    number = -(-(high - low) // GROUP)
    cuts = [low + (high - low) * n // number for n in range(number + 1)]
    return [(first, last - first) for first, last in zip(cuts[:-1], cuts[1:])]


def inverted(diagonal):
    both = lax.broadcasted_iota(jnp.int32, (2, NZ, CA), 2)
    good = any_of(both, (0, 65), (66, 74), (118, 126), (127, 128)) & (diagonal > 0.0)
    return jnp.where(good, 1.0 / jnp.where(good, diagonal, 1.0), 0.0)


def around(weights, row, count, here, below, above):
    face_x, face_z, face_r = weights
    at = pl.ds(row, count)
    fx, fz = face_x[at], face_z[at]
    even, uneven = here[:, 0], here[:, 1]
    summed = face_r[at] * below + face_r[pl.ds(row + 1, count)] * above
    summed += fz * turn(here, -1, 2) + turn(fz * here, 1, 2)
    sum_even = fx[:, 0] * uneven + turn(fx[:, 1] * uneven, 1, 2)
    sum_odd = fx[:, 0] * even + fx[:, 1] * turn(even, -1, 2)
    return summed + jnp.stack([sum_even, sum_odd], axis=1)


def prepare_own(main, strips, rhs, cond, face_x, face_z, face_r, part, inverse, levels):
    halves = [pl.ds(first, 8) for first in range(0, CR, 8)]
    for at in halves:
        strip = strips[at]
        cond[at] = merge(main[1, at], strip, 1)
        part[at] = merge(main[2, at], strip, 2)
        rhs[at] = merge(main[0, at], strip, 0)
    for at in halves:
        cond[at] = fill(cond[at])
        part[at] = fill(part[at])
    for at in halves:
        face_x[at], face_z[at], part[at] = spread(cond[at], part[at])
    face_r[pl.ds(0, 1)] = jnp.zeros((1, 2, NZ, CA), jnp.float32)
    for first, count in pieces(1, CR):
        face_r[pl.ds(first, count)] = cond[pl.ds(first - 1, count)] + cond[pl.ds(first, count)]
    for first, count in pieces(1, CR - 1):
        at = pl.ds(first, count)
        inverse[at] = inverted(part[at] + (cond[pl.ds(first - 1, count)] + cond[pl.ds(first + 1, count)]))
        levels[0, at] = inverse[at] * rhs[at]
    weights = face_x, face_z, face_r
    for done, power in enumerate(reversed(POWERS)):
        for first, count in pieces(2 + done, CR - 2 - done):
            here, below, above = [levels[done, pl.ds(first + n, count)] for n in (0, -1, 1)]
            at = pl.ds(first, count)
            levels[done + 1, at] = inverse[at] * (power * rhs[at] + around(weights, first, count, here, below, above))


def solve_all(own_rhs, own_cond, own_x, own_z, own_r, own_part, own_inverse, levels, near, far, far_strips, near_strips, out,
              cond, face_x, face_z, face_r, part, inverse, rhs, est_a, est_b, total):
    row_at = lax.axis_index("row")
    odd = lax.rem(row_at, 2)
    far_there = jnp.where(odd == 0, row_at > 0, row_at < lax.axis_size("row") - 1)
    far_level = far_there.astype(jnp.float32)
    far_tile = jnp.full((NZ, CA), far_level) > 0.5
    lane = lanes()

    own = pl.ds(DK, CR)
    cond[own] = own_cond[...]
    face_x[own] = own_x[...]
    face_z[own] = own_z[...]
    part[own] = own_part[...]
    p0, count, at, guarded = OWN_BOX
    zeros = jnp.zeros((1, 2, NZ, CA), jnp.float32)
    rhs[pl.ds(at + OV, CR)] = own_rhs[...]
    for row in (SIDE - 2, SIDE - 1, SIDE, SIDE + 1, SIDE + OWN - 2, SIDE + OWN - 1, SIDE + OWN, SIDE + OWN + 1):
        rhs[pl.ds(row, 1)] = zeros
    for est in (est_a, est_b):
        for row in (0, SIDE + 1, SIDE + OWN + 2, GUARDED - 1):
            est[pl.ds(row, 1)] = zeros

    sides = [(far, unpack_strips(far_strips, lane)[::-1], True), (near, unpack_strips(near_strips, lane), False)]
    for block, strip, is_far in sides:
        for low, high in ((0, 7), (7, DK)):
            at = pl.ds((0 if is_far else DK + CR) + low, high - low)
            cond[at] = merge(block[pl.ds(DG + low, high - low)], jnp.stack(strip[low:high]), 1)
        strip = strip[1:] if is_far else strip[:DG]
        for low, high in ((0, 7), (7, DG)):
            beside = jnp.stack(strip[low:high])
            at = pl.ds((1 if is_far else DK + CR) + low, high - low)
            part[at] = merge(block[pl.ds(DG + DK + low, high - low)], beside, 2)
            at = pl.ds((0 if is_far else NEAR_BOX[2] + OV) + low, high - low)
            rhs[at] = merge(block[pl.ds(low, high - low)], beside, 0)
    for first in (0, DK + CR):
        for low, high in ((0, 7), (7, DK)):
            at = pl.ds(first + low, high - low)
            cond[at] = fill(cond[at])
        for low, high in ((0, 7), (7, DG)):
            at = pl.ds((first or 1) + low, high - low)
            part[at] = fill(part[at])
    for first in (1, DK + CR):
        for low, high in ((0, 7), (7, DG)):
            at = pl.ds(first + low, high - low)
            shift = part[at]
            if first == 1:
                shift = jnp.where(far_tile, shift, 2.0)
            face_x[at], face_z[at], part[at] = spread(cond[at], shift)

    face_r[pl.ds(DK + 1, CR - 1)] = own_r[pl.ds(1, CR - 1)]
    for first, last in ((1, DK + 1), (DK + CR, 2 * DG + CR + 2)):
        for low, count in pieces(first, last):
            face_r[pl.ds(low, count)] = cond[pl.ds(low - 1, count)] + cond[pl.ds(low, count)]

    both = lax.broadcasted_iota(jnp.int32, (2, NZ, CA), 2)
    core = any_of(both, (0, 64), (67, 74), (118, 125))

    def invert(box, first, count, has_below=True, has_above=True):
        p0, _, at, _ = box
        place = p0 + first + DK
        diagonal = part[pl.ds(place, count)]
        if has_below:
            diagonal += cond[pl.ds(place - 1, count)]
        if has_above:
            diagonal += cond[pl.ds(place + 1, count)]
        inverse[pl.ds(at + first, count)] = inverted(diagonal)

    for low, high in ((0, 7), (7, SIDE - 1)):
        invert(FAR_BOX, low, high - low)
        invert(NEAR_BOX, low + 1, high - low)
    invert(FAR_BOX, SIDE - 1, 1, has_above=False)
    invert(NEAR_BOX, 0, 1, has_below=False)
    inverse[pl.ds(OWN_BOX[2] + OV + 1, CR - 2)] = own_inverse[pl.ds(1, CR - 2)]
    for low in (1, OV + CR - 1):
        invert(OWN_BOX, low, OV)
    invert(OWN_BOX, 0, 1, has_below=False)
    invert(OWN_BOX, OWN - 1, 1, has_above=False)

    weights = face_x, face_z, face_r

    def solve(spans, borrow):
        for p0, _, at, guarded, low, high in spans(0):
            for first, count in pieces(low, high):
                here = pl.ds(at + first, count)
                est_a[pl.ds(guarded + first, count)] = inverse[here] * rhs[here]
        source, target = est_a, est_b
        for done, power in enumerate(reversed(POWERS)):
            borrow(done, source)
            for p0, _, at, guarded, low, high in spans(done + 1):
                for first, count in pieces(low, high):
                    here, below, above = [source[pl.ds(guarded + first + n, count)] for n in (0, -1, 1)]
                    summed = power * rhs[pl.ds(at + first, count)]
                    summed += around(weights, p0 + first + DK, count, here, below, above)
                    target[pl.ds(guarded + first, count)] = inverse[pl.ds(at + first, count)] * summed
            source, target = target, source
        borrow(SWEEPS, source)

    def first_spans(done):
        low = (0, OV + 1 + done)
        high = (OWN - OV - 1 - done, OWN)
        return (FAR_BOX + (done, SIDE), NEAR_BOX + (0, SIDE - done), OWN_BOX + low, OWN_BOX + high)

    def from_own(done, est):
        rows = (7, 8) if done == SWEEPS else (done + 1, done + 2, CR - 3 - done, CR - 2 - done)
        for p in rows:
            est[pl.ds(OWN_BOX[3] + OV + p, 1)] = levels[done, pl.ds(p, 1)]

    solve(first_spans, from_own)
    est = est_a if SWEEPS % 2 == 0 else est_b

    to_low = any_of(both, (63, 65), (124, 126))
    to_high = any_of(both, (66, 68), (127, 128), (0, 1))

    def joined(value):
        other = jnp.where(to_low, turn(value, -TWIN, 3), jnp.where(to_high, turn(value, TWIN, 3), 0.0))
        return value + other

    def summed_boxes(p, count):
        value = None
        for p0, rows, _, guarded in (FAR_BOX, OWN_BOX, NEAR_BOX):
            if p0 <= p and p + count <= p0 + rows:
                share = est[pl.ds(guarded + p - p0, count)]
                value = share if value is None else value + share
        return value

    for low, high in ((-REACH, -OV), (-OV, 0), (0, OV), (OV, 8), (8, CR - OV), (CR - OV, CR + OV), (CR + OV, CR + REACH)):
        value = joined(summed_boxes(low, high - low))
        if low < 0:
            value = jnp.where(far_tile, value, 0.0)
        total[pl.ds(low + REACH, high - low)] = value

    def remainder(box, p, count):
        p0, _, at, _ = box
        here, below, above = [total[pl.ds(p + REACH + n, count)] for n in (0, -1, 1)]
        place = p + DK
        diagonal = part[pl.ds(place, count)] + (cond[pl.ds(place - 1, count)] + cond[pl.ds(place + 1, count)])
        summed = around(weights, p + DK, count, here, below, above)
        here_rhs = pl.ds(at + p - p0, count)
        value = jnp.where(core, rhs[here_rhs] - LEAD * (diagonal * here - summed), 0.0)
        if p < 0:
            value = jnp.where(far_tile, value, 0.0)
        rhs[here_rhs] = value

    remainder(FAR_BOX, -SWEEPS, SWEEPS)
    for p in range(0, CR, 8):
        remainder(OWN_BOX, p, 8)
    remainder(NEAR_BOX, CR, SWEEPS)

    def second_spans(done):
        cut = max(0, done + OV - SWEEPS)
        return (
            FAR_BOX + (DG - SWEEPS + done, SIDE), OWN_BOX + (cut, OWN - cut), NEAR_BOX + (0, SWEEPS + OV - done)
        )

    solve(second_spans, lambda done, est: None)

    order = lax.div(lane, 2) + HALF * lax.rem(lane, 2)
    for low, high in ((0, OV), (OV, 8), (8, CR - OV), (CR - OV, CR)):
        value = joined(summed_boxes(low, high - low)) + total[pl.ds(low + REACH, high - low)]
        value = jnp.where(lane < HALF, value[:, 0], turn(value[:, 1], HALF, 2))
        value = value.reshape((high - low) * NZ, CA)
        value = jnp.take_along_axis(value, jnp.concatenate([order] * (high - low)), axis=1)
        for n in range(high - low):
            row = low + n
            out[pl.ds(odd * (CR - 1 - 2 * row) + row, NZ, stride=CR), :] = value[n * NZ : (n + 1) * NZ]


def call(kernel, outs, *args, scratch=(), limit=4, cost=None):
    vmem = pl.BlockSpec(memory_space=pltpu.VMEM)
    return pl.pallas_call(
        kernel,
        out_shape=outs,
        in_specs=[vmem] * len(args),
        out_specs=jax.tree.map(lambda _: vmem, outs),
        scratch_shapes=scratch,
        compiler_params=pltpu.CompilerParams(vmem_limit_bytes=limit * MIB),
        cost_estimate=cost,
        name=kernel.__name__,
    )(*args)


def body(source, conduct, solid):
    aisles = lax.axis_size("aisle")
    rows = lax.axis_size("row")
    flat = (NZ * CR, CA)
    tile = lambda *lead: jax.ShapeDtypeStruct(lead + (NZ, CA), jnp.float32)
    busy = pl.CostEstimate(flops=10**11, bytes_accessed=1024 * MIB, transcendentals=0)
    shift = 0.1 + 40.0 * solid.astype(jnp.float32)
    main, to_other, to_pair = call(
        pack_edges, (tile(3, CR), tile(CR // 2), tile(CR // 2)),
        source.reshape(flat), conduct.reshape(flat), shift.reshape(flat),
    )
    pair = [(i, i ^ 1) for i in range(aisles)]
    other = [(i, (i - 1 + 2 * (i % 2)) % aisles) for i in range(aisles)]
    far_pairs = [(i, i + 1) for i in range(1, rows - 1, 2)]
    far_pairs += [(b, a) for a, b in far_pairs]
    near_pairs = [(i, i ^ 1) for i in range(rows)]
    from_other = lax.ppermute(to_other, "aisle", other)
    from_pair = lax.ppermute(to_pair, "aisle", pair)
    to_far, to_near = call(
        pack_rows, (tile(TILES), tile(TILES)), main,
        cost=busy,
    )
    near = lax.ppermute(to_near, "row", near_pairs)
    far = lax.ppermute(to_far, "row", far_pairs)
    strips, strips_far, strips_near = call(
        pack_strips, (tile(CR), tile(DK // 2), tile(DK // 2)), from_other, from_pair
    )
    far_strips = lax.ppermute(strips_far, "row", far_pairs)
    near_strips = lax.ppermute(strips_near, "row", near_pairs)
    own_rows = (tile(CR, 2),) * 7 + (tile(SWEEPS + 1, CR, 2),)
    own = call(prepare_own, own_rows, main, strips, limit=8, cost=busy)
    pair_rows = lambda count: pltpu.VMEM((count, 2, NZ, CA), jnp.float32)
    around = CR + 2 * DK
    result = call(
        solve_all,
        jax.ShapeDtypeStruct(flat, jnp.float32),
        *own, near, far, far_strips, near_strips,
        scratch=[
            pair_rows(around), pair_rows(around), pair_rows(around), pair_rows(around), pair_rows(around),
            pair_rows(ROWS), pair_rows(ROWS), pair_rows(GUARDED), pair_rows(GUARDED), pair_rows(CR + 2 * REACH),
        ],
        limit=16,
    )
    return result.reshape(NZ, CR, CA)


def solution(mesh):
    spec = P(None, "row", "aisle")
    return jax.shard_map(body, mesh=mesh, in_specs=(spec, spec, spec), out_specs=spec, check_vma=False)
```

```python
import jax
import jax.numpy as jnp
from jax import lax
from jax.experimental import pallas as pl
from jax.experimental.pallas import tpu as pltpu
from jax.sharding import PartitionSpec as P

OV = 2
SWEEPS = 6
LOWER_END = 0.2
UPPER_END = 2.0
MIDDLE = 0.5 * (UPPER_END + LOWER_END)
SPREAD = 0.5 * (UPPER_END - LOWER_END)

NZ = 8
CR = 16
CA = 128
HALF = CA // 2
MIB = 1024 * 1024
DG = 2 * SWEEPS + 1
DK = DG + 1
TILES = 2 * DG + DK
SIDE = DG + OV
OWN = CR + 2 * OV
ROWS = 2 * SIDE + OWN
REACH = SWEEPS + 1
FAR_BOX = (-DG, SIDE, 0, 1)
OWN_BOX = (-OV, OWN, SIDE, SIDE + 2)
NEAR_BOX = (CR - OV, SIDE, SIDE + OWN, SIDE + OWN + 3)
GUARDED = ROWS + 4
TWIN = 3
GROUP = 8
STRIP = 7
RIGHT0 = 67
LEFT0 = 118
SPAN = 48
LEFT_AT = LEFT0 - RIGHT0


def coefficients():
    ratio = SPREAD / MIDDLE
    update = [1.0 / MIDDLE] + [0.0] * SWEEPS
    estimate = list(update)
    for _ in range(SWEEPS):
        image = [0.0] + estimate[:-1]
        remain = [float(n == 0) - e + i for n, (e, i) in enumerate(zip(estimate, image))]
        ratio_next = 1.0 / (2.0 * MIDDLE / SPREAD - ratio)
        update = [ratio_next * ratio * u + 2.0 * ratio_next / SPREAD * r for u, r in zip(update, remain)]
        estimate = [e + u for e, u in zip(estimate, update)]
        ratio = ratio_next
    return estimate


LEAD = coefficients()[-1]
POWERS = [power / LEAD for power in coefficients()[:-1]]


def lanes():
    return lax.broadcasted_iota(jnp.int32, (NZ, CA), 1)


def turn(value, by, axis=1):
    return pltpu.roll(value, by % value.shape[axis], axis)


def any_of(lane, *spans):
    mask = None
    for low, high in spans:
        here = (lane >= low) & (lane < high)
        mask = here if mask is None else mask | here
    return mask


def needed(layer):
    return (max(DK - 1 - layer, OV) + 1) // 2


def block_of(ref, first, count):
    return ref[pl.ds(first, count)]


def pack_edges(source, conduct, shift, main, to_other, to_pair):
    odd = lax.rem(lax.axis_index("row"), 2)
    half = CR // 2
    shape = (half * NZ, CA)
    lane = lax.broadcasted_iota(jnp.int32, shape, 1)
    order = jnp.where(lane < HALF, 2 * lane, 2 * lane - (CA - 1))

    def edge(slot, first):
        return first + 2 * lax.rem(slot, 8) + lax.rem(lax.div(slot, 8), 2)

    end = CA - 2 * STRIP
    left_order = edge(lane, 0)
    right_order = jnp.where(lane < SPAN, edge(lane, end), edge(lane + (16 * 4 - LEFT_AT), end))
    right_order = jnp.minimum(right_order, CA - 1)
    pick = lambda value, index: jnp.take_along_axis(value, index, axis=1)
    left = right = jnp.zeros(shape, jnp.float32)
    for number, (field, scale) in enumerate(((source, 2.0 * LEAD), (conduct, 1.0), (shift, 1.0))):
        for part in range(2):
            rows = []
            for row in range(part * half, (part + 1) * half):
                rows.append(field[pl.ds(odd * (CR - 1 - 2 * row) + row, NZ, stride=CR), :])
            rows = scale * jnp.concatenate(rows)
            main[number, pl.ds(part * half, half)] = pick(rows, order).reshape(half, NZ, CA)
            base = part * SPAN + 16 * number
            left = jnp.where(any_of(lane, (base, base + 16)), pick(rows, left_order), left)
            base = (1 - part) * LEFT_AT + 16 * number
            right = jnp.where(any_of(lane, (base, base + 16)), pick(rows, right_order), right)
    left = left.reshape(half, NZ, CA)
    right = right.reshape(half, NZ, CA)
    uneven = odd_aisle()
    to_pair[...] = jnp.where(uneven, left, right)
    to_other[...] = jnp.where(uneven, right, left)


def odd_aisle():
    return jnp.full((NZ, CA), lax.rem(lax.axis_index("aisle"), 2)) > 0


def pack_rows(main, to_far, to_near):
    start = 0
    for number, depth in enumerate((DG, DK, DG)):
        to_far[pl.ds(start, depth)] = jnp.stack([main[number, depth - 1 - n] for n in range(depth)])
        to_near[pl.ds(start, depth)] = jnp.stack([main[number, CR - 1 - n] for n in range(depth)])
        start += depth


def slots(lane):
    return lax.rem(lane, 8), lax.rem(lane + 6, 8)


def pack_strips(from_other, from_pair, strips, to_far, to_near):
    lane = lanes()
    in_right = lane < SPAN
    slot_right, slot_left = slots(lane)
    uneven = odd_aisle()
    from_right = jnp.where(uneven, from_other[...], from_pair[...])
    from_left = jnp.where(uneven, from_pair[...], from_other[...])
    half = CR // 2
    rows = []
    for row in range(half):
        rows.append(jnp.where(in_right, from_right[row], from_left[row]))
    for row in range(half):
        rows.append(jnp.where(in_right, turn(from_right[row], -SPAN), turn(from_left[row], LEFT_AT)))
    strips[...] = jnp.stack(rows)
    around_left = any_of(lane, (LEFT_AT - 1, LEFT_AT + SPAN))
    for out, place in ((to_far, lambda q: q), (to_near, lambda q: CR - 1 - q)):
        for layer in range(DK // 2):
            first, second = needed(layer), needed(DK - 1 - layer)
            deep = rows[place(DK - 1 - layer)]
            takes_right = in_right & (slot_right >= 8 - second)
            takes_left = around_left & (slot_left >= 8 - first - second) & (slot_left < 8 - first)
            value = jnp.where(takes_left, turn(deep, -first), rows[place(layer)])
            out[layer] = jnp.where(takes_right, turn(deep, 8 - second), value)


def unpack_strips(pairs, lane):
    slot_right, slot_left = slots(lane)
    half = DK // 2
    near_part = [pairs[layer] for layer in range(half)]
    deep_part = []
    for layer in reversed(range(half)):
        first, second = needed(layer), needed(DK - 1 - layer)
        right = (lane < SPAN) & (slot_right < second)
        left = any_of(lane, (LEFT_AT, LEFT_AT + SPAN)) & (slot_left >= 8 - second)
        value = jnp.where(left, turn(pairs[layer], first), 0.0)
        deep_part.append(jnp.where(right, turn(pairs[layer], second - 8), value))
    return near_part + deep_part


def picked(value, index):
    rows = value.reshape(-1, CA)
    return jnp.take_along_axis(rows, jnp.concatenate([index] * (rows.shape[0] // NZ)), axis=1).reshape(value.shape)


def split(block, copies):
    lane = lanes()
    in_block = lane < HALF
    index = lane
    if copies:
        in_block |= any_of(lane, (66, 67), (125, 126))
        index = jnp.where(lane == 66, HALF - 1, jnp.where(lane == 125, 0, index))
    tiles = []
    for colour in range(2):
        part = block
        if copies or colour:
            part = picked(block, jnp.clip(index + HALF * colour, 0, CA - 1))
        tiles.append(jnp.where(in_block, part, 0.0))
    return jnp.stack(tiles, axis=1)


def expand(tiles, strip, number, copies):
    lane = lanes()
    in_strip = any_of(lane, (RIGHT0, RIGHT0 + STRIP), (LEFT0, LEFT0 + STRIP))
    index = lane - RIGHT0
    if copies:
        in_strip |= any_of(lane, (64, 65), (127, 128))
        index = jnp.where(lane == 64, 0, jnp.where(lane == 127, LEFT_AT + STRIP - 1, index))
    beside = [picked(strip, jnp.clip(index + (16 * number + 8 * colour), 0, CA - 1)) for colour in range(2)]
    return jnp.where(in_strip, jnp.stack(beside, axis=1), tiles)


def spread(here, shift):
    level = lax.broadcasted_iota(jnp.int32, here.shape, 2)
    even, uneven = here[:, 0], here[:, 1]
    after, before = turn(even, -1, 2), turn(uneven, 1, 2)
    x_up = jnp.stack([uneven, after], axis=1)
    x_both = jnp.stack([uneven + before, even + after], axis=1)
    z_up = turn(here, -1, 2)
    z_both = jnp.where(level == NZ - 1, 0.0, z_up) + jnp.where(level == 0, 0.0, turn(here, 1, 2))
    part = shift + 6.0 * here + (z_both + x_both)
    return here + x_up, jnp.where(level == NZ - 1, 0.0, here + z_up), part


def pieces(low, high):
    number = -(-(high - low) // GROUP)
    cuts = [low + (high - low) * n // number for n in range(number + 1)]
    return [(first, last - first) for first, last in zip(cuts[:-1], cuts[1:])]


def inverted(diagonal):
    both = lax.broadcasted_iota(jnp.int32, (2, NZ, CA), 2)
    good = any_of(both, (0, 65), (66, 74), (118, 126), (127, 128)) & (diagonal > 0.0)
    return jnp.where(good, 1.0 / jnp.where(good, diagonal, 1.0), 0.0)


def around(weights, row, count, here, below, above):
    face_x, face_z, face_r = weights
    at = pl.ds(row, count)
    fx, fz = face_x[at], face_z[at]
    even, uneven = here[:, 0], here[:, 1]
    summed = face_r[at] * below + face_r[pl.ds(row + 1, count)] * above
    summed += fz * turn(here, -1, 2) + turn(fz * here, 1, 2)
    sum_even = fx[:, 0] * uneven + turn(fx[:, 1] * uneven, 1, 2)
    sum_odd = fx[:, 0] * even + fx[:, 1] * turn(even, -1, 2)
    return summed + jnp.stack([sum_even, sum_odd], axis=1)


def prepare_own(main, strips, rhs, cond, face_x, face_z, face_r, part, inverse, levels):
    halves = [pl.ds(first, 8) for first in range(0, CR, 8)]
    for at in halves:
        strip = strips[at]
        cond[at] = expand(split(main[1, at], True), strip, 1, True)
        part[at] = expand(split(main[2, at], True), strip, 2, True)
        rhs[at] = expand(split(main[0, at], False), strip, 0, False)
    for at in halves:
        face_x[at], face_z[at], part[at] = spread(cond[at], part[at])
    face_r[pl.ds(0, 1)] = jnp.zeros((1, 2, NZ, CA), jnp.float32)
    for first, count in pieces(1, CR):
        face_r[pl.ds(first, count)] = cond[pl.ds(first - 1, count)] + cond[pl.ds(first, count)]
    for first, count in pieces(1, CR - 1):
        at = pl.ds(first, count)
        inverse[at] = inverted(part[at] + (cond[pl.ds(first - 1, count)] + cond[pl.ds(first + 1, count)]))
        levels[0, at] = inverse[at] * rhs[at]
    weights = face_x, face_z, face_r
    for done, power in enumerate(reversed(POWERS)):
        for first, count in pieces(2 + done, CR - 2 - done):
            here, below, above = [levels[done, pl.ds(first + n, count)] for n in (0, -1, 1)]
            at = pl.ds(first, count)
            levels[done + 1, at] = inverse[at] * (power * rhs[at] + around(weights, first, count, here, below, above))


def split_near(near, tiles):
    tiles[:DG] = split(near[:DG], False)
    tiles[DG:] = split(near[DG:], True)


def solve_all(own_rhs, own_cond, own_x, own_z, own_r, own_part, own_inverse, levels, near, far, far_strips, near_strips, out,
              cond, face_x, face_z, face_r, part, inverse, rhs, est_a, est_b, total):
    row_at = lax.axis_index("row")
    odd = lax.rem(row_at, 2)
    far_there = jnp.where(odd == 0, row_at > 0, row_at < lax.axis_size("row") - 1)
    far_level = far_there.astype(jnp.float32)
    far_tile = jnp.full((NZ, CA), far_level) > 0.5
    lane = lanes()

    own = pl.ds(DK, CR)
    cond[own] = own_cond[...]
    face_x[own] = own_x[...]
    face_z[own] = own_z[...]
    part[own] = own_part[...]
    p0, count, at, guarded = OWN_BOX
    zeros = jnp.zeros((1, 2, NZ, CA), jnp.float32)
    rhs[pl.ds(at + OV, CR)] = own_rhs[...]
    for row in (SIDE - 2, SIDE - 1, SIDE, SIDE + 1, SIDE + OWN - 2, SIDE + OWN - 1, SIDE + OWN, SIDE + OWN + 1):
        rhs[pl.ds(row, 1)] = zeros
    for est in (est_a, est_b):
        for row in (0, SIDE + 1, SIDE + OWN + 2, GUARDED - 1):
            est[pl.ds(row, 1)] = zeros

    sides = [(far, unpack_strips(far_strips, lane)[::-1], True), (near, unpack_strips(near_strips, lane), False)]
    for block, strip, is_far in sides:
        part_of = (lambda at, copies: split(block[at], copies)) if is_far else (lambda at, copies: block[at])
        for low, high in ((0, 7), (7, DK)):
            at = pl.ds((0 if is_far else DK + CR) + low, high - low)
            cond[at] = expand(part_of(pl.ds(DG + low, high - low), True), jnp.stack(strip[low:high]), 1, True)
        strip = strip[1:] if is_far else strip[:DG]
        for low, high in ((0, 7), (7, DG)):
            beside = jnp.stack(strip[low:high])
            at = pl.ds((1 if is_far else DK + CR) + low, high - low)
            part[at] = expand(part_of(pl.ds(DG + DK + low, high - low), True), beside, 2, True)
            at = pl.ds((0 if is_far else NEAR_BOX[2] + OV) + low, high - low)
            rhs[at] = expand(part_of(pl.ds(low, high - low), False), beside, 0, False)
    for first in (1, DK + CR):
        for low, high in ((0, 7), (7, DG)):
            at = pl.ds(first + low, high - low)
            shift = part[at]
            if first == 1:
                shift = jnp.where(far_tile, shift, 2.0)
            face_x[at], face_z[at], part[at] = spread(cond[at], shift)

    face_r[pl.ds(DK + 1, CR - 1)] = own_r[pl.ds(1, CR - 1)]
    for first, last in ((1, DK + 1), (DK + CR, 2 * DG + CR + 2)):
        for low, count in pieces(first, last):
            face_r[pl.ds(low, count)] = cond[pl.ds(low - 1, count)] + cond[pl.ds(low, count)]

    both = lax.broadcasted_iota(jnp.int32, (2, NZ, CA), 2)
    core = any_of(both, (0, 64), (67, 74), (118, 125))

    def invert(box, first, count, has_below=True, has_above=True):
        p0, _, at, _ = box
        place = p0 + first + DK
        diagonal = part[pl.ds(place, count)]
        if has_below:
            diagonal += cond[pl.ds(place - 1, count)]
        if has_above:
            diagonal += cond[pl.ds(place + 1, count)]
        inverse[pl.ds(at + first, count)] = inverted(diagonal)

    for low, high in ((0, 7), (7, SIDE - 1)):
        invert(FAR_BOX, low, high - low)
        invert(NEAR_BOX, low + 1, high - low)
    invert(FAR_BOX, SIDE - 1, 1, has_above=False)
    invert(NEAR_BOX, 0, 1, has_below=False)
    inverse[pl.ds(OWN_BOX[2] + OV + 1, CR - 2)] = own_inverse[pl.ds(1, CR - 2)]
    for low in (1, OV + CR - 1):
        invert(OWN_BOX, low, OV)
    invert(OWN_BOX, 0, 1, has_below=False)
    invert(OWN_BOX, OWN - 1, 1, has_above=False)

    weights = face_x, face_z, face_r

    def solve(spans, borrow):
        for p0, _, at, guarded, low, high in spans(0):
            for first, count in pieces(low, high):
                here = pl.ds(at + first, count)
                est_a[pl.ds(guarded + first, count)] = inverse[here] * rhs[here]
        source, target = est_a, est_b
        for done, power in enumerate(reversed(POWERS)):
            borrow(done, source)
            for p0, _, at, guarded, low, high in spans(done + 1):
                for first, count in pieces(low, high):
                    here, below, above = [source[pl.ds(guarded + first + n, count)] for n in (0, -1, 1)]
                    summed = power * rhs[pl.ds(at + first, count)]
                    summed += around(weights, p0 + first + DK, count, here, below, above)
                    target[pl.ds(guarded + first, count)] = inverse[pl.ds(at + first, count)] * summed
            source, target = target, source
        borrow(SWEEPS, source)

    def first_spans(done):
        low = (0, OV + 1 + done)
        high = (OWN - OV - 1 - done, OWN)
        return (FAR_BOX + (done, SIDE), NEAR_BOX + (0, SIDE - done), OWN_BOX + low, OWN_BOX + high)

    def from_own(done, est):
        rows = (7, 8) if done == SWEEPS else (done + 1, done + 2, CR - 3 - done, CR - 2 - done)
        for p in rows:
            est[pl.ds(OWN_BOX[3] + OV + p, 1)] = levels[done, pl.ds(p, 1)]

    solve(first_spans, from_own)
    est = est_a if SWEEPS % 2 == 0 else est_b

    to_low = any_of(lane, (63, 65), (124, 126))
    to_high = any_of(lane, (66, 68), (127, 128), (0, 1))
    twins = lax.rem(lane + jnp.where(to_low, TWIN, jnp.where(to_high, CA - TWIN, 0)), CA)
    twice = to_low | to_high

    def joined(value):
        return value + jnp.where(twice, picked(value, twins), 0.0)

    def summed_boxes(p, count):
        value = None
        for p0, rows, _, guarded in (FAR_BOX, OWN_BOX, NEAR_BOX):
            if p0 <= p and p + count <= p0 + rows:
                share = est[pl.ds(guarded + p - p0, count)]
                value = share if value is None else value + share
        return value

    for low, high in ((-REACH, -OV), (-OV, 0), (0, OV), (OV, 8), (8, CR - OV), (CR - OV, CR + OV), (CR + OV, CR + REACH)):
        value = joined(summed_boxes(low, high - low))
        if low < 0:
            value = jnp.where(far_tile, value, 0.0)
        total[pl.ds(low + REACH, high - low)] = value

    def remainder(box, p, count):
        p0, _, at, _ = box
        here, below, above = [total[pl.ds(p + REACH + n, count)] for n in (0, -1, 1)]
        place = p + DK
        diagonal = part[pl.ds(place, count)] + (cond[pl.ds(place - 1, count)] + cond[pl.ds(place + 1, count)])
        summed = around(weights, p + DK, count, here, below, above)
        here_rhs = pl.ds(at + p - p0, count)
        value = jnp.where(core, rhs[here_rhs] - LEAD * (diagonal * here - summed), 0.0)
        if p < 0:
            value = jnp.where(far_tile, value, 0.0)
        rhs[here_rhs] = value

    remainder(FAR_BOX, -SWEEPS, SWEEPS)
    for p in range(0, CR, 8):
        remainder(OWN_BOX, p, 8)
    remainder(NEAR_BOX, CR, SWEEPS)

    def second_spans(done):
        cut = max(0, done + OV - SWEEPS)
        return (
            FAR_BOX + (DG - SWEEPS + done, SIDE), OWN_BOX + (cut, OWN - cut), NEAR_BOX + (0, SWEEPS + OV - done)
        )

    solve(second_spans, lambda done, est: None)

    order = lax.div(lane, 2)
    is_even = lax.rem(lane, 2) == 0
    for low, high in ((0, OV), (OV, 8), (8, CR - OV), (CR - OV, CR)):
        value = joined(summed_boxes(low, high - low)) + total[pl.ds(low + REACH, high - low)]
        value = jnp.where(is_even, picked(value[:, 0], order), picked(value[:, 1], order))
        value = value.reshape((high - low) * NZ, CA)
        for n in range(high - low):
            row = low + n
            out[pl.ds(odd * (CR - 1 - 2 * row) + row, NZ, stride=CR), :] = value[n * NZ : (n + 1) * NZ]


def call(kernel, outs, *args, scratch=(), limit=4, cost=None):
    vmem = pl.BlockSpec(memory_space=pltpu.VMEM)
    return pl.pallas_call(
        kernel,
        out_shape=outs,
        in_specs=[vmem] * len(args),
        out_specs=jax.tree.map(lambda _: vmem, outs),
        scratch_shapes=scratch,
        compiler_params=pltpu.CompilerParams(vmem_limit_bytes=limit * MIB),
        cost_estimate=cost,
        name=kernel.__name__,
    )(*args)


def body(source, conduct, solid):
    aisles = lax.axis_size("aisle")
    rows = lax.axis_size("row")
    flat = (NZ * CR, CA)
    tile = lambda *lead: jax.ShapeDtypeStruct(lead + (NZ, CA), jnp.float32)
    busy = pl.CostEstimate(flops=10**11, bytes_accessed=0, transcendentals=0)
    shift = 0.1 + 40.0 * solid.astype(jnp.float32)
    main, to_other, to_pair = call(
        pack_edges, (tile(3, CR), tile(CR // 2), tile(CR // 2)),
        source.reshape(flat), conduct.reshape(flat), shift.reshape(flat),
    )
    pair = [(i, i ^ 1) for i in range(aisles)]
    other = [(i, (i - 1 + 2 * (i % 2)) % aisles) for i in range(aisles)]
    far_pairs = [(i, i + 1) for i in range(1, rows - 1, 2)]
    far_pairs += [(b, a) for a, b in far_pairs]
    near_pairs = [(i, i ^ 1) for i in range(rows)]
    from_other = lax.ppermute(to_other, "aisle", other)
    from_pair = lax.ppermute(to_pair, "aisle", pair)
    to_far, to_near = call(
        pack_rows, (tile(TILES), tile(TILES)), main,
        cost=busy,
    )
    near = lax.ppermute(to_near, "row", near_pairs)
    far = lax.ppermute(to_far, "row", far_pairs)
    strips, strips_far, strips_near = call(
        pack_strips, (tile(CR), tile(DK // 2), tile(DK // 2)), from_other, from_pair
    )
    far_strips = lax.ppermute(strips_far, "row", far_pairs)
    near_strips = lax.ppermute(strips_near, "row", near_pairs)
    own_rows = (tile(CR, 2),) * 7 + (tile(SWEEPS + 1, CR, 2),)
    own = call(prepare_own, own_rows, main, strips, limit=8, cost=busy)
    pair_rows = lambda count: pltpu.VMEM((count, 2, NZ, CA), jnp.float32)
    around = CR + 2 * DK
    result = call(
        solve_all,
        jax.ShapeDtypeStruct(flat, jnp.float32),
        *own, call(split_near, tile(TILES, 2), near, cost=None), far, far_strips, near_strips,
        scratch=[
            pair_rows(around), pair_rows(around), pair_rows(around), pair_rows(around), pair_rows(around),
            pair_rows(ROWS), pair_rows(ROWS), pair_rows(GUARDED), pair_rows(GUARDED), pair_rows(CR + 2 * REACH),
        ],
        limit=16,
    )
    return result.reshape(NZ, CR, CA)


def solution(mesh):
    spec = P(None, "row", "aisle")
    return jax.shard_map(body, mesh=mesh, in_specs=(spec, spec, spec), out_specs=spec, check_vma=False)
```

```python
import jax
import jax.numpy as jnp
from jax import lax
from jax.experimental import pallas as pl
from jax.experimental.pallas import tpu as pltpu
from jax.sharding import PartitionSpec as P

OV = 2
SWEEPS = 6
LOWER_END = 0.2
UPPER_END = 2.0
MIDDLE = 0.5 * (UPPER_END + LOWER_END)
SPREAD = 0.5 * (UPPER_END - LOWER_END)

NZ = 8
CR = 16
CA = 128
HALF = CA // 2
MIB = 1024 * 1024
DG = 2 * SWEEPS + 1
DK = DG + 1
TILES = 2 * DG + DK
SIDE = DG + OV
OWN = CR + 2 * OV
ROWS = 2 * SIDE + OWN
REACH = SWEEPS + 1
FAR_BOX = (-DG, SIDE, 0, 1)
OWN_BOX = (-OV, OWN, SIDE, SIDE + 2)
NEAR_BOX = (CR - OV, SIDE, SIDE + OWN, SIDE + OWN + 3)
GUARDED = ROWS + 4
TWIN = 3
GROUP = 8
STRIP = 7
RIGHT0 = 67
LEFT0 = 118
SPAN = 48
LEFT_AT = LEFT0 - RIGHT0


def coefficients():
    ratio = SPREAD / MIDDLE
    update = [1.0 / MIDDLE] + [0.0] * SWEEPS
    estimate = list(update)
    for _ in range(SWEEPS):
        image = [0.0] + estimate[:-1]
        remain = [float(n == 0) - e + i for n, (e, i) in enumerate(zip(estimate, image))]
        ratio_next = 1.0 / (2.0 * MIDDLE / SPREAD - ratio)
        update = [ratio_next * ratio * u + 2.0 * ratio_next / SPREAD * r for u, r in zip(update, remain)]
        estimate = [e + u for e, u in zip(estimate, update)]
        ratio = ratio_next
    return estimate


LEAD = coefficients()[-1]
POWERS = [power / LEAD for power in coefficients()[:-1]]


def lanes():
    return lax.broadcasted_iota(jnp.int32, (NZ, CA), 1)


def turn(value, by, axis=1):
    return pltpu.roll(value, by % value.shape[axis], axis)


def any_of(lane, *spans):
    mask = None
    for low, high in spans:
        here = (lane >= low) & (lane < high)
        mask = here if mask is None else mask | here
    return mask


def needed(layer):
    return (max(DK - 1 - layer, OV) + 1) // 2


def block_of(ref, first, count):
    return ref[pl.ds(first, count)]


def pack_edges(source, conduct, shift, main, to_other, to_pair):
    odd = lax.rem(lax.axis_index("row"), 2)
    half = CR // 2
    shape = (half * NZ, CA)
    lane = lax.broadcasted_iota(jnp.int32, shape, 1)
    order = jnp.where(lane < HALF, 2 * lane, 2 * lane - (CA - 1))

    def edge(slot, first):
        return first + 2 * lax.rem(slot, 8) + lax.rem(lax.div(slot, 8), 2)

    end = CA - 2 * STRIP
    left_order = edge(lane, 0)
    right_order = jnp.where(lane < SPAN, edge(lane, end), edge(lane + (16 * 4 - LEFT_AT), end))
    right_order = jnp.minimum(right_order, CA - 1)
    pick = lambda value, index: jnp.take_along_axis(value, index, axis=1)
    left = right = jnp.zeros(shape, jnp.float32)
    for number, (field, scale) in enumerate(((source, 2.0 * LEAD), (conduct, 1.0), (shift, 1.0))):
        for part in range(2):
            rows = []
            for row in range(part * half, (part + 1) * half):
                rows.append(field[pl.ds(odd * (CR - 1 - 2 * row) + row, NZ, stride=CR), :])
            rows = scale * jnp.concatenate(rows)
            main[number, pl.ds(part * half, half)] = pick(rows, order).reshape(half, NZ, CA)
            base = part * SPAN + 16 * number
            left = jnp.where(any_of(lane, (base, base + 16)), pick(rows, left_order), left)
            base = (1 - part) * LEFT_AT + 16 * number
            right = jnp.where(any_of(lane, (base, base + 16)), pick(rows, right_order), right)
    left = left.reshape(half, NZ, CA)
    right = right.reshape(half, NZ, CA)
    uneven = odd_aisle()
    to_pair[...] = jnp.where(uneven, left, right)
    to_other[...] = jnp.where(uneven, right, left)


def odd_aisle():
    return jnp.full((NZ, CA), lax.rem(lax.axis_index("aisle"), 2)) > 0


def pack_rows(main, to_far, to_near):
    start = 0
    for number, depth in enumerate((DG, DK, DG)):
        to_far[pl.ds(start, depth)] = jnp.stack([main[number, depth - 1 - n] for n in range(depth)])
        to_near[pl.ds(start, depth)] = jnp.stack([main[number, CR - 1 - n] for n in range(depth)])
        start += depth


def slots(lane):
    return lax.rem(lane, 8), lax.rem(lane + 6, 8)


def right_and_left(from_other, from_pair):
    uneven = odd_aisle()
    return jnp.where(uneven, from_other[...], from_pair[...]), jnp.where(uneven, from_pair[...], from_other[...])


def side_by_side(from_right, from_left):
    in_right = lanes() < SPAN
    first = jnp.where(in_right, from_right, from_left)
    return jnp.concatenate([first, jnp.where(in_right, turn(from_right, -SPAN, 2), turn(from_left, LEFT_AT, 2))])


def pack_strips(from_other, from_pair, strips, to_far):
    lane = lanes()
    in_right = lane < SPAN
    slot_right, slot_left = slots(lane)
    rows = side_by_side(*right_and_left(from_other, from_pair))
    strips[...] = rows
    around_left = any_of(lane, (LEFT_AT - 1, LEFT_AT + SPAN))
    for layer in range(DK // 2):
        first, second = needed(layer), needed(DK - 1 - layer)
        deep = rows[DK - 1 - layer]
        takes_right = in_right & (slot_right >= 8 - second)
        takes_left = around_left & (slot_left >= 8 - first - second) & (slot_left < 8 - first)
        value = jnp.where(takes_left, turn(deep, -first), rows[layer])
        to_far[layer] = jnp.where(takes_right, turn(deep, 8 - second), value)


def unpack_strips(pairs, lane):
    slot_right, slot_left = slots(lane)
    half = DK // 2
    near_part = [pairs[layer] for layer in range(half)]
    deep_part = []
    for layer in reversed(range(half)):
        first, second = needed(layer), needed(DK - 1 - layer)
        right = (lane < SPAN) & (slot_right < second)
        left = any_of(lane, (LEFT_AT, LEFT_AT + SPAN)) & (slot_left >= 8 - second)
        value = jnp.where(left, turn(pairs[layer], first), 0.0)
        deep_part.append(jnp.where(right, turn(pairs[layer], second - 8), value))
    return near_part + deep_part


def picked(value, index):
    rows = value.reshape(-1, CA)
    return jnp.take_along_axis(rows, jnp.concatenate([index] * (rows.shape[0] // NZ)), axis=1).reshape(value.shape)


def split(block, copies):
    lane = lanes()
    in_block = lane < HALF
    index = lane
    if copies:
        in_block |= any_of(lane, (66, 67), (125, 126))
        index = jnp.where(lane == 66, HALF - 1, jnp.where(lane == 125, 0, index))
    tiles = []
    for colour in range(2):
        part = block
        if copies or colour:
            part = picked(block, jnp.clip(index + HALF * colour, 0, CA - 1))
        tiles.append(jnp.where(in_block, part, 0.0))
    return jnp.stack(tiles, axis=1)


def expand(tiles, strip, number, copies):
    lane = lanes()
    in_strip = any_of(lane, (RIGHT0, RIGHT0 + STRIP), (LEFT0, LEFT0 + STRIP))
    index = lane - RIGHT0
    if copies:
        in_strip |= any_of(lane, (64, 65), (127, 128))
        index = jnp.where(lane == 64, 0, jnp.where(lane == 127, LEFT_AT + STRIP - 1, index))
    beside = [picked(strip, jnp.clip(index + (16 * number + 8 * colour), 0, CA - 1)) for colour in range(2)]
    return jnp.where(in_strip, jnp.stack(beside, axis=1), tiles)


def spread(here, shift):
    level = lax.broadcasted_iota(jnp.int32, here.shape, 2)
    even, uneven = here[:, 0], here[:, 1]
    after, before = turn(even, -1, 2), turn(uneven, 1, 2)
    x_up = jnp.stack([uneven, after], axis=1)
    x_both = jnp.stack([uneven + before, even + after], axis=1)
    z_up = turn(here, -1, 2)
    z_both = jnp.where(level == NZ - 1, 0.0, z_up) + jnp.where(level == 0, 0.0, turn(here, 1, 2))
    part = shift + 6.0 * here + (z_both + x_both)
    return here + x_up, jnp.where(level == NZ - 1, 0.0, here + z_up), part


def pieces(low, high):
    number = -(-(high - low) // GROUP)
    cuts = [low + (high - low) * n // number for n in range(number + 1)]
    return [(first, last - first) for first, last in zip(cuts[:-1], cuts[1:])]


def inverted(diagonal):
    both = lax.broadcasted_iota(jnp.int32, (2, NZ, CA), 2)
    good = any_of(both, (0, 65), (66, 74), (118, 126), (127, 128)) & (diagonal > 0.0)
    return jnp.where(good, 1.0 / jnp.where(good, diagonal, 1.0), 0.0)


def around(weights, row, count, here, below, above):
    face_x, face_z, face_r = weights
    at = pl.ds(row, count)
    fx, fz = face_x[at], face_z[at]
    even, uneven = here[:, 0], here[:, 1]
    summed = face_r[at] * below + face_r[pl.ds(row + 1, count)] * above
    summed += fz * turn(here, -1, 2) + turn(fz * here, 1, 2)
    sum_even = fx[:, 0] * uneven + turn(fx[:, 1] * uneven, 1, 2)
    sum_odd = fx[:, 0] * even + fx[:, 1] * turn(even, -1, 2)
    return summed + jnp.stack([sum_even, sum_odd], axis=1)


def prepare_own(main, strips, near, tiles, rhs, cond, face_x, face_z, face_r, part, inverse, levels):
    tiles[:DG] = split(near[:DG], False)
    tiles[DG:] = split(near[DG:], True)
    halves = [pl.ds(first, 8) for first in range(0, CR, 8)]
    for at in halves:
        strip = strips[at]
        cond[at] = expand(split(main[1, at], True), strip, 1, True)
        part[at] = expand(split(main[2, at], True), strip, 2, True)
        rhs[at] = expand(split(main[0, at], False), strip, 0, False)
    for at in halves:
        face_x[at], face_z[at], part[at] = spread(cond[at], part[at])
    face_r[pl.ds(0, 1)] = jnp.zeros((1, 2, NZ, CA), jnp.float32)
    for first, count in pieces(1, CR):
        face_r[pl.ds(first, count)] = cond[pl.ds(first - 1, count)] + cond[pl.ds(first, count)]
    for first, count in pieces(1, CR - 1):
        at = pl.ds(first, count)
        inverse[at] = inverted(part[at] + (cond[pl.ds(first - 1, count)] + cond[pl.ds(first + 1, count)]))
        levels[0, at] = inverse[at] * rhs[at]
    weights = face_x, face_z, face_r
    for done, power in enumerate(reversed(POWERS)):
        for first, count in pieces(2 + done, CR - 2 - done):
            here, below, above = [levels[done, pl.ds(first + n, count)] for n in (0, -1, 1)]
            at = pl.ds(first, count)
            levels[done + 1, at] = inverse[at] * (power * rhs[at] + around(weights, first, count, here, below, above))


def pack_near_edges(near, to_other, to_pair):
    half = DK // 2
    lane = lanes()

    def edge(slot, first):
        index = first + lax.rem(slot, 8) + HALF * lax.rem(lax.div(slot, 8), 2)
        return jnp.clip(index, 0, CA - 1)

    left_order = edge(lane, 0)
    right_order = jnp.where(lane < SPAN, edge(lane, HALF - STRIP), edge(lane + (16 * 4 - LEFT_AT), HALF - STRIP))
    left = right = jnp.zeros((half, NZ, CA), jnp.float32)
    for number, start in enumerate((0, DG, DG + DK)):
        for part in range(2):
            last = DK if number == 1 else DG
            rows = jnp.stack([near[start + min(part * half + n, last - 1)] for n in range(half)])
            base = part * SPAN + 16 * number
            left = jnp.where(any_of(lane, (base, base + 16)), picked(rows, left_order), left)
            base = (1 - part) * LEFT_AT + 16 * number
            right = jnp.where(any_of(lane, (base, base + 16)), picked(rows, right_order), right)
    uneven = odd_aisle()
    to_pair[...] = jnp.where(uneven, left, right)
    to_other[...] = jnp.where(uneven, right, left)


def solve_all(own_rhs, own_cond, own_x, own_z, own_r, own_part, own_inverse, levels, near, far, far_strips, near_other, near_pair, out,
              cond, face_x, face_z, face_r, part, inverse, rhs, est_a, est_b, total):
    row_at = lax.axis_index("row")
    odd = lax.rem(row_at, 2)
    far_there = jnp.where(odd == 0, row_at > 0, row_at < lax.axis_size("row") - 1)
    far_level = far_there.astype(jnp.float32)
    far_tile = jnp.full((NZ, CA), far_level) > 0.5
    lane = lanes()

    own = pl.ds(DK, CR)
    cond[own] = own_cond[...]
    face_x[own] = own_x[...]
    face_z[own] = own_z[...]
    part[own] = own_part[...]
    p0, count, at, guarded = OWN_BOX
    zeros = jnp.zeros((1, 2, NZ, CA), jnp.float32)
    rhs[pl.ds(at + OV, CR)] = own_rhs[...]
    for row in (SIDE - 2, SIDE - 1, SIDE, SIDE + 1, SIDE + OWN - 2, SIDE + OWN - 1, SIDE + OWN, SIDE + OWN + 1):
        rhs[pl.ds(row, 1)] = zeros
    for est in (est_a, est_b):
        for row in (0, SIDE + 1, SIDE + OWN + 2, GUARDED - 1):
            est[pl.ds(row, 1)] = zeros

    sides = [(far, unpack_strips(far_strips, lane)[::-1], True), (near, side_by_side(*right_and_left(near_other, near_pair)), False)]
    for block, strip, is_far in sides:
        part_of = (lambda at, copies: split(block[at], copies)) if is_far else (lambda at, copies: block[at])
        for low, high in ((0, 7), (7, DK)):
            at = pl.ds((0 if is_far else DK + CR) + low, high - low)
            cond[at] = expand(part_of(pl.ds(DG + low, high - low), True), jnp.stack(strip[low:high]), 1, True)
        strip = strip[1:] if is_far else strip[:DG]
        for low, high in ((0, 7), (7, DG)):
            beside = jnp.stack(strip[low:high])
            at = pl.ds((1 if is_far else DK + CR) + low, high - low)
            part[at] = expand(part_of(pl.ds(DG + DK + low, high - low), True), beside, 2, True)
            at = pl.ds((0 if is_far else NEAR_BOX[2] + OV) + low, high - low)
            rhs[at] = expand(part_of(pl.ds(low, high - low), False), beside, 0, False)
    for first in (1, DK + CR):
        for low, high in ((0, 7), (7, DG)):
            at = pl.ds(first + low, high - low)
            shift = part[at]
            if first == 1:
                shift = jnp.where(far_tile, shift, 2.0)
            face_x[at], face_z[at], part[at] = spread(cond[at], shift)

    face_r[pl.ds(DK + 1, CR - 1)] = own_r[pl.ds(1, CR - 1)]
    for first, last in ((1, DK + 1), (DK + CR, 2 * DG + CR + 2)):
        for low, count in pieces(first, last):
            face_r[pl.ds(low, count)] = cond[pl.ds(low - 1, count)] + cond[pl.ds(low, count)]

    both = lax.broadcasted_iota(jnp.int32, (2, NZ, CA), 2)
    core = any_of(both, (0, 64), (67, 74), (118, 125))

    def invert(box, first, count, has_below=True, has_above=True):
        p0, _, at, _ = box
        place = p0 + first + DK
        diagonal = part[pl.ds(place, count)]
        if has_below:
            diagonal += cond[pl.ds(place - 1, count)]
        if has_above:
            diagonal += cond[pl.ds(place + 1, count)]
        inverse[pl.ds(at + first, count)] = inverted(diagonal)

    for low, high in ((0, 7), (7, SIDE - 1)):
        invert(FAR_BOX, low, high - low)
        invert(NEAR_BOX, low + 1, high - low)
    invert(FAR_BOX, SIDE - 1, 1, has_above=False)
    invert(NEAR_BOX, 0, 1, has_below=False)
    inverse[pl.ds(OWN_BOX[2] + OV + 1, CR - 2)] = own_inverse[pl.ds(1, CR - 2)]
    for low in (1, OV + CR - 1):
        invert(OWN_BOX, low, OV)
    invert(OWN_BOX, 0, 1, has_below=False)
    invert(OWN_BOX, OWN - 1, 1, has_above=False)

    weights = face_x, face_z, face_r

    def solve(spans, borrow):
        for p0, _, at, guarded, low, high in spans(0):
            for first, count in pieces(low, high):
                here = pl.ds(at + first, count)
                est_a[pl.ds(guarded + first, count)] = inverse[here] * rhs[here]
        source, target = est_a, est_b
        for done, power in enumerate(reversed(POWERS)):
            borrow(done, source)
            for p0, _, at, guarded, low, high in spans(done + 1):
                for first, count in pieces(low, high):
                    here, below, above = [source[pl.ds(guarded + first + n, count)] for n in (0, -1, 1)]
                    summed = power * rhs[pl.ds(at + first, count)]
                    summed += around(weights, p0 + first + DK, count, here, below, above)
                    target[pl.ds(guarded + first, count)] = inverse[pl.ds(at + first, count)] * summed
            source, target = target, source
        borrow(SWEEPS, source)

    def first_spans(done):
        low = (0, OV + 1 + done)
        high = (OWN - OV - 1 - done, OWN)
        return (FAR_BOX + (done, SIDE), NEAR_BOX + (0, SIDE - done), OWN_BOX + low, OWN_BOX + high)

    def from_own(done, est):
        rows = (7, 8) if done == SWEEPS else (done + 1, done + 2, CR - 3 - done, CR - 2 - done)
        for p in rows:
            est[pl.ds(OWN_BOX[3] + OV + p, 1)] = levels[done, pl.ds(p, 1)]

    solve(first_spans, from_own)
    est = est_a if SWEEPS % 2 == 0 else est_b

    to_low = any_of(lane, (63, 65), (124, 126))
    to_high = any_of(lane, (66, 68), (127, 128), (0, 1))
    twins = lax.rem(lane + jnp.where(to_low, TWIN, jnp.where(to_high, CA - TWIN, 0)), CA)
    twice = to_low | to_high

    def joined(value):
        return value + jnp.where(twice, picked(value, twins), 0.0)

    def summed_boxes(p, count):
        value = None
        for p0, rows, _, guarded in (FAR_BOX, OWN_BOX, NEAR_BOX):
            if p0 <= p and p + count <= p0 + rows:
                share = est[pl.ds(guarded + p - p0, count)]
                value = share if value is None else value + share
        return value

    for low, high in ((-REACH, -OV), (-OV, 0), (0, OV), (OV, 8), (8, CR - OV), (CR - OV, CR + OV), (CR + OV, CR + REACH)):
        value = joined(summed_boxes(low, high - low))
        if low < 0:
            value = jnp.where(far_tile, value, 0.0)
        total[pl.ds(low + REACH, high - low)] = value

    def remainder(box, p, count):
        p0, _, at, _ = box
        here, below, above = [total[pl.ds(p + REACH + n, count)] for n in (0, -1, 1)]
        place = p + DK
        diagonal = part[pl.ds(place, count)] + (cond[pl.ds(place - 1, count)] + cond[pl.ds(place + 1, count)])
        summed = around(weights, p + DK, count, here, below, above)
        here_rhs = pl.ds(at + p - p0, count)
        value = jnp.where(core, rhs[here_rhs] - LEAD * (diagonal * here - summed), 0.0)
        if p < 0:
            value = jnp.where(far_tile, value, 0.0)
        rhs[here_rhs] = value

    remainder(FAR_BOX, -SWEEPS, SWEEPS)
    for p in range(0, CR, 8):
        remainder(OWN_BOX, p, 8)
    remainder(NEAR_BOX, CR, SWEEPS)

    def second_spans(done):
        cut = max(0, done + OV - SWEEPS)
        return (
            FAR_BOX + (DG - SWEEPS + done, SIDE), OWN_BOX + (cut, OWN - cut), NEAR_BOX + (0, SWEEPS + OV - done)
        )

    solve(second_spans, lambda done, est: None)

    order = lax.div(lane, 2)
    is_even = lax.rem(lane, 2) == 0
    for low, high in ((0, OV), (OV, 8), (8, CR - OV), (CR - OV, CR)):
        value = joined(summed_boxes(low, high - low)) + total[pl.ds(low + REACH, high - low)]
        value = jnp.where(is_even, picked(value[:, 0], order), picked(value[:, 1], order))
        value = value.reshape((high - low) * NZ, CA)
        for n in range(high - low):
            row = low + n
            out[pl.ds(odd * (CR - 1 - 2 * row) + row, NZ, stride=CR), :] = value[n * NZ : (n + 1) * NZ]


def call(kernel, outs, *args, scratch=(), limit=4, cost=None):
    vmem = pl.BlockSpec(memory_space=pltpu.VMEM)
    return pl.pallas_call(
        kernel,
        out_shape=outs,
        in_specs=[vmem] * len(args),
        out_specs=jax.tree.map(lambda _: vmem, outs),
        scratch_shapes=scratch,
        compiler_params=pltpu.CompilerParams(vmem_limit_bytes=limit * MIB),
        cost_estimate=cost,
        name=kernel.__name__,
    )(*args)


def body(source, conduct, solid):
    aisles = lax.axis_size("aisle")
    rows = lax.axis_size("row")
    flat = (NZ * CR, CA)
    tile = lambda *lead: jax.ShapeDtypeStruct(lead + (NZ, CA), jnp.float32)
    busy = pl.CostEstimate(flops=10**11, bytes_accessed=0, transcendentals=0)
    shift = 0.1 + 40.0 * solid.astype(jnp.float32)
    main, to_other, to_pair = call(
        pack_edges, (tile(3, CR), tile(CR // 2), tile(CR // 2)),
        source.reshape(flat), conduct.reshape(flat), shift.reshape(flat),
    )
    pair = [(i, i ^ 1) for i in range(aisles)]
    other = [(i, (i - 1 + 2 * (i % 2)) % aisles) for i in range(aisles)]
    far_pairs = [(i, i + 1) for i in range(1, rows - 1, 2)]
    far_pairs += [(b, a) for a, b in far_pairs]
    near_pairs = [(i, i ^ 1) for i in range(rows)]
    from_other = lax.ppermute(to_other, "aisle", other)
    from_pair = lax.ppermute(to_pair, "aisle", pair)
    to_far, to_near = call(
        pack_rows, (tile(TILES), tile(TILES)), main,
        cost=busy,
    )
    near = lax.ppermute(to_near, "row", near_pairs)
    far = lax.ppermute(to_far, "row", far_pairs)
    strips, strips_far = call(pack_strips, (tile(CR), tile(DK // 2)), from_other, from_pair)
    far_strips = lax.ppermute(strips_far, "row", far_pairs)
    near_to_other, near_to_pair = call(pack_near_edges, (tile(DK // 2), tile(DK // 2)), near, cost=None)
    near_other = lax.ppermute(near_to_other, "aisle", other)
    near_pair = lax.ppermute(near_to_pair, "aisle", pair)
    own_rows = (tile(CR, 2),) * 7 + (tile(SWEEPS + 1, CR, 2),)
    near_tiles, *own = call(
        prepare_own, (tile(TILES, 2),) + own_rows, main, strips, near, limit=8, cost=pl.CostEstimate(flops=2000*10**6, bytes_accessed=0, transcendentals=0)
    )
    pair_rows = lambda count: pltpu.VMEM((count, 2, NZ, CA), jnp.float32)
    around = CR + 2 * DK
    result = call(
        solve_all,
        jax.ShapeDtypeStruct(flat, jnp.float32),
        *own, near_tiles, far, far_strips, near_other, near_pair,
        scratch=[
            pair_rows(around), pair_rows(around), pair_rows(around), pair_rows(around), pair_rows(around),
            pair_rows(ROWS), pair_rows(ROWS), pair_rows(GUARDED), pair_rows(GUARDED), pair_rows(CR + 2 * REACH),
        ],
        limit=16,
    )
    return result.reshape(NZ, CR, CA)


def solution(mesh):
    spec = P(None, "row", "aisle")
    return jax.shard_map(body, mesh=mesh, in_specs=(spec, spec, spec), out_specs=spec, check_vma=False)
```

```python
import jax
import jax.numpy as jnp
from jax import lax
from jax.experimental import pallas as pl
from jax.experimental.pallas import tpu as pltpu
from jax.sharding import PartitionSpec as P

OV = 2
SWEEPS = 6
LOWER_END = 0.2
UPPER_END = 2.0
MIDDLE = 0.5 * (UPPER_END + LOWER_END)
SPREAD = 0.5 * (UPPER_END - LOWER_END)

NZ = 8
CR = 16
CA = 128
HALF = CA // 2
MIB = 1024 * 1024
DG = 2 * SWEEPS + 1
DK = DG + 1
TILES = 2 * DG + DK
SIDE = DG + OV
OWN = CR + 2 * OV
ROWS = 2 * SIDE + OWN
REACH = SWEEPS + 1
FAR_BOX = (-DG, SIDE, 0, 1)
OWN_BOX = (-OV, OWN, SIDE, SIDE + 2)
NEAR_BOX = (CR - OV, SIDE, SIDE + OWN, SIDE + OWN + 3)
GUARDED = ROWS + 4
TWIN = 3
GROUP = 8
STRIP = 7
RIGHT0 = 67
LEFT0 = 118
SPAN = 48
LEFT_AT = LEFT0 - RIGHT0


def coefficients():
    ratio = SPREAD / MIDDLE
    update = [1.0 / MIDDLE] + [0.0] * SWEEPS
    estimate = list(update)
    for _ in range(SWEEPS):
        image = [0.0] + estimate[:-1]
        remain = [float(n == 0) - e + i for n, (e, i) in enumerate(zip(estimate, image))]
        ratio_next = 1.0 / (2.0 * MIDDLE / SPREAD - ratio)
        update = [ratio_next * ratio * u + 2.0 * ratio_next / SPREAD * r for u, r in zip(update, remain)]
        estimate = [e + u for e, u in zip(estimate, update)]
        ratio = ratio_next
    return estimate


LEAD = coefficients()[-1]
POWERS = [power / LEAD for power in coefficients()[:-1]]


def lanes():
    return lax.broadcasted_iota(jnp.int32, (NZ, CA), 1)


def turn(value, by, axis=1):
    return pltpu.roll(value, by % value.shape[axis], axis)


def any_of(lane, *spans):
    mask = None
    for low, high in spans:
        here = (lane >= low) & (lane < high)
        mask = here if mask is None else mask | here
    return mask


def needed(layer):
    return (max(DK - 1 - layer, OV) + 1) // 2


def block_of(ref, first, count):
    return ref[pl.ds(first, count)]


def pack_edges(source, conduct, shift, main, to_other, to_pair):
    odd = lax.rem(lax.axis_index("row"), 2)
    half = CR // 2
    shape = (half * NZ, CA)
    lane = lax.broadcasted_iota(jnp.int32, shape, 1)
    order = jnp.where(lane < HALF, 2 * lane, 2 * lane - (CA - 1))

    def edge(slot, first):
        return first + 2 * lax.rem(slot, 8) + lax.rem(lax.div(slot, 8), 2)

    end = CA - 2 * STRIP
    left_order = edge(lane, 0)
    right_order = jnp.where(lane < SPAN, edge(lane, end), edge(lane + (16 * 4 - LEFT_AT), end))
    right_order = jnp.minimum(right_order, CA - 1)
    pick = lambda value, index: jnp.take_along_axis(value, index, axis=1)
    left = right = jnp.zeros(shape, jnp.float32)
    for number, (field, scale) in enumerate(((source, 2.0 * LEAD), (conduct, 1.0), (shift, 1.0))):
        for part in range(2):
            rows = []
            for row in range(part * half, (part + 1) * half):
                rows.append(field[pl.ds(odd * (CR - 1 - 2 * row) + row, NZ, stride=CR), :])
            rows = scale * jnp.concatenate(rows)
            main[number, pl.ds(part * half, half)] = pick(rows, order).reshape(half, NZ, CA)
            base = part * SPAN + 16 * number
            left = jnp.where(any_of(lane, (base, base + 16)), pick(rows, left_order), left)
            base = (1 - part) * LEFT_AT + 16 * number
            right = jnp.where(any_of(lane, (base, base + 16)), pick(rows, right_order), right)
    left = left.reshape(half, NZ, CA)
    right = right.reshape(half, NZ, CA)
    uneven = odd_aisle()
    to_pair[...] = jnp.where(uneven, left, right)
    to_other[...] = jnp.where(uneven, right, left)


def odd_aisle():
    return jnp.full((NZ, CA), lax.rem(lax.axis_index("aisle"), 2)) > 0


def pack_rows(main, to_far, to_near):
    start = 0
    for number, depth in enumerate((DG, DK, DG)):
        to_far[pl.ds(start, depth)] = jnp.stack([main[number, depth - 1 - n] for n in range(depth)])
        to_near[pl.ds(start, depth)] = jnp.stack([main[number, CR - 1 - n] for n in range(depth)])
        start += depth


def slots(lane):
    return lax.rem(lane, 8), lax.rem(lane + 6, 8)


def right_and_left(from_other, from_pair):
    uneven = odd_aisle()
    return jnp.where(uneven, from_other[...], from_pair[...]), jnp.where(uneven, from_pair[...], from_other[...])


def side_by_side(from_right, from_left):
    in_right = lanes() < SPAN
    first = jnp.where(in_right, from_right, from_left)
    return jnp.concatenate([first, jnp.where(in_right, turn(from_right, -SPAN, 2), turn(from_left, LEFT_AT, 2))])


def pack_strips(from_pair, from_other, near, strips, to_far, near_other, near_pair):
    lane = lanes()
    in_right = lane < SPAN
    slot_right, slot_left = slots(lane)
    rows = side_by_side(*right_and_left(from_other, from_pair))
    strips[...] = rows
    around_left = any_of(lane, (LEFT_AT - 1, LEFT_AT + SPAN))
    for layer in range(DK // 2):
        first, second = needed(layer), needed(DK - 1 - layer)
        deep = rows[DK - 1 - layer]
        takes_right = in_right & (slot_right >= 8 - second)
        takes_left = around_left & (slot_left >= 8 - first - second) & (slot_left < 8 - first)
        value = jnp.where(takes_left, turn(deep, -first), rows[layer])
        to_far[layer] = jnp.where(takes_right, turn(deep, 8 - second), value)
    half = DK // 2

    def edge(slot, first):
        index = first + lax.rem(slot, 8) + HALF * lax.rem(lax.div(slot, 8), 2)
        return jnp.clip(index, 0, CA - 1)

    left_order = edge(lane, 0)
    right_order = jnp.where(lane < SPAN, edge(lane, HALF - STRIP), edge(lane + (16 * 4 - LEFT_AT), HALF - STRIP))
    left = right = jnp.zeros((half, NZ, CA), jnp.float32)
    for number, start in enumerate((0, DG, DG + DK)):
        for part in range(2):
            last = DK if number == 1 else DG
            edges = jnp.stack([near[start + min(part * half + n, last - 1)] for n in range(half)])
            base = part * SPAN + 16 * number
            left = jnp.where(any_of(lane, (base, base + 16)), picked(edges, left_order), left)
            base = (1 - part) * LEFT_AT + 16 * number
            right = jnp.where(any_of(lane, (base, base + 16)), picked(edges, right_order), right)
    uneven = odd_aisle()
    near_pair[...] = jnp.where(uneven, left, right)
    near_other[...] = jnp.where(uneven, right, left)


def unpack_strips(pairs, lane):
    slot_right, slot_left = slots(lane)
    half = DK // 2
    near_part = [pairs[layer] for layer in range(half)]
    deep_part = []
    for layer in reversed(range(half)):
        first, second = needed(layer), needed(DK - 1 - layer)
        right = (lane < SPAN) & (slot_right < second)
        left = any_of(lane, (LEFT_AT, LEFT_AT + SPAN)) & (slot_left >= 8 - second)
        value = jnp.where(left, turn(pairs[layer], first), 0.0)
        deep_part.append(jnp.where(right, turn(pairs[layer], second - 8), value))
    return near_part + deep_part


def picked(value, index):
    rows = value.reshape(-1, CA)
    return jnp.take_along_axis(rows, jnp.concatenate([index] * (rows.shape[0] // NZ)), axis=1).reshape(value.shape)


def split(block, copies):
    lane = lanes()
    in_block = lane < HALF
    index = lane
    if copies:
        in_block |= any_of(lane, (66, 67), (125, 126))
        index = jnp.where(lane == 66, HALF - 1, jnp.where(lane == 125, 0, index))
    tiles = []
    for colour in range(2):
        part = block
        if copies or colour:
            part = picked(block, jnp.clip(index + HALF * colour, 0, CA - 1))
        tiles.append(jnp.where(in_block, part, 0.0))
    return jnp.stack(tiles, axis=1)


def expand(tiles, strip, number, copies):
    lane = lanes()
    in_strip = any_of(lane, (RIGHT0, RIGHT0 + STRIP), (LEFT0, LEFT0 + STRIP))
    index = lane - RIGHT0
    if copies:
        in_strip |= any_of(lane, (64, 65), (127, 128))
        index = jnp.where(lane == 64, 0, jnp.where(lane == 127, LEFT_AT + STRIP - 1, index))
    beside = [picked(strip, jnp.clip(index + (16 * number + 8 * colour), 0, CA - 1)) for colour in range(2)]
    return jnp.where(in_strip, jnp.stack(beside, axis=1), tiles)


def spread(here, shift):
    level = lax.broadcasted_iota(jnp.int32, here.shape, 2)
    even, uneven = here[:, 0], here[:, 1]
    after, before = turn(even, -1, 2), turn(uneven, 1, 2)
    x_up = jnp.stack([uneven, after], axis=1)
    x_both = jnp.stack([uneven + before, even + after], axis=1)
    z_up = turn(here, -1, 2)
    z_both = jnp.where(level == NZ - 1, 0.0, z_up) + jnp.where(level == 0, 0.0, turn(here, 1, 2))
    part = shift + 6.0 * here + (z_both + x_both)
    return here + x_up, jnp.where(level == NZ - 1, 0.0, here + z_up), part


def pieces(low, high):
    number = -(-(high - low) // GROUP)
    cuts = [low + (high - low) * n // number for n in range(number + 1)]
    return [(first, last - first) for first, last in zip(cuts[:-1], cuts[1:])]


def inverted(diagonal):
    both = lax.broadcasted_iota(jnp.int32, (2, NZ, CA), 2)
    good = any_of(both, (0, 65), (66, 74), (118, 126), (127, 128)) & (diagonal > 0.0)
    return jnp.where(good, 1.0 / jnp.where(good, diagonal, 1.0), 0.0)


def around(weights, row, count, here, below, above):
    face_x, face_z, face_r = weights
    at = pl.ds(row, count)
    fx, fz = face_x[at], face_z[at]
    even, uneven = here[:, 0], here[:, 1]
    summed = face_r[at] * below + face_r[pl.ds(row + 1, count)] * above
    summed += fz * turn(here, -1, 2) + turn(fz * here, 1, 2)
    sum_even = fx[:, 0] * uneven + turn(fx[:, 1] * uneven, 1, 2)
    sum_odd = fx[:, 0] * even + fx[:, 1] * turn(even, -1, 2)
    return summed + jnp.stack([sum_even, sum_odd], axis=1)


def prepare_own(main, strips, near, tiles, rhs, cond, face_x, face_z, face_r, part, inverse, levels):
    tiles[:DG] = split(near[:DG], False)
    tiles[DG:] = split(near[DG:], True)
    halves = [pl.ds(first, 8) for first in range(0, CR, 8)]
    for at in halves:
        strip = strips[at]
        cond[at] = expand(split(main[1, at], True), strip, 1, True)
        part[at] = expand(split(main[2, at], True), strip, 2, True)
        rhs[at] = expand(split(main[0, at], False), strip, 0, False)
    for at in halves:
        face_x[at], face_z[at], part[at] = spread(cond[at], part[at])
    face_r[pl.ds(0, 1)] = jnp.zeros((1, 2, NZ, CA), jnp.float32)
    for first, count in pieces(1, CR):
        face_r[pl.ds(first, count)] = cond[pl.ds(first - 1, count)] + cond[pl.ds(first, count)]
    for first, count in pieces(1, CR - 1):
        at = pl.ds(first, count)
        inverse[at] = inverted(part[at] + (cond[pl.ds(first - 1, count)] + cond[pl.ds(first + 1, count)]))
        levels[0, at] = inverse[at] * rhs[at]
    weights = face_x, face_z, face_r
    for done, power in enumerate(reversed(POWERS)):
        for first, count in pieces(2 + done, CR - 2 - done):
            here, below, above = [levels[done, pl.ds(first + n, count)] for n in (0, -1, 1)]
            at = pl.ds(first, count)
            levels[done + 1, at] = inverse[at] * (power * rhs[at] + around(weights, first, count, here, below, above))


def split_far(far, tiles):
    tiles[:DG] = split(far[:DG], False)
    tiles[DG:] = split(far[DG:], True)


def solve_all(own_rhs, own_cond, own_x, own_z, own_r, own_part, own_inverse, levels, near, far, far_strips, near_other, near_pair, out,
              cond, face_x, face_z, face_r, part, inverse, rhs, est_a, est_b, total):
    row_at = lax.axis_index("row")
    odd = lax.rem(row_at, 2)
    far_there = jnp.where(odd == 0, row_at > 0, row_at < lax.axis_size("row") - 1)
    far_level = far_there.astype(jnp.float32)
    far_tile = jnp.full((NZ, CA), far_level) > 0.5
    lane = lanes()

    own = pl.ds(DK, CR)
    cond[own] = own_cond[...]
    face_x[own] = own_x[...]
    face_z[own] = own_z[...]
    part[own] = own_part[...]
    p0, count, at, guarded = OWN_BOX
    zeros = jnp.zeros((1, 2, NZ, CA), jnp.float32)
    rhs[pl.ds(at + OV, CR)] = own_rhs[...]
    for row in (SIDE - 2, SIDE - 1, SIDE, SIDE + 1, SIDE + OWN - 2, SIDE + OWN - 1, SIDE + OWN, SIDE + OWN + 1):
        rhs[pl.ds(row, 1)] = zeros
    for est in (est_a, est_b):
        for row in (0, SIDE + 1, SIDE + OWN + 2, GUARDED - 1):
            est[pl.ds(row, 1)] = zeros

    sides = [(far, unpack_strips(far_strips, lane)[::-1], True), (near, side_by_side(*right_and_left(near_other, near_pair)), False)]
    for block, strip, is_far in sides:
        for low, high in ((0, 7), (7, DK)):
            at = pl.ds((0 if is_far else DK + CR) + low, high - low)
            cond[at] = expand(block[pl.ds(DG + low, high - low)], jnp.stack(strip[low:high]), 1, True)
        strip = strip[1:] if is_far else strip[:DG]
        for low, high in ((0, 7), (7, DG)):
            beside = jnp.stack(strip[low:high])
            at = pl.ds((1 if is_far else DK + CR) + low, high - low)
            part[at] = expand(block[pl.ds(DG + DK + low, high - low)], beside, 2, True)
            at = pl.ds((0 if is_far else NEAR_BOX[2] + OV) + low, high - low)
            rhs[at] = expand(block[pl.ds(low, high - low)], beside, 0, False)
    for first in (1, DK + CR):
        for low, high in ((0, 7), (7, DG)):
            at = pl.ds(first + low, high - low)
            shift = part[at]
            if first == 1:
                shift = jnp.where(far_tile, shift, 2.0)
            face_x[at], face_z[at], part[at] = spread(cond[at], shift)

    face_r[pl.ds(DK + 1, CR - 1)] = own_r[pl.ds(1, CR - 1)]
    for first, last in ((1, DK + 1), (DK + CR, 2 * DG + CR + 2)):
        for low, count in pieces(first, last):
            face_r[pl.ds(low, count)] = cond[pl.ds(low - 1, count)] + cond[pl.ds(low, count)]

    both = lax.broadcasted_iota(jnp.int32, (2, NZ, CA), 2)
    core = any_of(both, (0, 64), (67, 74), (118, 125))

    def invert(box, first, count, has_below=True, has_above=True):
        p0, _, at, _ = box
        place = p0 + first + DK
        diagonal = part[pl.ds(place, count)]
        if has_below:
            diagonal += cond[pl.ds(place - 1, count)]
        if has_above:
            diagonal += cond[pl.ds(place + 1, count)]
        inverse[pl.ds(at + first, count)] = inverted(diagonal)

    for low, high in ((0, 7), (7, SIDE - 1)):
        invert(FAR_BOX, low, high - low)
        invert(NEAR_BOX, low + 1, high - low)
    invert(FAR_BOX, SIDE - 1, 1, has_above=False)
    invert(NEAR_BOX, 0, 1, has_below=False)
    inverse[pl.ds(OWN_BOX[2] + OV + 1, CR - 2)] = own_inverse[pl.ds(1, CR - 2)]
    for low in (1, OV + CR - 1):
        invert(OWN_BOX, low, OV)
    invert(OWN_BOX, 0, 1, has_below=False)
    invert(OWN_BOX, OWN - 1, 1, has_above=False)

    weights = face_x, face_z, face_r

    def solve(spans, borrow):
        for p0, _, at, guarded, low, high in spans(0):
            for first, count in pieces(low, high):
                here = pl.ds(at + first, count)
                est_a[pl.ds(guarded + first, count)] = inverse[here] * rhs[here]
        source, target = est_a, est_b
        for done, power in enumerate(reversed(POWERS)):
            borrow(done, source)
            for p0, _, at, guarded, low, high in spans(done + 1):
                for first, count in pieces(low, high):
                    here, below, above = [source[pl.ds(guarded + first + n, count)] for n in (0, -1, 1)]
                    summed = power * rhs[pl.ds(at + first, count)]
                    summed += around(weights, p0 + first + DK, count, here, below, above)
                    target[pl.ds(guarded + first, count)] = inverse[pl.ds(at + first, count)] * summed
            source, target = target, source
        borrow(SWEEPS, source)

    def first_spans(done):
        low = (0, OV + 1 + done)
        high = (OWN - OV - 1 - done, OWN)
        return (FAR_BOX + (done, SIDE), NEAR_BOX + (0, SIDE - done), OWN_BOX + low, OWN_BOX + high)

    def from_own(done, est):
        rows = (7, 8) if done == SWEEPS else (done + 1, done + 2, CR - 3 - done, CR - 2 - done)
        for p in rows:
            est[pl.ds(OWN_BOX[3] + OV + p, 1)] = levels[done, pl.ds(p, 1)]

    solve(first_spans, from_own)
    est = est_a if SWEEPS % 2 == 0 else est_b

    to_low = any_of(lane, (63, 65), (124, 126))
    to_high = any_of(lane, (66, 68), (127, 128), (0, 1))
    twins = lax.rem(lane + jnp.where(to_low, TWIN, jnp.where(to_high, CA - TWIN, 0)), CA)
    twice = to_low | to_high

    def joined(value):
        return value + jnp.where(twice, picked(value, twins), 0.0)

    def summed_boxes(p, count):
        value = None
        for p0, rows, _, guarded in (FAR_BOX, OWN_BOX, NEAR_BOX):
            if p0 <= p and p + count <= p0 + rows:
                share = est[pl.ds(guarded + p - p0, count)]
                value = share if value is None else value + share
        return value

    for low, high in ((-REACH, -OV), (-OV, 0), (0, OV), (OV, 8), (8, CR - OV), (CR - OV, CR + OV), (CR + OV, CR + REACH)):
        value = joined(summed_boxes(low, high - low))
        if low < 0:
            value = jnp.where(far_tile, value, 0.0)
        total[pl.ds(low + REACH, high - low)] = value

    def remainder(box, p, count):
        p0, _, at, _ = box
        here, below, above = [total[pl.ds(p + REACH + n, count)] for n in (0, -1, 1)]
        place = p + DK
        diagonal = part[pl.ds(place, count)] + (cond[pl.ds(place - 1, count)] + cond[pl.ds(place + 1, count)])
        summed = around(weights, p + DK, count, here, below, above)
        here_rhs = pl.ds(at + p - p0, count)
        value = jnp.where(core, rhs[here_rhs] - LEAD * (diagonal * here - summed), 0.0)
        if p < 0:
            value = jnp.where(far_tile, value, 0.0)
        rhs[here_rhs] = value

    remainder(FAR_BOX, -SWEEPS, SWEEPS)
    for p in range(0, CR, 8):
        remainder(OWN_BOX, p, 8)
    remainder(NEAR_BOX, CR, SWEEPS)

    def second_spans(done):
        cut = max(0, done + OV - SWEEPS)
        return (
            FAR_BOX + (DG - SWEEPS + done, SIDE), OWN_BOX + (cut, OWN - cut), NEAR_BOX + (0, SWEEPS + OV - done)
        )

    solve(second_spans, lambda done, est: None)

    order = lax.div(lane, 2)
    is_even = lax.rem(lane, 2) == 0
    for low, high in ((0, OV), (OV, 8), (8, CR - OV), (CR - OV, CR)):
        value = joined(summed_boxes(low, high - low)) + total[pl.ds(low + REACH, high - low)]
        value = jnp.where(is_even, picked(value[:, 0], order), picked(value[:, 1], order))
        value = value.reshape((high - low) * NZ, CA)
        for n in range(high - low):
            row = low + n
            out[pl.ds(odd * (CR - 1 - 2 * row) + row, NZ, stride=CR), :] = value[n * NZ : (n + 1) * NZ]


def call(kernel, outs, *args, scratch=(), limit=4, cost=None):
    vmem = pl.BlockSpec(memory_space=pltpu.VMEM)
    return pl.pallas_call(
        kernel,
        out_shape=outs,
        in_specs=[vmem] * len(args),
        out_specs=jax.tree.map(lambda _: vmem, outs),
        scratch_shapes=scratch,
        compiler_params=pltpu.CompilerParams(vmem_limit_bytes=limit * MIB),
        cost_estimate=cost,
        name=kernel.__name__,
    )(*args)


def body(source, conduct, solid):
    aisles = lax.axis_size("aisle")
    rows = lax.axis_size("row")
    flat = (NZ * CR, CA)
    tile = lambda *lead: jax.ShapeDtypeStruct(lead + (NZ, CA), jnp.float32)
    busy = pl.CostEstimate(flops=10**11, bytes_accessed=0, transcendentals=0)
    shift = 0.1 + 40.0 * solid.astype(jnp.float32)
    main, to_other, to_pair = call(
        pack_edges, (tile(3, CR), tile(CR // 2), tile(CR // 2)),
        source.reshape(flat), conduct.reshape(flat), shift.reshape(flat),
    )
    pair = [(i, i ^ 1) for i in range(aisles)]
    other = [(i, (i - 1 + 2 * (i % 2)) % aisles) for i in range(aisles)]
    far_pairs = [(i, i + 1) for i in range(1, rows - 1, 2)]
    far_pairs += [(b, a) for a, b in far_pairs]
    near_pairs = [(i, i ^ 1) for i in range(rows)]
    from_pair = lax.ppermute(to_pair, "aisle", pair)
    from_other = lax.ppermute(to_other, "aisle", other)
    to_far, to_near = call(
        pack_rows, (tile(TILES), tile(TILES)), main,
        cost=busy,
    )
    near = lax.ppermute(to_near, "row", near_pairs)
    far = lax.ppermute(to_far, "row", far_pairs)
    half = tile(DK // 2)
    strips, strips_far, near_to_other, near_to_pair = call(pack_strips, (tile(CR), half, half, half), from_pair, from_other, near)
    far_strips = lax.ppermute(strips_far, "row", far_pairs)
    near_other = lax.ppermute(near_to_other, "aisle", other)
    near_pair = lax.ppermute(near_to_pair, "aisle", pair)
    own_rows = (tile(CR, 2),) * 7 + (tile(SWEEPS + 1, CR, 2),)
    near_tiles, *own = call(
        prepare_own, (tile(TILES, 2),) + own_rows, main, strips, near, limit=8, cost=pl.CostEstimate(flops=2000*10**6, bytes_accessed=0, transcendentals=0)
    )
    pair_rows = lambda count: pltpu.VMEM((count, 2, NZ, CA), jnp.float32)
    around = CR + 2 * DK
    result = call(
        solve_all,
        jax.ShapeDtypeStruct(flat, jnp.float32),
        *own, near_tiles, call(split_far, tile(TILES, 2), far), far_strips, near_other, near_pair,
        scratch=[
            pair_rows(around), pair_rows(around), pair_rows(around), pair_rows(around), pair_rows(around),
            pair_rows(ROWS), pair_rows(ROWS), pair_rows(GUARDED), pair_rows(GUARDED), pair_rows(CR + 2 * REACH),
        ],
        limit=16,
    )
    return result.reshape(NZ, CR, CA)


def solution(mesh):
    spec = P(None, "row", "aisle")
    return jax.shard_map(body, mesh=mesh, in_specs=(spec, spec, spec), out_specs=spec, check_vma=False)
```

```python
import jax
import jax.numpy as jnp
from jax import lax
from jax.experimental import pallas as pl
from jax.experimental.pallas import tpu as pltpu
from jax.sharding import PartitionSpec as P

OV = 2
SWEEPS = 6
LOWER_END = 0.2
UPPER_END = 2.0
MIDDLE = 0.5 * (UPPER_END + LOWER_END)
SPREAD = 0.5 * (UPPER_END - LOWER_END)

NZ = 8
CR = 16
CA = 128
HALF = CA // 2
MIB = 1024 * 1024
DG = 2 * SWEEPS + 1
DK = DG + 1
TILES = 2 * DG + DK
SIDE = DG + OV
OWN = CR + 2 * OV
ROWS = 2 * SIDE + OWN
REACH = SWEEPS + 1
FAR_BOX = (-DG, SIDE, 0, 1)
OWN_BOX = (-OV, OWN, SIDE, SIDE + 2)
NEAR_BOX = (CR - OV, SIDE, SIDE + OWN, SIDE + OWN + 3)
GUARDED = ROWS + 4
TWIN = 3
GROUP = 8
STRIP = 7
RIGHT0 = 67
LEFT0 = 118
SPAN = 48
LEFT_AT = LEFT0 - RIGHT0


def coefficients():
    ratio = SPREAD / MIDDLE
    update = [1.0 / MIDDLE] + [0.0] * SWEEPS
    estimate = list(update)
    for _ in range(SWEEPS):
        image = [0.0] + estimate[:-1]
        remain = [float(n == 0) - e + i for n, (e, i) in enumerate(zip(estimate, image))]
        ratio_next = 1.0 / (2.0 * MIDDLE / SPREAD - ratio)
        update = [ratio_next * ratio * u + 2.0 * ratio_next / SPREAD * r for u, r in zip(update, remain)]
        estimate = [e + u for e, u in zip(estimate, update)]
        ratio = ratio_next
    return estimate


LEAD = coefficients()[-1]
POWERS = [power / LEAD for power in coefficients()[:-1]]


def lanes():
    return lax.broadcasted_iota(jnp.int32, (NZ, CA), 1)


def turn(value, by, axis=1):
    return pltpu.roll(value, by % value.shape[axis], axis)


def any_of(lane, *spans):
    mask = None
    for low, high in spans:
        here = (lane >= low) & (lane < high)
        mask = here if mask is None else mask | here
    return mask


def needed(layer):
    return (max(DK - 1 - layer, OV) + 1) // 2


def block_of(ref, first, count):
    return ref[pl.ds(first, count)]


def pack_edges(source, conduct, shift, main, to_other, to_pair, to_far, to_near):
    odd = lax.rem(lax.axis_index("row"), 2)
    half = CR // 2
    shape = (half * NZ, CA)
    lane = lax.broadcasted_iota(jnp.int32, shape, 1)
    order = jnp.where(lane < HALF, 2 * lane, 2 * lane - (CA - 1))

    def edge(slot, first):
        return first + 2 * lax.rem(slot, 8) + lax.rem(lax.div(slot, 8), 2)

    end = CA - 2 * STRIP
    left_order = edge(lane, 0)
    right_order = jnp.where(lane < SPAN, edge(lane, end), edge(lane + (16 * 4 - LEFT_AT), end))
    right_order = jnp.minimum(right_order, CA - 1)
    pick = lambda value, index: jnp.take_along_axis(value, index, axis=1)
    left = right = jnp.zeros(shape, jnp.float32)
    for number, (field, scale) in enumerate(((source, 2.0 * LEAD), (conduct, 1.0), (shift, 1.0))):
        for part in range(2):
            rows = []
            for row in range(part * half, (part + 1) * half):
                rows.append(field[pl.ds(odd * (CR - 1 - 2 * row) + row, NZ, stride=CR), :])
            rows = scale * jnp.concatenate(rows)
            main[number, pl.ds(part * half, half)] = pick(rows, order).reshape(half, NZ, CA)
            base = part * SPAN + 16 * number
            left = jnp.where(any_of(lane, (base, base + 16)), pick(rows, left_order), left)
            base = (1 - part) * LEFT_AT + 16 * number
            right = jnp.where(any_of(lane, (base, base + 16)), pick(rows, right_order), right)
    left = left.reshape(half, NZ, CA)
    right = right.reshape(half, NZ, CA)
    start = 0
    for number, depth in enumerate((DG, DK, DG)):
        to_far[pl.ds(start, depth)] = jnp.stack([main[number, depth - 1 - n] for n in range(depth)])
        to_near[pl.ds(start, depth)] = jnp.stack([main[number, CR - 1 - n] for n in range(depth)])
        start += depth
    uneven = odd_aisle()
    to_pair[...] = jnp.where(uneven, left, right)
    to_other[...] = jnp.where(uneven, right, left)


def odd_aisle():
    return jnp.full((NZ, CA), lax.rem(lax.axis_index("aisle"), 2)) > 0


def slots(lane):
    return lax.rem(lane, 8), lax.rem(lane + 6, 8)


def right_and_left(from_other, from_pair):
    uneven = odd_aisle()
    return jnp.where(uneven, from_other[...], from_pair[...]), jnp.where(uneven, from_pair[...], from_other[...])


def side_by_side(from_right, from_left):
    in_right = lanes() < SPAN
    first = jnp.where(in_right, from_right, from_left)
    return jnp.concatenate([first, jnp.where(in_right, turn(from_right, -SPAN, 2), turn(from_left, LEFT_AT, 2))])


def pack_strips(from_pair, from_other, near, strips, to_far, near_other, near_pair):
    lane = lanes()
    in_right = lane < SPAN
    slot_right, slot_left = slots(lane)
    rows = side_by_side(*right_and_left(from_other, from_pair))
    strips[...] = rows
    around_left = any_of(lane, (LEFT_AT - 1, LEFT_AT + SPAN))
    for layer in range(DK // 2):
        first, second = needed(layer), needed(DK - 1 - layer)
        deep = rows[DK - 1 - layer]
        takes_right = in_right & (slot_right >= 8 - second)
        takes_left = around_left & (slot_left >= 8 - first - second) & (slot_left < 8 - first)
        value = jnp.where(takes_left, turn(deep, -first), rows[layer])
        to_far[layer] = jnp.where(takes_right, turn(deep, 8 - second), value)
    half = DK // 2

    def edge(slot, first):
        index = first + lax.rem(slot, 8) + HALF * lax.rem(lax.div(slot, 8), 2)
        return jnp.clip(index, 0, CA - 1)

    left_order = edge(lane, 0)
    right_order = jnp.where(lane < SPAN, edge(lane, HALF - STRIP), edge(lane + (16 * 4 - LEFT_AT), HALF - STRIP))
    left = right = jnp.zeros((half, NZ, CA), jnp.float32)
    for number, start in enumerate((0, DG, DG + DK)):
        for part in range(2):
            last = DK if number == 1 else DG
            edges = jnp.stack([near[start + min(part * half + n, last - 1)] for n in range(half)])
            base = part * SPAN + 16 * number
            left = jnp.where(any_of(lane, (base, base + 16)), picked(edges, left_order), left)
            base = (1 - part) * LEFT_AT + 16 * number
            right = jnp.where(any_of(lane, (base, base + 16)), picked(edges, right_order), right)
    uneven = odd_aisle()
    near_pair[...] = jnp.where(uneven, left, right)
    near_other[...] = jnp.where(uneven, right, left)


def unpack_strips(pairs, lane):
    slot_right, slot_left = slots(lane)
    half = DK // 2
    near_part = [pairs[layer] for layer in range(half)]
    deep_part = []
    for layer in reversed(range(half)):
        first, second = needed(layer), needed(DK - 1 - layer)
        right = (lane < SPAN) & (slot_right < second)
        left = any_of(lane, (LEFT_AT, LEFT_AT + SPAN)) & (slot_left >= 8 - second)
        value = jnp.where(left, turn(pairs[layer], first), 0.0)
        deep_part.append(jnp.where(right, turn(pairs[layer], second - 8), value))
    return near_part + deep_part


def picked(value, index):
    rows = value.reshape(-1, CA)
    return jnp.take_along_axis(rows, jnp.concatenate([index] * (rows.shape[0] // NZ)), axis=1).reshape(value.shape)


def split(block, copies):
    lane = lanes()
    in_block = lane < HALF
    index = lane
    if copies:
        in_block |= any_of(lane, (66, 67), (125, 126))
        index = jnp.where(lane == 66, HALF - 1, jnp.where(lane == 125, 0, index))
    tiles = []
    for colour in range(2):
        part = block
        if copies or colour:
            part = picked(block, jnp.clip(index + HALF * colour, 0, CA - 1))
        tiles.append(jnp.where(in_block, part, 0.0))
    return jnp.stack(tiles, axis=1)


def expand(tiles, strip, number, copies):
    lane = lanes()
    in_strip = any_of(lane, (RIGHT0, RIGHT0 + STRIP), (LEFT0, LEFT0 + STRIP))
    index = lane - RIGHT0
    if copies:
        in_strip |= any_of(lane, (64, 65), (127, 128))
        index = jnp.where(lane == 64, 0, jnp.where(lane == 127, LEFT_AT + STRIP - 1, index))
    beside = [picked(strip, jnp.clip(index + (16 * number + 8 * colour), 0, CA - 1)) for colour in range(2)]
    return jnp.where(in_strip, jnp.stack(beside, axis=1), tiles)


def spread(here, shift):
    level = lax.broadcasted_iota(jnp.int32, here.shape, 2)
    even, uneven = here[:, 0], here[:, 1]
    after, before = turn(even, -1, 2), turn(uneven, 1, 2)
    x_up = jnp.stack([uneven, after], axis=1)
    x_both = jnp.stack([uneven + before, even + after], axis=1)
    z_up = turn(here, -1, 2)
    z_both = jnp.where(level == NZ - 1, 0.0, z_up) + jnp.where(level == 0, 0.0, turn(here, 1, 2))
    part = shift + 6.0 * here + (z_both + x_both)
    return here + x_up, jnp.where(level == NZ - 1, 0.0, here + z_up), part


def pieces(low, high):
    number = -(-(high - low) // GROUP)
    cuts = [low + (high - low) * n // number for n in range(number + 1)]
    return [(first, last - first) for first, last in zip(cuts[:-1], cuts[1:])]


def inverted(diagonal):
    both = lax.broadcasted_iota(jnp.int32, (2, NZ, CA), 2)
    good = any_of(both, (0, 65), (66, 74), (118, 126), (127, 128)) & (diagonal > 0.0)
    return jnp.where(good, 1.0 / jnp.where(good, diagonal, 1.0), 0.0)


def around(weights, row, count, here, below, above):
    face_x, face_z, face_r = weights
    at = pl.ds(row, count)
    fx, fz = face_x[at], face_z[at]
    even, uneven = here[:, 0], here[:, 1]
    summed = face_r[at] * below + face_r[pl.ds(row + 1, count)] * above
    summed += fz * turn(here, -1, 2) + turn(fz * here, 1, 2)
    sum_even = fx[:, 0] * uneven + turn(fx[:, 1] * uneven, 1, 2)
    sum_odd = fx[:, 0] * even + fx[:, 1] * turn(even, -1, 2)
    return summed + jnp.stack([sum_even, sum_odd], axis=1)


def prepare_own(main, strips, near, tiles, rhs, cond, face_x, face_z, face_r, part, inverse, levels):
    tiles[:DG] = split(near[:DG], False)
    tiles[DG:] = split(near[DG:], True)
    halves = [pl.ds(first, 8) for first in range(0, CR, 8)]
    for at in halves:
        strip = strips[at]
        cond[at] = expand(split(main[1, at], True), strip, 1, True)
        part[at] = expand(split(main[2, at], True), strip, 2, True)
        rhs[at] = expand(split(main[0, at], False), strip, 0, False)
    for at in halves:
        face_x[at], face_z[at], part[at] = spread(cond[at], part[at])
    face_r[pl.ds(0, 1)] = jnp.zeros((1, 2, NZ, CA), jnp.float32)
    for first, count in pieces(1, CR):
        face_r[pl.ds(first, count)] = cond[pl.ds(first - 1, count)] + cond[pl.ds(first, count)]
    for first, count in pieces(1, CR - 1):
        at = pl.ds(first, count)
        inverse[at] = inverted(part[at] + (cond[pl.ds(first - 1, count)] + cond[pl.ds(first + 1, count)]))
        levels[0, at] = inverse[at] * rhs[at]
    weights = face_x, face_z, face_r
    for done, power in enumerate(reversed(POWERS)):
        for first, count in pieces(2 + done, CR - 2 - done):
            here, below, above = [levels[done, pl.ds(first + n, count)] for n in (0, -1, 1)]
            at = pl.ds(first, count)
            levels[done + 1, at] = inverse[at] * (power * rhs[at] + around(weights, first, count, here, below, above))


def split_far(far, tiles):
    tiles[:DG] = split(far[:DG], False)
    tiles[DG:] = split(far[DG:], True)


def in_core(p0, row):
    p = p0 + row
    return {FAR_BOX[0]: p < 0, OWN_BOX[0]: 0 <= p < CR, NEAR_BOX[0]: p >= CR}[p0]


def solve_all(own_rhs, own_cond, own_x, own_z, own_r, own_part, own_inverse, levels, near, far, far_strips, near_other, near_pair, out,
              cond, face_x, face_z, face_r, part, inverse, rhs, est_a, est_b, total):
    row_at = lax.axis_index("row")
    odd = lax.rem(row_at, 2)
    far_there = jnp.where(odd == 0, row_at > 0, row_at < lax.axis_size("row") - 1)
    far_level = far_there.astype(jnp.float32)
    far_tile = jnp.full((NZ, CA), far_level) > 0.5
    lane = lanes()

    own = pl.ds(DK, CR)
    cond[own] = own_cond[...]
    face_x[own] = own_x[...]
    face_z[own] = own_z[...]
    part[own] = own_part[...]
    p0, count, at, guarded = OWN_BOX
    zeros = jnp.zeros((1, 2, NZ, CA), jnp.float32)
    rhs[pl.ds(at + OV, CR)] = own_rhs[...]
    for row in (SIDE - 2, SIDE - 1, SIDE, SIDE + 1, SIDE + OWN - 2, SIDE + OWN - 1, SIDE + OWN, SIDE + OWN + 1):
        rhs[pl.ds(row, 1)] = zeros
    for est in (est_a, est_b):
        for row in (0, SIDE + 1, SIDE + OWN + 2, GUARDED - 1):
            est[pl.ds(row, 1)] = zeros

    sides = [(far, unpack_strips(far_strips, lane)[::-1], True), (near, side_by_side(*right_and_left(near_other, near_pair)), False)]
    for block, strip, is_far in sides:
        for low, high in ((0, 7), (7, DK)):
            at = pl.ds((0 if is_far else DK + CR) + low, high - low)
            cond[at] = expand(block[pl.ds(DG + low, high - low)], jnp.stack(strip[low:high]), 1, True)
        strip = strip[1:] if is_far else strip[:DG]
        for low, high in ((0, 7), (7, DG)):
            beside = jnp.stack(strip[low:high])
            at = pl.ds((1 if is_far else DK + CR) + low, high - low)
            part[at] = expand(block[pl.ds(DG + DK + low, high - low)], beside, 2, True)
            at = pl.ds((0 if is_far else NEAR_BOX[2] + OV) + low, high - low)
            rhs[at] = expand(block[pl.ds(low, high - low)], beside, 0, False)
    for first in (1, DK + CR):
        for low, high in ((0, 7), (7, DG)):
            at = pl.ds(first + low, high - low)
            shift = part[at]
            if first == 1:
                shift = jnp.where(far_tile, shift, 2.0)
            face_x[at], face_z[at], part[at] = spread(cond[at], shift)

    face_r[pl.ds(DK + 1, CR - 1)] = own_r[pl.ds(1, CR - 1)]
    for first, last in ((1, DK + 1), (DK + CR, 2 * DG + CR + 2)):
        for low, count in pieces(first, last):
            face_r[pl.ds(low, count)] = cond[pl.ds(low - 1, count)] + cond[pl.ds(low, count)]

    both = lax.broadcasted_iota(jnp.int32, (2, NZ, CA), 2)
    core = any_of(both, (0, 64), (67, 74), (118, 125))

    def invert(box, first, count, has_below=True, has_above=True):
        p0, _, at, _ = box
        place = p0 + first + DK
        diagonal = part[pl.ds(place, count)]
        if has_below:
            diagonal += cond[pl.ds(place - 1, count)]
        if has_above:
            diagonal += cond[pl.ds(place + 1, count)]
        inverse[pl.ds(at + first, count)] = inverted(diagonal)

    for low, high in ((0, 7), (7, SIDE - 1)):
        invert(FAR_BOX, low, high - low)
        invert(NEAR_BOX, low + 1, high - low)
    invert(FAR_BOX, SIDE - 1, 1, has_above=False)
    invert(NEAR_BOX, 0, 1, has_below=False)
    inverse[pl.ds(OWN_BOX[2] + OV + 1, CR - 2)] = own_inverse[pl.ds(1, CR - 2)]
    for low in (1, OV + CR - 1):
        invert(OWN_BOX, low, OV)
    invert(OWN_BOX, 0, 1, has_below=False)
    invert(OWN_BOX, OWN - 1, 1, has_above=False)

    weights = face_x, face_z, face_r

    def solve(spans, borrow):
        for p0, _, at, guarded, low, high in spans(0):
            for first, count in pieces(low, high):
                here = pl.ds(at + first, count)
                est_a[pl.ds(guarded + first, count)] = inverse[here] * rhs[here]
        source, target = est_a, est_b
        for done, power in enumerate(reversed(POWERS)):
            borrow(done, source)
            for p0, _, at, guarded, low, high in spans(done + 1):
                for first, count in pieces(low, high):
                    here, below, above = [source[pl.ds(guarded + first + n, count)] for n in (0, -1, 1)]
                    summed = around(weights, p0 + first + DK, count, here, below, above)
                    given = [row for row in range(first, first + count) if in_core(p0, row)]
                    if len(given) == count:
                        summed += power * rhs[pl.ds(at + first, count)]
                    elif given:
                        skip, end = given[0] - first, given[-1] + 1 - first
                        more = summed[skip:end] + power * rhs[pl.ds(at + given[0], len(given))]
                        summed = jnp.concatenate([v for v in (summed[:skip], more, summed[end:]) if v.shape[0]])
                    target[pl.ds(guarded + first, count)] = inverse[pl.ds(at + first, count)] * summed
            source, target = target, source
        borrow(SWEEPS, source)

    def first_spans(done):
        low = (0, OV + 1 + done)
        high = (OWN - OV - 1 - done, OWN)
        return (FAR_BOX + (done, SIDE), NEAR_BOX + (0, SIDE - done), OWN_BOX + low, OWN_BOX + high)

    def from_own(done, est):
        rows = (7, 8) if done == SWEEPS else (done + 1, done + 2, CR - 3 - done, CR - 2 - done)
        for p in rows:
            est[pl.ds(OWN_BOX[3] + OV + p, 1)] = levels[done, pl.ds(p, 1)]

    solve(first_spans, from_own)
    est = est_a if SWEEPS % 2 == 0 else est_b

    to_low = any_of(lane, (63, 65), (124, 126))
    to_high = any_of(lane, (66, 68), (127, 128), (0, 1))
    twins = lax.rem(lane + jnp.where(to_low, TWIN, jnp.where(to_high, CA - TWIN, 0)), CA)
    twice = to_low | to_high

    def joined(value):
        return value + jnp.where(twice, picked(value, twins), 0.0)

    def summed_boxes(p, count):
        value = None
        for p0, rows, _, guarded in (FAR_BOX, OWN_BOX, NEAR_BOX):
            if p0 <= p and p + count <= p0 + rows:
                share = est[pl.ds(guarded + p - p0, count)]
                value = share if value is None else value + share
        return value

    for low, high in ((-REACH, -OV), (-OV, 0), (0, OV), (OV, 8), (8, CR - OV), (CR - OV, CR + OV), (CR + OV, CR + REACH)):
        value = joined(summed_boxes(low, high - low))
        if low < 0:
            value = jnp.where(far_tile, value, 0.0)
        total[pl.ds(low + REACH, high - low)] = value

    def remainder(box, p, count):
        p0, _, at, _ = box
        here, below, above = [total[pl.ds(p + REACH + n, count)] for n in (0, -1, 1)]
        place = p + DK
        diagonal = part[pl.ds(place, count)] + (cond[pl.ds(place - 1, count)] + cond[pl.ds(place + 1, count)])
        summed = around(weights, p + DK, count, here, below, above)
        here_rhs = pl.ds(at + p - p0, count)
        value = jnp.where(core, rhs[here_rhs] - LEAD * (diagonal * here - summed), 0.0)
        if p < 0:
            value = jnp.where(far_tile, value, 0.0)
        rhs[here_rhs] = value

    remainder(FAR_BOX, -SWEEPS, SWEEPS)
    for p in range(0, CR, 8):
        remainder(OWN_BOX, p, 8)
    remainder(NEAR_BOX, CR, SWEEPS)

    def second_spans(done):
        cut = max(0, done + OV - SWEEPS)
        return (
            FAR_BOX + (DG - SWEEPS + done, SIDE), OWN_BOX + (cut, OWN - cut), NEAR_BOX + (0, SWEEPS + OV - done)
        )

    solve(second_spans, lambda done, est: None)

    order = lax.div(lane, 2)
    is_even = lax.rem(lane, 2) == 0
    for low, high in ((0, OV), (OV, 8), (8, CR - OV), (CR - OV, CR)):
        value = joined(summed_boxes(low, high - low)) + total[pl.ds(low + REACH, high - low)]
        value = jnp.where(is_even, picked(value[:, 0], order), picked(value[:, 1], order))
        value = value.reshape((high - low) * NZ, CA)
        for n in range(high - low):
            row = low + n
            out[pl.ds(odd * (CR - 1 - 2 * row) + row, NZ, stride=CR), :] = value[n * NZ : (n + 1) * NZ]


def call(kernel, outs, *args, scratch=(), limit=4, cost=None):
    vmem = pl.BlockSpec(memory_space=pltpu.VMEM)
    return pl.pallas_call(
        kernel,
        out_shape=outs,
        in_specs=[vmem] * len(args),
        out_specs=jax.tree.map(lambda _: vmem, outs),
        scratch_shapes=scratch,
        compiler_params=pltpu.CompilerParams(vmem_limit_bytes=limit * MIB),
        cost_estimate=cost,
        name=kernel.__name__,
    )(*args)


def body(source, conduct, solid):
    aisles = lax.axis_size("aisle")
    rows = lax.axis_size("row")
    flat = (NZ * CR, CA)
    tile = lambda *lead: jax.ShapeDtypeStruct(lead + (NZ, CA), jnp.float32)
    busy = pl.CostEstimate(flops=10**11, bytes_accessed=0, transcendentals=0)
    shift = 0.1 + 40.0 * solid.astype(jnp.float32)
    main, to_other, to_pair, to_far, to_near = call(
        pack_edges, (tile(3, CR), tile(CR // 2), tile(CR // 2), tile(TILES), tile(TILES)),
        source.reshape(flat), conduct.reshape(flat), shift.reshape(flat),
    )
    pair = [(i, i ^ 1) for i in range(aisles)]
    other = [(i, (i - 1 + 2 * (i % 2)) % aisles) for i in range(aisles)]
    far_pairs = [(i, i + 1) for i in range(1, rows - 1, 2)]
    far_pairs += [(b, a) for a, b in far_pairs]
    near_pairs = [(i, i ^ 1) for i in range(rows)]
    from_pair = lax.ppermute(to_pair, "aisle", pair)
    from_other = lax.ppermute(to_other, "aisle", other)
    near = lax.ppermute(to_near, "row", near_pairs)
    far = lax.ppermute(to_far, "row", far_pairs)
    half = tile(DK // 2)
    strips, strips_far, near_to_other, near_to_pair = call(pack_strips, (tile(CR), half, half, half), from_pair, from_other, near)
    far_strips = lax.ppermute(strips_far, "row", far_pairs)
    near_other = lax.ppermute(near_to_other, "aisle", other)
    near_pair = lax.ppermute(near_to_pair, "aisle", pair)
    own_rows = (tile(CR, 2),) * 7 + (tile(SWEEPS + 1, CR, 2),)
    near_tiles, *own = call(
        prepare_own, (tile(TILES, 2),) + own_rows, main, strips, near, limit=8, cost=pl.CostEstimate(flops=2000*10**6, bytes_accessed=0, transcendentals=0)
    )
    pair_rows = lambda count: pltpu.VMEM((count, 2, NZ, CA), jnp.float32)
    around = CR + 2 * DK
    result = call(
        solve_all,
        jax.ShapeDtypeStruct(flat, jnp.float32),
        *own, near_tiles, call(split_far, tile(TILES, 2), far), far_strips, near_other, near_pair,
        scratch=[
            pair_rows(around), pair_rows(around), pair_rows(around), pair_rows(around), pair_rows(around),
            pair_rows(ROWS), pair_rows(ROWS), pair_rows(GUARDED), pair_rows(GUARDED), pair_rows(CR + 2 * REACH),
        ],
        limit=16,
    )
    return result.reshape(NZ, CR, CA)


def solution(mesh):
    spec = P(None, "row", "aisle")
    return jax.shard_map(body, mesh=mesh, in_specs=(spec, spec, spec), out_specs=spec, check_vma=False)
```

```python
import jax
import jax.numpy as jnp
from jax import lax
from jax.experimental import pallas as pl
from jax.experimental.pallas import tpu as pltpu
from jax.sharding import PartitionSpec as P

OV = 2
SWEEPS = 6
LOWER_END = 0.2
UPPER_END = 2.0
MIDDLE = 0.5 * (UPPER_END + LOWER_END)
SPREAD = 0.5 * (UPPER_END - LOWER_END)

NZ = 8
CR = 16
CA = 128
HALF = CA // 2
MIB = 1024 * 1024
DG = 2 * SWEEPS + 1
DK = DG + 1
TILES = 2 * DG + DK
SIDE = DG + OV
OWN = CR + 2 * OV
ROWS = 2 * SIDE + OWN
REACH = SWEEPS + 1
FAR_BOX = (-DG, SIDE, 0, 1)
OWN_BOX = (-OV, OWN, SIDE, SIDE + 2)
NEAR_BOX = (CR - OV, SIDE, SIDE + OWN, SIDE + OWN + 3)
GUARDED = ROWS + 4
TWIN = 3
GROUP = 8
STRIP = 7
RIGHT0 = 67
LEFT0 = 118
SPAN = 48
LEFT_AT = LEFT0 - RIGHT0


def coefficients():
    ratio = SPREAD / MIDDLE
    update = [1.0 / MIDDLE] + [0.0] * SWEEPS
    estimate = list(update)
    for _ in range(SWEEPS):
        image = [0.0] + estimate[:-1]
        remain = [float(n == 0) - e + i for n, (e, i) in enumerate(zip(estimate, image))]
        ratio_next = 1.0 / (2.0 * MIDDLE / SPREAD - ratio)
        update = [ratio_next * ratio * u + 2.0 * ratio_next / SPREAD * r for u, r in zip(update, remain)]
        estimate = [e + u for e, u in zip(estimate, update)]
        ratio = ratio_next
    return estimate


LEAD = coefficients()[-1]
POWERS = [power / LEAD for power in coefficients()[:-1]]


def lanes():
    return lax.broadcasted_iota(jnp.int32, (NZ, CA), 1)


def turn(value, by, axis=1):
    return pltpu.roll(value, by % value.shape[axis], axis)


def any_of(lane, *spans):
    mask = None
    for low, high in spans:
        here = (lane >= low) & (lane < high)
        mask = here if mask is None else mask | here
    return mask


def needed(layer):
    return (max(DK - 1 - layer, OV) + 1) // 2


def block_of(ref, first, count):
    return ref[pl.ds(first, count)]


def pack_edges(source, conduct, shift, main, to_other, to_pair, to_far, to_near):
    odd = lax.rem(lax.axis_index("row"), 2)
    half = CR // 2
    shape = (half * NZ, CA)
    lane = lax.broadcasted_iota(jnp.int32, shape, 1)
    order = jnp.where(lane < HALF, 2 * lane, 2 * lane - (CA - 1))

    def edge(slot, first):
        return first + 2 * lax.rem(slot, 8) + lax.rem(lax.div(slot, 8), 2)

    end = CA - 2 * STRIP
    left_order = edge(lane, 0)
    right_order = jnp.where(lane < SPAN, edge(lane, end), edge(lane + (16 * 4 - LEFT_AT), end))
    right_order = jnp.minimum(right_order, CA - 1)
    pick = lambda value, index: jnp.take_along_axis(value, index, axis=1)
    left = right = jnp.zeros(shape, jnp.float32)
    for number, (field, scale) in enumerate(((source, 2.0 * LEAD), (conduct, 1.0), (shift, 1.0))):
        for part in range(2):
            rows = []
            for row in range(part * half, (part + 1) * half):
                rows.append(field[pl.ds(odd * (CR - 1 - 2 * row) + row, NZ, stride=CR), :])
            rows = scale * jnp.concatenate(rows)
            main[number, pl.ds(part * half, half)] = pick(rows, order).reshape(half, NZ, CA)
            base = part * SPAN + 16 * number
            left = jnp.where(any_of(lane, (base, base + 16)), pick(rows, left_order), left)
            base = (1 - part) * LEFT_AT + 16 * number
            right = jnp.where(any_of(lane, (base, base + 16)), pick(rows, right_order), right)
    left = left.reshape(half, NZ, CA)
    right = right.reshape(half, NZ, CA)
    start = 0
    for number, depth in enumerate((DG, DK, DG)):
        to_far[pl.ds(start, depth)] = jnp.stack([main[number, depth - 1 - n] for n in range(depth)])
        to_near[pl.ds(start, depth)] = jnp.stack([main[number, CR - 1 - n] for n in range(depth)])
        start += depth
    uneven = odd_aisle()
    to_pair[...] = jnp.where(uneven, left, right)
    to_other[...] = jnp.where(uneven, right, left)


def odd_aisle():
    return jnp.full((NZ, CA), lax.rem(lax.axis_index("aisle"), 2)) > 0


def slots(lane):
    return lax.rem(lane, 8), lax.rem(lane + 6, 8)


def right_and_left(from_other, from_pair):
    uneven = odd_aisle()
    return jnp.where(uneven, from_other[...], from_pair[...]), jnp.where(uneven, from_pair[...], from_other[...])


def side_by_side(from_right, from_left):
    in_right = lanes() < SPAN
    first = jnp.where(in_right, from_right, from_left)
    return jnp.concatenate([first, jnp.where(in_right, turn(from_right, -SPAN, 2), turn(from_left, LEFT_AT, 2))])


def pack_strips(from_pair, from_other, near, strips, to_far, near_other, near_pair):
    lane = lanes()
    in_right = lane < SPAN
    slot_right, slot_left = slots(lane)
    rows = side_by_side(*right_and_left(from_other, from_pair))
    strips[...] = rows
    around_left = any_of(lane, (LEFT_AT - 1, LEFT_AT + SPAN))
    for layer in range(DK // 2):
        first, second = needed(layer), needed(DK - 1 - layer)
        deep = rows[DK - 1 - layer]
        takes_right = in_right & (slot_right >= 8 - second)
        takes_left = around_left & (slot_left >= 8 - first - second) & (slot_left < 8 - first)
        value = jnp.where(takes_left, turn(deep, -first), rows[layer])
        to_far[layer] = jnp.where(takes_right, turn(deep, 8 - second), value)
    half = DK // 2

    def edge(slot, first):
        index = first + lax.rem(slot, 8) + HALF * lax.rem(lax.div(slot, 8), 2)
        return jnp.clip(index, 0, CA - 1)

    left_order = edge(lane, 0)
    right_order = jnp.where(lane < SPAN, edge(lane, HALF - STRIP), edge(lane + (16 * 4 - LEFT_AT), HALF - STRIP))
    left = right = jnp.zeros((half, NZ, CA), jnp.float32)
    for number, start in enumerate((0, DG, DG + DK)):
        for part in range(2):
            last = DK if number == 1 else DG
            edges = jnp.stack([near[start + min(part * half + n, last - 1)] for n in range(half)])
            base = part * SPAN + 16 * number
            left = jnp.where(any_of(lane, (base, base + 16)), picked(edges, left_order), left)
            base = (1 - part) * LEFT_AT + 16 * number
            right = jnp.where(any_of(lane, (base, base + 16)), picked(edges, right_order), right)
    uneven = odd_aisle()
    near_pair[...] = jnp.where(uneven, left, right)
    near_other[...] = jnp.where(uneven, right, left)


def unpack_strips(pairs, lane):
    slot_right, slot_left = slots(lane)
    half = DK // 2
    near_part = [pairs[layer] for layer in range(half)]
    deep_part = []
    for layer in reversed(range(half)):
        first, second = needed(layer), needed(DK - 1 - layer)
        right = (lane < SPAN) & (slot_right < second)
        left = any_of(lane, (LEFT_AT, LEFT_AT + SPAN)) & (slot_left >= 8 - second)
        value = jnp.where(left, turn(pairs[layer], first), 0.0)
        deep_part.append(jnp.where(right, turn(pairs[layer], second - 8), value))
    return near_part + deep_part


def picked(value, index):
    rows = value.reshape(-1, CA)
    return jnp.take_along_axis(rows, jnp.concatenate([index] * (rows.shape[0] // NZ)), axis=1).reshape(value.shape)


def split(block, copies):
    lane = lanes()
    in_block = lane < HALF
    index = lane
    if copies:
        in_block |= any_of(lane, (66, 67), (125, 126))
        index = jnp.where(lane == 66, HALF - 1, jnp.where(lane == 125, 0, index))
    tiles = []
    for colour in range(2):
        part = block
        if copies or colour:
            part = picked(block, jnp.clip(index + HALF * colour, 0, CA - 1))
        tiles.append(jnp.where(in_block, part, 0.0))
    return jnp.stack(tiles, axis=1)


def expand(tiles, strip, number, copies):
    lane = lanes()
    in_strip = any_of(lane, (RIGHT0, RIGHT0 + STRIP), (LEFT0, LEFT0 + STRIP))
    index = lane - RIGHT0
    if copies:
        in_strip |= any_of(lane, (64, 65), (127, 128))
        index = jnp.where(lane == 64, 0, jnp.where(lane == 127, LEFT_AT + STRIP - 1, index))
    beside = [picked(strip, jnp.clip(index + (16 * number + 8 * colour), 0, CA - 1)) for colour in range(2)]
    return jnp.where(in_strip, jnp.stack(beside, axis=1), tiles)


def spread(here, shift):
    level = lax.broadcasted_iota(jnp.int32, here.shape, 2)
    even, uneven = here[:, 0], here[:, 1]
    after, before = turn(even, -1, 2), turn(uneven, 1, 2)
    x_up = jnp.stack([uneven, after], axis=1)
    x_both = jnp.stack([uneven + before, even + after], axis=1)
    z_up = turn(here, -1, 2)
    z_both = jnp.where(level == NZ - 1, 0.0, z_up) + jnp.where(level == 0, 0.0, turn(here, 1, 2))
    part = shift + 6.0 * here + (z_both + x_both)
    return here + x_up, jnp.where(level == NZ - 1, 0.0, here + z_up), part


def pieces(low, high):
    number = -(-(high - low) // GROUP)
    cuts = [low + (high - low) * n // number for n in range(number + 1)]
    return [(first, last - first) for first, last in zip(cuts[:-1], cuts[1:])]


def inverted(diagonal):
    both = lax.broadcasted_iota(jnp.int32, (2, NZ, CA), 2)
    good = any_of(both, (0, 65), (66, 74), (118, 126), (127, 128)) & (diagonal > 0.0)
    return jnp.where(good, 1.0 / jnp.where(good, diagonal, 1.0), 0.0)


def around(weights, row, count, here, below, above):
    face_x, face_z, face_r = weights
    at = pl.ds(row, count)
    fx, fz = face_x[at], face_z[at]
    even, uneven = here[:, 0], here[:, 1]
    summed = face_r[at] * below + face_r[pl.ds(row + 1, count)] * above
    summed += fz * turn(here, -1, 2) + turn(fz * here, 1, 2)
    sum_even = fx[:, 0] * uneven + turn(fx[:, 1] * uneven, 1, 2)
    sum_odd = fx[:, 0] * even + fx[:, 1] * turn(even, -1, 2)
    return summed + jnp.stack([sum_even, sum_odd], axis=1)


def prepare_own(main, strips, near, tiles, rhs, cond, face_x, face_z, face_r, part, inverse, levels):
    tiles[:DG] = split(near[:DG], False)
    tiles[DG:] = split(near[DG:], True)
    halves = [pl.ds(first, 8) for first in range(0, CR, 8)]
    for at in halves:
        strip = strips[at]
        cond[at] = expand(split(main[1, at], True), strip, 1, True)
        part[at] = expand(split(main[2, at], True), strip, 2, True)
        rhs[at] = expand(split(main[0, at], False), strip, 0, False)
    for at in halves:
        face_x[at], face_z[at], part[at] = spread(cond[at], part[at])
    face_r[pl.ds(0, 1)] = jnp.zeros((1, 2, NZ, CA), jnp.float32)
    for first, count in pieces(1, CR):
        face_r[pl.ds(first, count)] = cond[pl.ds(first - 1, count)] + cond[pl.ds(first, count)]
    for first, count in pieces(1, CR - 1):
        at = pl.ds(first, count)
        inverse[at] = inverted(part[at] + (cond[pl.ds(first - 1, count)] + cond[pl.ds(first + 1, count)]))
        levels[0, at] = inverse[at] * rhs[at]
    weights = face_x, face_z, face_r
    for done, power in enumerate(reversed(POWERS)):
        for first, count in pieces(2 + done, CR - 2 - done):
            here, below, above = [levels[done, pl.ds(first + n, count)] for n in (0, -1, 1)]
            at = pl.ds(first, count)
            levels[done + 1, at] = inverse[at] * (power * rhs[at] + around(weights, first, count, here, below, above))


def split_far(far, tiles):
    tiles[:DG] = split(far[:DG], False)
    tiles[DG:] = split(far[DG:], True)


def in_core(p0, row):
    p = p0 + row
    return {FAR_BOX[0]: p < 0, OWN_BOX[0]: 0 <= p < CR, NEAR_BOX[0]: p >= CR}[p0]


def solve_all(own_rhs, own_cond, own_x, own_z, own_r, own_part, own_inverse, levels, near, far, far_strips, near_other, near_pair, out,
              cond, face_x, face_z, face_r, part, inverse, rhs, est_a, est_b, total):
    row_at = lax.axis_index("row")
    odd = lax.rem(row_at, 2)
    far_there = jnp.where(odd == 0, row_at > 0, row_at < lax.axis_size("row") - 1)
    far_level = far_there.astype(jnp.float32)
    far_tile = jnp.full((NZ, CA), far_level) > 0.5
    lane = lanes()

    own = pl.ds(DK, CR)
    cond[own] = own_cond[...]
    face_x[own] = own_x[...]
    face_z[own] = own_z[...]
    part[own] = own_part[...]
    p0, count, at, guarded = OWN_BOX
    zeros = jnp.zeros((1, 2, NZ, CA), jnp.float32)
    rhs[pl.ds(at + OV, CR)] = own_rhs[...]
    for row in (SIDE - 2, SIDE - 1, SIDE, SIDE + 1, SIDE + OWN - 2, SIDE + OWN - 1, SIDE + OWN, SIDE + OWN + 1):
        rhs[pl.ds(row, 1)] = zeros
    for est in (est_a, est_b):
        for row in (0, SIDE + 1, SIDE + OWN + 2, GUARDED - 1):
            est[pl.ds(row, 1)] = zeros

    sides = [(far, unpack_strips(far_strips, lane)[::-1], True), (near, side_by_side(*right_and_left(near_other, near_pair)), False)]
    for block, strip, is_far in sides:
        for low, high in ((0, 7), (7, DK)):
            at = pl.ds((0 if is_far else DK + CR) + low, high - low)
            cond[at] = expand(block[pl.ds(DG + low, high - low)], jnp.stack(strip[low:high]), 1, True)
        strip = strip[1:] if is_far else strip[:DG]
        for low, high in ((0, 7), (7, DG)):
            beside = jnp.stack(strip[low:high])
            at = pl.ds((1 if is_far else DK + CR) + low, high - low)
            part[at] = expand(block[pl.ds(DG + DK + low, high - low)], beside, 2, True)
            at = pl.ds((0 if is_far else NEAR_BOX[2] + OV) + low, high - low)
            rhs[at] = expand(block[pl.ds(low, high - low)], beside, 0, False)
    for first in (1, DK + CR):
        for low, high in ((0, 7), (7, DG)):
            at = pl.ds(first + low, high - low)
            shift = part[at]
            if first == 1:
                shift = jnp.where(far_tile, shift, 2.0)
            face_x[at], face_z[at], part[at] = spread(cond[at], shift)

    face_r[pl.ds(DK + 1, CR - 1)] = own_r[pl.ds(1, CR - 1)]
    for first, last in ((1, DK + 1), (DK + CR, 2 * DG + CR + 2)):
        for low, count in pieces(first, last):
            face_r[pl.ds(low, count)] = cond[pl.ds(low - 1, count)] + cond[pl.ds(low, count)]

    both = lax.broadcasted_iota(jnp.int32, (2, NZ, CA), 2)
    core = any_of(both, (0, 64), (67, 74), (118, 125))

    def invert(box, first, count, has_below=True, has_above=True):
        p0, _, at, _ = box
        place = p0 + first + DK
        diagonal = part[pl.ds(place, count)]
        if has_below:
            diagonal += cond[pl.ds(place - 1, count)]
        if has_above:
            diagonal += cond[pl.ds(place + 1, count)]
        inverse[pl.ds(at + first, count)] = inverted(diagonal)

    for low, high in ((0, 7), (7, SIDE - 1)):
        invert(FAR_BOX, low, high - low)
        invert(NEAR_BOX, low + 1, high - low)
    invert(FAR_BOX, SIDE - 1, 1, has_above=False)
    invert(NEAR_BOX, 0, 1, has_below=False)
    inverse[pl.ds(OWN_BOX[2] + OV + 1, CR - 2)] = own_inverse[pl.ds(1, CR - 2)]
    for low in (1, OV + CR - 1):
        invert(OWN_BOX, low, OV)
    invert(OWN_BOX, 0, 1, has_below=False)
    invert(OWN_BOX, OWN - 1, 1, has_above=False)

    weights = face_x, face_z, face_r

    def solve(spans, borrow):
        for p0, _, at, guarded, low, high in spans(0):
            for first, count in pieces(low, high):
                here = pl.ds(at + first, count)
                est_a[pl.ds(guarded + first, count)] = inverse[here] * rhs[here]
        source, target = est_a, est_b
        for done, power in enumerate(reversed(POWERS)):
            borrow(done, source)
            for p0, _, at, guarded, low, high in spans(done + 1):
                for first, count in pieces(low, high):
                    here, below, above = [source[pl.ds(guarded + first + n, count)] for n in (0, -1, 1)]
                    summed = around(weights, p0 + first + DK, count, here, below, above)
                    given = [row for row in range(first, first + count) if in_core(p0, row)]
                    if len(given) == count:
                        summed += power * rhs[pl.ds(at + first, count)]
                    elif given:
                        skip, end = given[0] - first, given[-1] + 1 - first
                        more = summed[skip:end] + power * rhs[pl.ds(at + given[0], len(given))]
                        summed = jnp.concatenate([v for v in (summed[:skip], more, summed[end:]) if v.shape[0]])
                    target[pl.ds(guarded + first, count)] = inverse[pl.ds(at + first, count)] * summed
            source, target = target, source
        borrow(SWEEPS, source)

    def first_spans(done):
        low = (0, OV + 1 + done)
        high = (OWN - OV - 1 - done, OWN)
        return (FAR_BOX + (done, SIDE), NEAR_BOX + (0, SIDE - done), OWN_BOX + low, OWN_BOX + high)

    def from_own(done, est):
        rows = (7, 8) if done == SWEEPS else (done + 1, done + 2, CR - 3 - done, CR - 2 - done)
        for p in rows:
            est[pl.ds(OWN_BOX[3] + OV + p, 1)] = levels[done, pl.ds(p, 1)]

    solve(first_spans, from_own)
    est = est_a if SWEEPS % 2 == 0 else est_b

    to_low = any_of(lane, (63, 65), (124, 126))
    to_high = any_of(lane, (66, 68), (127, 128), (0, 1))
    twins = lax.rem(lane + jnp.where(to_low, TWIN, jnp.where(to_high, CA - TWIN, 0)), CA)
    twice = to_low | to_high

    def joined(value):
        return value + jnp.where(twice, picked(value, twins), 0.0)

    def summed_boxes(p, count):
        value = None
        for p0, rows, _, guarded in (FAR_BOX, OWN_BOX, NEAR_BOX):
            if p0 <= p and p + count <= p0 + rows:
                share = est[pl.ds(guarded + p - p0, count)]
                value = share if value is None else value + share
        return value

    for low, high in ((-REACH, -OV), (-OV, 0), (0, OV), (OV, 8), (8, CR - OV), (CR - OV, CR + OV), (CR + OV, CR + REACH)):
        value = joined(summed_boxes(low, high - low))
        if low < 0:
            value = jnp.where(far_tile, value, 0.0)
        total[pl.ds(low + REACH, high - low)] = value

    def remainder(box, p, count):
        p0, _, at, _ = box
        here, below, above = [total[pl.ds(p + REACH + n, count)] for n in (0, -1, 1)]
        place = p + DK
        diagonal = part[pl.ds(place, count)] + (cond[pl.ds(place - 1, count)] + cond[pl.ds(place + 1, count)])
        summed = around(weights, p + DK, count, here, below, above)
        here_rhs = pl.ds(at + p - p0, count)
        value = jnp.where(core, rhs[here_rhs] - LEAD * (diagonal * here - summed), 0.0)
        if p < 0:
            value = jnp.where(far_tile, value, 0.0)
        rhs[here_rhs] = value

    remainder(FAR_BOX, -SWEEPS, SWEEPS)
    for p in range(0, CR, 8):
        remainder(OWN_BOX, p, 8)
    remainder(NEAR_BOX, CR, SWEEPS)

    def second_spans(done):
        cut = max(0, done + OV - SWEEPS)
        return (
            FAR_BOX + (DG - SWEEPS + done, SIDE), OWN_BOX + (cut, OWN - cut), NEAR_BOX + (0, SWEEPS + OV - done)
        )

    solve(second_spans, lambda done, est: None)

    order = lax.div(lane, 2)
    is_even = lax.rem(lane, 2) == 0
    at_edge = (order == 0) | (order == HALF - 1)
    other = jnp.where(order == 0, CA - TWIN, order + TWIN)

    def in_order(value, index):
        return jnp.where(is_even, picked(value[:, 0], index), picked(value[:, 1], index))

    for low, high in ((0, OV), (OV, 8), (8, CR - OV), (CR - OV, CR)):
        value = summed_boxes(low, high - low)
        first = in_order(total[pl.ds(low + REACH, high - low)], order)
        value = first + (in_order(value, order) + jnp.where(at_edge, in_order(value, other), 0.0))
        value = value.reshape((high - low) * NZ, CA)
        for n in range(high - low):
            row = low + n
            out[pl.ds(odd * (CR - 1 - 2 * row) + row, NZ, stride=CR), :] = value[n * NZ : (n + 1) * NZ]


def call(kernel, outs, *args, scratch=(), limit=4, cost=None):
    vmem = pl.BlockSpec(memory_space=pltpu.VMEM)
    return pl.pallas_call(
        kernel,
        out_shape=outs,
        in_specs=[vmem] * len(args),
        out_specs=jax.tree.map(lambda _: vmem, outs),
        scratch_shapes=scratch,
        compiler_params=pltpu.CompilerParams(vmem_limit_bytes=limit * MIB),
        cost_estimate=cost,
        name=kernel.__name__,
    )(*args)


def body(source, conduct, solid):
    aisles = lax.axis_size("aisle")
    rows = lax.axis_size("row")
    flat = (NZ * CR, CA)
    tile = lambda *lead: jax.ShapeDtypeStruct(lead + (NZ, CA), jnp.float32)
    busy = pl.CostEstimate(flops=10**11, bytes_accessed=0, transcendentals=0)
    shift = 0.1 + 40.0 * solid.astype(jnp.float32)
    main, to_other, to_pair, to_far, to_near = call(
        pack_edges, (tile(3, CR), tile(CR // 2), tile(CR // 2), tile(TILES), tile(TILES)),
        source.reshape(flat), conduct.reshape(flat), shift.reshape(flat),
    )
    pair = [(i, i ^ 1) for i in range(aisles)]
    other = [(i, (i - 1 + 2 * (i % 2)) % aisles) for i in range(aisles)]
    far_pairs = [(i, i + 1) for i in range(1, rows - 1, 2)]
    far_pairs += [(b, a) for a, b in far_pairs]
    near_pairs = [(i, i ^ 1) for i in range(rows)]
    from_pair = lax.ppermute(to_pair, "aisle", pair)
    from_other = lax.ppermute(to_other, "aisle", other)
    near = lax.ppermute(to_near, "row", near_pairs)
    far = lax.ppermute(to_far, "row", far_pairs)
    half = tile(DK // 2)
    strips, strips_far, near_to_other, near_to_pair = call(pack_strips, (tile(CR), half, half, half), from_pair, from_other, near)
    far_strips = lax.ppermute(strips_far, "row", far_pairs)
    near_other = lax.ppermute(near_to_other, "aisle", other)
    near_pair = lax.ppermute(near_to_pair, "aisle", pair)
    own_rows = (tile(CR, 2),) * 7 + (tile(SWEEPS + 1, CR, 2),)
    near_tiles, *own = call(
        prepare_own, (tile(TILES, 2),) + own_rows, main, strips, near, limit=8, cost=pl.CostEstimate(flops=2000*10**6, bytes_accessed=0, transcendentals=0)
    )
    pair_rows = lambda count: pltpu.VMEM((count, 2, NZ, CA), jnp.float32)
    around = CR + 2 * DK
    result = call(
        solve_all,
        jax.ShapeDtypeStruct(flat, jnp.float32),
        *own, near_tiles, call(split_far, tile(TILES, 2), far), far_strips, near_other, near_pair,
        scratch=[
            pair_rows(around), pair_rows(around), pair_rows(around), pair_rows(around), pair_rows(around),
            pair_rows(ROWS), pair_rows(ROWS), pair_rows(GUARDED), pair_rows(GUARDED), pair_rows(CR + 2 * REACH),
        ],
        limit=16,
    )
    return result.reshape(NZ, CR, CA)


def solution(mesh):
    spec = P(None, "row", "aisle")
    return jax.shard_map(body, mesh=mesh, in_specs=(spec, spec, spec), out_specs=spec, check_vma=False)
```
